256 devices in a mesh: grp: 16 (over z, core), voc: 16 (over y, x).
Axes of the slice: x: 4, y: 4, z: 8, core: 2. Of those that a mesh axis runs over, the one named last changes fastest.
Arguments:
- student_hidden: bfloat16 [384, 4096], P('grp', 'voc')
- norm_gain: float32 [4096], P('voc'), may hold values from 0.5 to 1.5
- teacher_hidden: bfloat16 [384, 5120], P('grp', 'voc')
- student_head: bfloat16 [4096, 98304], P(None, ('grp', 'voc'))
- teacher_head: bfloat16 [5120, 98304], P(None, ('grp', 'voc'))
- episode_source: int32 [192], replicated, may hold values from 0 to 191, as said below
- lengths: int32 [192], replicated, may hold values from 1 to 2, 240 in all
Outputs:
- loss: float32 [], replicated
- grad_hidden: bfloat16 [384, 4096], P('grp', 'voc')
- grad_gain: float32 [4096], P('voc')
- grad_head: bfloat16 [4096, 98304], P(None, ('grp', 'voc'))
The draws below stay inside these ranges and needn't reach their ends.
Inputs may be any that keep to these rules, and one draw needn't show every extreme that they name: `episode_source`: A permutation of the episodes. Student episodes 12 * s to 12 * s + 11 form group s, teacher episodes likewise form teacher group t; at most 2 episodes of one student group come from one teacher group, and that many in some pair.
All inputs are finite; a program needn't handle non-finite values.
Results may differ from the reference program's by a relative error of at most 0.04.
Values may be sent and summed in bfloat16 or wider, within the bound.
No kernel may reach another device: no remote copies, remote signals or barrier semaphores. Data moves between devices by JAX's collectives and lax.ppermute only.
A program may use at most 64 MiB of HBM per device.

```python
import math
import jax
import jax.numpy as jnp
import numpy as np
from jax import lax

DS = 4096
DT = 5120
VOC_DEV = 384
EP_GRP = 12
SEQ = 2
EPISODES = 192
TOKENS = 384
VOCAB = 98304
N_GRP = 16
N_VOC = 16


def student_base(key):
    return jax.random.normal(jax.random.fold_in(key, 101), (TOKENS, DS), jnp.float32)


def teacher_base(key):
    return jax.random.normal(jax.random.fold_in(key, 202), (TOKENS, DT), jnp.float32)


def column_ramp(ratio):
    steps = jnp.arange(DS, dtype=jnp.float32) / (DS - 1)
    return jnp.exp(steps * math.log(ratio))[None, :]


def draw_student_hidden(key, part):
    base_rows = student_base(key)
    base_rows = base_rows * column_ramp(5.0)
    return base_rows.astype(jnp.bfloat16)


def draw_student_head(key, part):
    key = jax.random.fold_in(key, 5)
    weights = jax.random.normal(key, (DS, VOCAB), jnp.float32) * (3.0 / math.sqrt(DS))
    return weights.astype(jnp.bfloat16)


def draw_teacher_hidden(key, part):
    base_rows = teacher_base(key)
    return base_rows.astype(jnp.bfloat16)


def draw_teacher_head(key, part):
    key = jax.random.fold_in(key, 8)
    weights = jax.random.normal(key, (DT, VOCAB), jnp.float32) * (3.0 / math.sqrt(DT))
    return weights.astype(jnp.bfloat16)


def draw_episode_source(key, part):
    key = jax.random.fold_in(key, 7)
    ranks = jax.random.permutation(jax.random.fold_in(key, 1), N_GRP).astype(jnp.int32)
    offset_ids = jnp.arange(N_GRP, dtype=jnp.int32)
    priority = jnp.where(offset_ids == N_GRP // 2, -2 * N_GRP, jnp.where(offset_ids == N_GRP - 1, -N_GRP, 0)).astype(jnp.int32)
    first = jnp.argsort(ranks + priority).astype(jnp.int32)
    offsets = jnp.concatenate([first[:1], first, first[1:]])[:EP_GRP]
    group_keys = jax.random.split(jax.random.fold_in(key, 2), N_GRP)
    orders = jax.vmap(lambda single: jax.random.permutation(single, EP_GRP))(group_keys)
    shifted = jnp.take(offsets, orders.astype(jnp.int32), axis=0)
    group_ids = jnp.arange(N_GRP, dtype=jnp.int32)[:, None]
    target = (group_ids + shifted) % N_GRP
    ranking = jax.random.permutation(jax.random.fold_in(key, 3), EPISODES).astype(jnp.int32)
    scores = target.reshape(-1) * EPISODES + ranking
    ordering = jnp.argsort(scores)
    source = jnp.zeros((EPISODES,), jnp.int32).at[ordering].set(jnp.arange(EPISODES, dtype=jnp.int32))
    return source


def split_up(number_of, total, most, skew):
    weights = [(1 << 20) // math.isqrt(grade ** skew) + 1 for grade in range(2, number_of + 1)]
    spare, given = total - most - (number_of - 1), [1] * (number_of - 1)
    while spare > 0:
        candidates = [i for i in range(number_of - 1) if given[i] < most]
        pool, remaining = sum([weights[i] for i in candidates]), spare
        for i in candidates:
            more = min(most - given[i], max(1, remaining * weights[i] // pool), spare)
            given[i] = given[i] + more
            spare = spare - more
    return np.array([most] + given)


def ragged_sizes(own_key, number_of, total, limit, skew):
    if number_of == 2:
        one = jax.random.randint(own_key, (), max(1, total - limit), min(limit, total - 1) + 1)
        return jnp.stack([one, total - one])
    sizes = jnp.asarray(split_up(number_of, total, limit, skew), jnp.int32)
    twos = (number_of - 1) // 2
    source_of, taker = sizes[1:1 + 2 * twos:2], sizes[2:2 + 2 * twos:2]
    margin = jnp.minimum(source_of - 1, limit - taker)
    moved = jax.random.randint(jax.random.fold_in(own_key, 1), (twos,), 0, 1 << 20) % (margin + 1)
    sizes = sizes.at[1:1 + 2 * twos:2].set(source_of - moved).at[2:2 + 2 * twos:2].set(taker + moved)
    return sizes[jax.random.permutation(jax.random.fold_in(own_key, 2), number_of)]


def setup_inputs(seed: int = 0) -> dict:
    streams_of = jax.random.split(jax.random.key(seed), 8)
    student_hidden = draw_student_hidden(jax.random.fold_in(streams_of[7], 71), 0)
    norm_gain = jnp.clip(1.0 + 0.1 * jax.random.normal(streams_of[1], (DS,), jnp.float32), 0.5, 1.5)
    teacher_hidden = draw_teacher_hidden(jax.random.fold_in(streams_of[7], 71), 0)
    student_head = draw_student_head(jax.random.fold_in(streams_of[7], 71), 0)
    teacher_head = draw_teacher_head(jax.random.fold_in(streams_of[7], 71), 0)
    episode_source = draw_episode_source(jax.random.fold_in(streams_of[7], 71), 0)
    lengths = ragged_sizes(streams_of[6], EPISODES, EPISODES * SEQ * 5 // 8, SEQ, 2).astype(jnp.int32)
    return dict(student_hidden=student_hidden, norm_gain=norm_gain, teacher_hidden=teacher_hidden, student_head=student_head, teacher_head=teacher_head, episode_source=episode_source, lengths=lengths)


EPSILON = 1e-06

def reference(student_hidden, norm_gain, teacher_hidden, student_head, teacher_head, episode_source, lengths):
    hidden_f32 = student_hidden.astype(jnp.float32)
    inverse_rms = lax.rsqrt(lax.optimization_barrier(jnp.mean(hidden_f32 * hidden_f32, axis=1)) + EPSILON)
    normed = (hidden_f32 * inverse_rms[:, None] * norm_gain[None, :]).astype(jnp.bfloat16)
    positions = jnp.arange(SEQ, dtype=jnp.int32)
    token_order = (episode_source[:, None] * SEQ + positions[None, :]).reshape(-1).astype(jnp.int32)
    teacher_rows = jnp.take(teacher_hidden, token_order, axis=0)
    student_logits = jnp.dot(normed, student_head, preferred_element_type=jnp.float32)
    teacher_logits = jnp.dot(teacher_rows, teacher_head, preferred_element_type=jnp.float32)
    log_student = jax.nn.log_softmax(student_logits, axis=1)
    log_teacher = jax.nn.log_softmax(teacher_logits, axis=1)
    prob_student = jnp.exp(log_student)
    log_ratio = log_student - log_teacher
    divergence = lax.optimization_barrier(jnp.sum(prob_student * log_ratio, axis=1))
    lengths_f32 = lengths.astype(jnp.float32)
    valid = positions[None, :] < lengths[:, None]
    token_weight = jnp.where(valid, 1.0 / lengths_f32[:, None], jnp.zeros_like(lengths_f32)[:, None]).reshape(-1)
    loss = jnp.sum(token_weight * divergence)
    logit_grad = (token_weight[:, None] * prob_student * (log_ratio - divergence[:, None])).astype(jnp.bfloat16)
    blocks = N_GRP * N_VOC
    grad_blocks = logit_grad.reshape(TOKENS, blocks, VOC_DEV).transpose(1, 0, 2)
    normed_t = normed.T

    def head_block(block):
        return jnp.dot(normed_t, block, preferred_element_type=jnp.float32).astype(jnp.bfloat16)
    grad_head = lax.map(head_block, grad_blocks).transpose(1, 0, 2).reshape(DS, VOCAB)
    normed_grad = jnp.dot(logit_grad, student_head.T, preferred_element_type=jnp.float32)
    grad_gain = lax.optimization_barrier(jnp.sum(normed_grad * hidden_f32 * inverse_rms[:, None], axis=0))
    scaled = normed_grad * norm_gain[None, :]
    inner = lax.optimization_barrier(jnp.sum(scaled * hidden_f32, axis=1))
    grad_hidden = inverse_rms[:, None] * scaled - hidden_f32 * (inverse_rms ** 3)[:, None] * inner[:, None] / DS
    return (loss, grad_hidden.astype(jnp.bfloat16), grad_gain, grad_head)
```

```python
import jax
import jax.numpy as jnp
from jax import lax
from jax.sharding import PartitionSpec as P

DS = 4096
SEQ = 2
VALID = 240
LANES = 256
EPSILON = 1e-06
BF = jnp.bfloat16
F32 = jnp.float32
CORE_SWAP = [(i, i ^ 1) for i in range(16)]


def rounded(x):
    return lax.reduce_precision(x, 8, 7)


def lane_tables(episode_source, lengths):
    episodes = lengths.shape[0]
    two = (lengths == 2).astype(jnp.int32)
    before = jnp.arange(episodes)[None, :] < jnp.arange(episodes)[:, None]
    rank = jnp.sum(jnp.where(before, two[None, :], 0), axis=1)
    lane = jnp.arange(LANES, dtype=jnp.int32)
    number = jnp.arange(episodes, dtype=jnp.int32)
    first = lane[None, :] == number[:, None]
    second = (two[:, None] == 1) & (lane[None, :] == episodes + rank[:, None])
    pick = first | second
    position = (lane >= episodes).astype(jnp.int32)
    inside = lane < VALID
    episode = jnp.sum(jnp.where(pick, number[:, None], 0), axis=0)
    source = jnp.sum(jnp.where(pick, episode_source[:, None], 0), axis=0)
    length = jnp.sum(jnp.where(pick, lengths[:, None], 0), axis=0)
    student_row = jnp.where(inside, episode * SEQ + position, -1)
    teacher_row = jnp.where(inside, source * SEQ + position, -1)
    weight = jnp.where(inside, 1.0 / jnp.maximum(length, 1).astype(F32), 0.0)
    return student_row, teacher_row, weight


def combine(stats):
    top_s, sum_s, top_t, sum_t, mean_d, mean_u, mean_du = [stats[:, k] for k in range(7)]
    all_s = jnp.max(top_s, axis=0)
    all_t = jnp.max(top_t, axis=0)
    shift_s = top_s - all_s[None]
    shift_t = top_t - all_t[None]
    scale_s = jnp.exp(shift_s)
    scale_t = jnp.exp(shift_t)
    shift_d = shift_s - shift_t
    out = [
        all_s,
        jnp.sum(scale_s * sum_s, axis=0),
        all_t,
        jnp.sum(scale_t * sum_t, axis=0),
        jnp.sum(scale_s * (mean_d + shift_d * sum_s), axis=0),
        jnp.sum(scale_s * (mean_u + shift_s * sum_s), axis=0),
        jnp.sum(
            scale_s
            * (mean_du + shift_s * mean_d + shift_d * mean_u + shift_s * shift_d * sum_s),
            axis=0,
        ),
    ]
    return jnp.stack(out + [jnp.zeros_like(all_s)])


def spread(x, axis):
    count = lax.axis_size(axis)
    return lax.all_to_all(jnp.broadcast_to(x[None], (count,) + x.shape), axis, 0, 0, tiled=True)


def with_gain(total):
    gain = total[..., VALID : VALID + 1] + total[..., VALID + 1 : VALID + 2]
    high = rounded(gain)
    lane = lax.broadcasted_iota(jnp.int32, total.shape, total.ndim - 1)
    kept = jnp.where(lane == VALID, high, jnp.where(lane == VALID + 1, gain - high, total))
    return kept.astype(BF)


def local(
    student_hidden, norm_gain, teacher_hidden, student_head, teacher_head, episode_source, lengths
):
    groups = lax.axis_size("grp")
    voc = lax.axis_size("voc")
    group_index = lax.axis_index("grp")
    core = group_index % 2
    rows = student_hidden.shape[0]
    half_s = student_hidden.shape[1] // 2
    half_t = teacher_hidden.shape[1] // 2
    half = half_s + half_t
    student_row, teacher_row, weight = lane_tables(episode_source, lengths)
    row_ids = jnp.arange(groups * rows, dtype=jnp.int32)
    lane = jnp.arange(LANES, dtype=jnp.int32)
    select_s = (row_ids[:, None] == student_row[None, :]).astype(BF)
    select_t = (row_ids[:, None] == teacher_row[None, :]).astype(BF)

    both = jnp.stack(
        [
            jnp.concatenate([student_hidden[:, :half_s], teacher_hidden[:, :half_t]], axis=1),
            jnp.concatenate([student_hidden[:, half_s:], teacher_hidden[:, half_t:]], axis=1),
        ]
    )
    outgoing = jnp.broadcast_to(both[None], (groups // 2, 2, rows, half)).reshape(groups, rows, half)
    held = lax.all_to_all(outgoing, "grp", 0, 0, tiled=True).reshape(groups * rows, half)

    transposed = (((0,), (0,)), ((), ()))
    block_s = lax.dot_general(
        held[:, :half_s], select_s, transposed, preferred_element_type=F32
    )
    block_t = lax.dot_general(
        held[:, half_s:], select_t, transposed, preferred_element_type=F32
    )
    gain_half = lax.dynamic_slice_in_dim(norm_gain, core * half_s, half_s)[:, None]
    gain_high = rounded(gain_half)
    gain_mid = rounded(gain_half - gain_high)
    gain_low = gain_half - gain_high - gain_mid
    block_s = jnp.where(
        lane == VALID,
        gain_high,
        jnp.where(lane == VALID + 1, gain_mid, jnp.where(lane == VALID + 2, gain_low, block_s)),
    )
    block = jnp.concatenate([block_s.astype(BF), block_t.astype(BF)], axis=0)
    mine = spread(block, "voc")
    other = lax.ppermute(mine, "grp", CORE_SWAP)
    ordered = jnp.stack(
        [jnp.where(core == 0, mine, other), jnp.where(core == 0, other, mine)], axis=1
    )
    hidden_t = ordered[:, :, :half_s].reshape(DS, LANES).astype(F32)
    teacher_t = ordered[:, :, half_s:].reshape(-1, LANES)

    gain = jnp.sum(hidden_t[:, VALID : VALID + 3], axis=1, keepdims=True)
    inverse_rms = lax.rsqrt(jnp.sum(hidden_t * hidden_t, axis=0) / DS + EPSILON)
    inside = lane < VALID
    scaled_rows = jnp.where(inside, hidden_t * inverse_rms, 0.0)
    normed_t = (scaled_rows * gain).astype(BF)

    student = lax.dot_general(student_head, normed_t, transposed, preferred_element_type=F32)
    teacher = lax.dot_general(teacher_head, teacher_t, transposed, preferred_element_type=F32)
    top_s = jnp.max(student, axis=0)
    top_t = jnp.max(teacher, axis=0)
    below = student - top_s
    exp_s = jnp.exp(below)
    below_t = teacher - top_t
    ratio = below - below_t
    stats = jnp.stack(
        [
            top_s,
            jnp.sum(exp_s, axis=0),
            top_t,
            jnp.sum(jnp.exp(below_t), axis=0),
            jnp.sum(exp_s * ratio, axis=0),
            jnp.sum(exp_s * below, axis=0),
            jnp.sum(exp_s * ratio * below, axis=0),
            jnp.zeros_like(top_s),
        ]
    )
    stats = combine(spread(stats, "voc"))
    stats = combine(spread(stats, "grp"))
    all_s, total_s, all_t, total_t = stats[0], stats[1], stats[2], stats[3]
    mean_d = stats[4] / total_s
    mean_u = stats[5] / total_s
    covariance = stats[6] / total_s - mean_d * mean_u
    divergence = mean_d - jnp.log(total_s) + jnp.log(total_t)
    loss = jnp.sum(weight * divergence)
    factor = weight * jnp.exp(top_s - all_s) / total_s
    offset = (top_s - all_s) - (top_t - all_t) - mean_d
    grad_t = (factor * exp_s * (ratio + offset)).astype(BF)

    term = lax.dot_general(
        student_head, grad_t, (((1,), (0,)), ((), ())), preferred_element_type=F32
    )
    gain_term = jnp.sum(term * scaled_rows, axis=1, keepdims=True)
    gain_top = rounded(gain_term)
    term = jnp.where(
        lane == VALID, gain_top, jnp.where(lane == VALID + 1, gain_term - gain_top, term)
    ).astype(BF)
    term = term.reshape(voc, 2, half_s, LANES)
    away = lax.dynamic_index_in_dim(term, 1 - core, 1, keepdims=False)
    stay = lax.dynamic_index_in_dim(term, core, 1, keepdims=False)
    arrived = lax.ppermute(away, "grp", CORE_SWAP)
    grad_head = lax.dot_general(
        normed_t, grad_t, (((1,), (1,)), ((), ())), preferred_element_type=F32
    ).astype(BF)
    pair = with_gain(stay.astype(F32) + arrived.astype(F32))
    pieces = lax.all_to_all(pair, "voc", 0, 0, tiled=True)
    feature_sum = with_gain(jnp.sum(pieces.astype(F32), axis=0))

    extra = 8
    slot = jnp.arange(rows + extra, dtype=jnp.int32)
    wanted = jnp.where(
        slot[None, :] < rows,
        jnp.arange(groups, dtype=jnp.int32)[:, None] * rows + slot[None, :],
        -2,
    )
    lane_row = jnp.where(inside, student_row, -1)
    select_out = (wanted[:, :, None] == lane_row) | (
        (slot[None, :, None] >= rows) & (lane == slot[None, :, None] - rows + VALID) & (lane < VALID + 2)
    )
    outgoing = lax.dot_general(
        select_out.reshape(-1, LANES).astype(BF),
        feature_sum,
        (((1,), (1,)), ((), ())),
        preferred_element_type=F32,
    ).astype(BF).reshape(groups, rows + extra, half_s)
    pieces = lax.all_to_all(outgoing, "grp", 0, 0, tiled=True)
    total = jnp.sum(pieces.reshape(groups // 2, 2, rows + extra, half_s).astype(F32), axis=0)
    total = jnp.concatenate([total[0], total[1]], axis=1)
    normed_grad = total[:rows]
    grad_gain = total[rows] + total[rows + 1]

    own = (group_index * rows + jnp.arange(rows, dtype=jnp.int32))[:, None] == student_row[None, :]
    own_rms = jnp.sum(jnp.where(own, inverse_rms, 0.0), axis=1, keepdims=True)
    pull = weight * covariance * inverse_rms * inverse_rms / DS
    own_pull = jnp.sum(jnp.where(own, pull, 0.0), axis=1, keepdims=True)
    grad_hidden = own_rms * (normed_grad * norm_gain) - student_hidden.astype(F32) * own_pull
    return (loss, grad_hidden.astype(BF), grad_gain, grad_head)


def solution(mesh):
    placed = (
        P("grp", "voc"),
        P("voc"),
        P("grp", "voc"),
        P(None, ("grp", "voc")),
        P(None, ("grp", "voc")),
        P(),
        P(),
    )
    return jax.shard_map(
        local,
        mesh=mesh,
        in_specs=placed,
        out_specs=(P(), P("grp", "voc"), P("voc"), P(None, ("grp", "voc"))),
        check_vma=False,
    )
```

```python
import jax
import jax.numpy as jnp
from jax import lax
from jax.experimental import pallas as pl
from jax.experimental.pallas import tpu as pltpu
from jax.sharding import PartitionSpec as P

DS = 4096
SEQ = 2
VALID = 240
LANES = 256
EPSILON = 1e-06
GROUPS = 16
VOC = 16
ROWS = 24
HALF_S = 128
HALF_T = 160
HALF = HALF_S + HALF_T
VOC_DEV = 384
STATS = 8
SEND = 32
CHUNKS = 4
PER = VOC // CHUNKS
BF = jnp.bfloat16
F32 = jnp.float32
CORE_SWAP = [(i, i ^ 1) for i in range(GROUPS)]
TN = (((0,), (0,)), ((), ()))
NT = (((1,), (1,)), ((), ()))
NN = (((1,), (0,)), ((), ()))


def rounded(x):
    return lax.reduce_precision(x, 8, 7)


def dot(a, b, dims):
    return lax.dot_general(a, b, dims, preferred_element_type=F32)


def lane_tables(episode_source, lengths):
    episodes = lengths.shape[0]
    two = (lengths == 2).astype(jnp.int32)
    before = jnp.arange(episodes)[None, :] < jnp.arange(episodes)[:, None]
    rank = jnp.sum(jnp.where(before, two[None, :], 0), axis=1)
    lane = jnp.arange(LANES, dtype=jnp.int32)
    number = jnp.arange(episodes, dtype=jnp.int32)
    first = lane[None, :] == number[:, None]
    second = (two[:, None] == 1) & (lane[None, :] == episodes + rank[:, None])
    pick = first | second
    position = (lane >= episodes).astype(jnp.int32)
    inside = lane < VALID
    episode = jnp.sum(jnp.where(pick, number[:, None], 0), axis=0)
    source = jnp.sum(jnp.where(pick, episode_source[:, None], 0), axis=0)
    length = jnp.sum(jnp.where(pick, lengths[:, None], 0), axis=0)
    student_row = jnp.where(inside, episode * SEQ + position, -1)
    teacher_row = jnp.where(inside, source * SEQ + position, -1)
    weight = jnp.where(inside, 1.0 / jnp.maximum(length, 1).astype(F32), 0.0)
    return student_row[None], teacher_row[None], weight[None]


def own_core():
    return lax.rem(lax.axis_index("grp"), 2)


def lane_iota(shape):
    return lax.broadcasted_iota(jnp.int32, shape, len(shape) - 1)


def pack_kernel(student, teacher, out):
    for c in range(2):
        half = jnp.concatenate(
            [
                student[:, c * HALF_S : (c + 1) * HALF_S],
                teacher[:, c * HALF_T : (c + 1) * HALF_T],
            ],
            axis=1,
        )
        for z in range(GROUPS // 2):
            out[2 * z + c] = half


def compact_kernel(held, student_row, teacher_row, gain, out):
    rows = jnp.concatenate([held[g].astype(F32) for g in range(GROUPS)], axis=0).astype(BF)
    ids = lax.broadcasted_iota(jnp.int32, (GROUPS * ROWS, LANES), 0)
    pick_s = jnp.where(ids == student_row[...], 1.0, 0.0).astype(BF)
    pick_t = jnp.where(ids == teacher_row[...], 1.0, 0.0).astype(BF)
    part = lax.broadcasted_iota(jnp.int32, (16, LANES), 0)
    place = jnp.where(lane_iota((16, LANES)) == part + VALID, 1.0, 0.0).astype(BF)
    block_s = dot(rows[:, :HALF_S], pick_s, TN) + dot(gain[...].astype(BF), place, TN)
    block_t = dot(rows[:, HALF_S:], pick_t, TN)
    block_s = block_s.astype(BF)
    block_t = block_t.astype(BF)
    for v in range(VOC):
        out[v, :HALF_S, :] = block_s
        out[v, HALF_S:, :] = block_t


def stack_rows(values):
    row = lax.broadcasted_iota(jnp.int32, (STATS, LANES), 0)
    out = jnp.zeros((STATS, LANES), F32)
    for k, value in enumerate(values):
        out = jnp.where(row == k, value, out)
    return out


def combined(stats):
    top_s, sum_s, top_t, sum_t, mean_d, mean_u, mean_du = [
        stats[:, k, :] for k in range(7)
    ]
    all_s = jnp.max(top_s, axis=0, keepdims=True)
    all_t = jnp.max(top_t, axis=0, keepdims=True)
    shift_s = top_s - all_s
    shift_t = top_t - all_t
    scale_s = jnp.exp(shift_s)
    scale_t = jnp.exp(shift_t)
    shift_d = shift_s - shift_t

    def total(x):
        return jnp.sum(x, axis=0, keepdims=True)

    return (
        all_s,
        total(scale_s * sum_s),
        all_t,
        total(scale_t * sum_t),
        total(scale_s * (mean_d + shift_d * sum_s)),
        total(scale_s * (mean_u + shift_s * sum_s)),
        total(
            scale_s
            * (mean_du + shift_s * mean_d + shift_d * mean_u + shift_s * shift_d * sum_s)
        ),
    )


def forward_kernel(
    mine, other, student_head, teacher_head,
    normed, exp_out, ratio_out, stats_out, inverse_out,
    rows_s, rows_t, head_s, head_t, row_sems, head_sems,
):
    core = own_core()
    copies = []
    for k, (block, place) in enumerate(((mine, core), (other, 1 - core))):
        copies.append(
            pltpu.make_async_copy(
                block.at[:, pl.ds(0, HALF_S), :], rows_s.at[:, place], row_sems.at[2 * k]
            )
        )
        copies.append(
            pltpu.make_async_copy(
                block.at[:, pl.ds(HALF_S, HALF_T), :], rows_t.at[:, place], row_sems.at[2 * k + 1]
            )
        )
    for copy in copies:
        copy.start()
    heads = []
    for j in range(CHUNKS):
        span_s = pl.ds(j * (DS // CHUNKS), DS // CHUNKS)
        span_t = pl.ds(j * (VOC * 2 * HALF_T // CHUNKS), VOC * 2 * HALF_T // CHUNKS)
        heads.append(
            (
                pltpu.make_async_copy(
                    student_head.at[span_s], head_s.at[span_s], head_sems.at[0, j]
                ),
                pltpu.make_async_copy(
                    teacher_head.at[span_t], head_t.at[span_t], head_sems.at[1, j]
                ),
            )
        )
    for copy_s, _ in heads:
        copy_s.start()
    for _, copy_t in heads:
        copy_t.start()
    for copy in copies:
        copy.wait()

    squares = jnp.zeros((1, LANES), F32)
    for v in range(VOC):
        part = rows_s[v].reshape(2 * HALF_S, LANES).astype(F32)
        squares = squares + jnp.sum(part * part, axis=0, keepdims=True)
    inverse = lax.rsqrt(squares / DS + EPSILON)
    inverse_out[...] = inverse
    kept = jnp.where(lane_iota((1, LANES)) < VALID, inverse, 0.0)
    for v in range(VOC):
        part = rows_s[v].reshape(2 * HALF_S, LANES).astype(F32)
        gain = (
            part[:, VALID : VALID + 1]
            + part[:, VALID + 1 : VALID + 2]
            + part[:, VALID + 2 : VALID + 3]
        )
        normed[pl.ds(v * 2 * HALF_S, 2 * HALF_S), :] = (part * kept * gain).astype(BF)

    student = jnp.zeros((VOC_DEV, LANES), F32)
    for j in range(CHUNKS):
        span = pl.ds(j * (DS // CHUNKS), DS // CHUNKS)
        heads[j][0].wait()
        student = student + dot(head_s[span, :], normed[span, :], TN)
    teacher = jnp.zeros((VOC_DEV, LANES), F32)
    for j in range(CHUNKS):
        size = VOC * 2 * HALF_T // CHUNKS
        heads[j][1].wait()
        rows = rows_t[pl.ds(j * PER, PER)].reshape(size, LANES)
        teacher = teacher + dot(head_t[pl.ds(j * size, size), :], rows, TN)

    top_s = jnp.max(student, axis=0, keepdims=True)
    top_t = jnp.max(teacher, axis=0, keepdims=True)
    below = student - top_s
    exp_s = jnp.exp(below)
    below_t = teacher - top_t
    ratio = below - below_t
    exp_out[...] = exp_s
    ratio_out[...] = ratio

    def total(x):
        return jnp.sum(x, axis=0, keepdims=True)

    weighted = exp_s * ratio
    stats = stack_rows(
        [
            top_s,
            total(exp_s),
            top_t,
            total(jnp.exp(below_t)),
            total(weighted),
            total(exp_s * below),
            total(weighted * below),
        ]
    )
    for v in range(VOC):
        stats_out[v] = stats


def combine_kernel(stats, out):
    tile = stack_rows(combined(stats))
    for g in range(GROUPS):
        out[g] = tile


def with_gain(total):
    lane = lane_iota(total.shape)
    gain = total[:, VALID : VALID + 1] + total[:, VALID + 1 : VALID + 2]
    return place_gain(total, gain, lane)


def place_gain(total, gain, lane):
    high = gain.astype(BF).astype(F32)
    low = gain - high
    return jnp.where(lane == VALID, high, jnp.where(lane == VALID + 1, low, total)).astype(BF)


def backward_kernel(
    stats, local_stats, exp_in, ratio_in, weight, inverse, student_head, normed,
    grad_out, stay, away, pull_out, loss_out,
    head_s, rows, sems,
):
    core = own_core()
    size = DS // CHUNKS
    copies = []
    for j in range(CHUNKS):
        span = pl.ds(j * size, size)
        copies.append(
            (
                pltpu.make_async_copy(student_head.at[span], head_s.at[span], sems.at[0, j]),
                pltpu.make_async_copy(normed.at[span], rows.at[span], sems.at[1, j]),
            )
        )
    for pair in copies:
        pair[0].start()
        pair[1].start()
    all_s, total_s, all_t, total_t, sum_d, sum_u, sum_du = combined(stats)
    mean_d = sum_d / total_s
    mean_u = sum_u / total_s
    covariance = sum_du / total_s - mean_d * mean_u
    divergence = mean_d - jnp.log(total_s) + jnp.log(total_t)
    loss_out[...] = jnp.sum(weight[...] * divergence, axis=1, keepdims=True)
    pull_out[...] = weight[...] * covariance * inverse[...] * inverse[...] / DS
    shift_s = local_stats[0:1, :] - all_s
    shift_t = local_stats[2:3, :] - all_t
    factor = weight[...] * jnp.exp(shift_s) / total_s
    offset = shift_s - shift_t - mean_d
    grad = (factor * exp_in[...] * (ratio_in[...] + offset)).astype(BF)
    grad_out[...] = grad
    lane = lane_iota((2 * HALF_S, LANES))
    for j in range(CHUNKS):
        copies[j][0].wait()
        copies[j][1].wait()
        for i in range(PER):
            v = j * PER + i
            span = pl.ds(v * 2 * HALF_S, 2 * HALF_S)
            term = dot(head_s[span, :], grad, NN)
            gain = jnp.sum(term * rows[span, :].astype(F32), axis=1, keepdims=True)
            term = place_gain(term, gain, lane)
            first, second = term[:HALF_S], term[HALF_S:]
            stay[v] = jnp.where(core == 0, first, second)
            away[v] = jnp.where(core == 0, second, first)


def pair_kernel(stay, arrived, out):
    for v in range(VOC):
        out[v] = with_gain(stay[v].astype(F32) + arrived[v].astype(F32))


def send_kernel(pieces, student_row, out):
    total = pieces[0].astype(F32)
    for v in range(1, VOC):
        total = total + pieces[v].astype(F32)
    total = with_gain(total)
    slot = lax.broadcasted_iota(jnp.int32, (SEND, LANES), 0)
    extra = (slot >= ROWS) & (slot < ROWS + 2) & (lane_iota((SEND, LANES)) == slot - ROWS + VALID)
    for g in range(GROUPS):
        pick = ((slot < ROWS) & (student_row[...] == slot + g * ROWS)) | extra
        out[g] = dot(jnp.where(pick, 1.0, 0.0).astype(BF), total, NT).astype(BF)


def finish_kernel(pieces, hidden, gain, student_row, inverse, pull, grad_hidden, grad_gain):
    halves = []
    for c in range(2):
        total = pieces[c].astype(F32)
        for z in range(1, GROUPS // 2):
            total = total + pieces[2 * z + c].astype(F32)
        halves.append(total)
    total = jnp.concatenate(halves, axis=1)
    grad_gain[...] = (total[ROWS : ROWS + 1] + total[ROWS + 1 : ROWS + 2]) / gain[...]
    first = lax.axis_index("grp") * ROWS
    own = lax.broadcasted_iota(jnp.int32, (ROWS, LANES), 0) + first == student_row[...]
    own_rms = jnp.sum(jnp.where(own, inverse[...], 0.0), axis=1, keepdims=True)
    own_pull = jnp.sum(jnp.where(own, pull[...], 0.0), axis=1, keepdims=True)
    normed_grad = total[:ROWS]
    result = own_rms * (normed_grad * gain[...]) - hidden[...].astype(F32) * own_pull
    grad_hidden[...] = result.astype(BF)


def shape(dims, dtype):
    return jax.ShapeDtypeStruct(dims, dtype)


def params(mib):
    return pltpu.CompilerParams(vmem_limit_bytes=mib * 1024 * 1024)


def exchange(x, axis):
    return lax.all_to_all(x, axis, 0, 0, tiled=True)


ANY = pl.BlockSpec(memory_space=pl.ANY)
VMEM = pl.BlockSpec(memory_space=pltpu.VMEM)


def local(
    student_hidden, norm_gain, teacher_hidden, student_head, teacher_head, episode_source, lengths
):
    core = own_core()
    width_t = VOC * 2 * HALF_T
    row = shape((1, LANES), F32)
    student_row, teacher_row, weight = lane_tables(episode_source, lengths)

    packed = pl.pallas_call(
        pack_kernel, out_shape=shape((GROUPS, ROWS, HALF), BF), compiler_params=params(16)
    )(student_hidden, teacher_hidden)
    held = exchange(packed, "grp")

    gain_half = lax.dynamic_slice_in_dim(norm_gain, core * HALF_S, HALF_S)
    gain_high = rounded(gain_half)
    gain_mid = rounded(gain_half - gain_high)
    gain_low = gain_half - gain_high - gain_mid
    gain_parts = jnp.concatenate(
        [jnp.stack([gain_high, gain_mid, gain_low]), jnp.zeros((13, HALF_S), F32)], axis=0
    )
    block = pl.pallas_call(
        compact_kernel, out_shape=shape((VOC, HALF, LANES), BF), compiler_params=params(16)
    )(held, student_row, teacher_row, gain_parts)
    mine = exchange(block, "voc")
    other = lax.ppermute(mine, "grp", CORE_SWAP)

    normed, exp_s, ratio, stats, inverse = pl.pallas_call(
        forward_kernel,
        out_shape=(
            shape((DS, LANES), BF),
            shape((VOC_DEV, LANES), F32),
            shape((VOC_DEV, LANES), F32),
            shape((VOC, STATS, LANES), F32),
            row,
        ),
        in_specs=[ANY] * 4,
        scratch_shapes=[
            pltpu.VMEM((VOC, 2, HALF_S, LANES), BF),
            pltpu.VMEM((VOC, 2, HALF_T, LANES), BF),
            pltpu.VMEM((DS, VOC_DEV), BF),
            pltpu.VMEM((width_t, VOC_DEV), BF),
            pltpu.SemaphoreType.DMA((4,)),
            pltpu.SemaphoreType.DMA((2, CHUNKS)),
        ],
        compiler_params=params(32),
    )(mine, other, student_head, teacher_head)

    from_voc = exchange(stats, "voc")
    spread = pl.pallas_call(
        combine_kernel, out_shape=shape((GROUPS, STATS, LANES), F32), compiler_params=params(16)
    )(from_voc)
    from_grp = exchange(spread, "grp")

    grad, stay, away, pull, loss = pl.pallas_call(
        backward_kernel,
        out_shape=(
            shape((VOC_DEV, LANES), BF),
            shape((VOC, HALF_S, LANES), BF),
            shape((VOC, HALF_S, LANES), BF),
            row,
            shape((1, 1), F32),
        ),
        in_specs=[VMEM] * 6 + [ANY] * 2,
        scratch_shapes=[
            pltpu.VMEM((DS, VOC_DEV), BF),
            pltpu.VMEM((DS, LANES), BF),
            pltpu.SemaphoreType.DMA((2, CHUNKS)),
        ],
        compiler_params=params(32),
    )(from_grp, stats[0], exp_s, ratio, weight, inverse, student_head, normed)

    arrived = lax.ppermute(away, "grp", CORE_SWAP)
    grad_head = dot(normed, grad, NT).astype(BF)
    pair = pl.pallas_call(
        pair_kernel, out_shape=shape((VOC, HALF_S, LANES), BF), compiler_params=params(16)
    )(stay, arrived)
    pieces = exchange(pair, "voc")
    outgoing = pl.pallas_call(
        send_kernel, out_shape=shape((GROUPS, SEND, HALF_S), BF), compiler_params=params(16)
    )(pieces, student_row)
    pieces = exchange(outgoing, "grp")
    grad_hidden, grad_gain = pl.pallas_call(
        finish_kernel, out_shape=(shape((ROWS, 2 * HALF_S), BF), row), compiler_params=params(16)
    )(pieces, student_hidden, norm_gain[None], student_row, inverse, pull)
    return (loss.reshape(()), grad_hidden, grad_gain.reshape(-1), grad_head)


def solution(mesh):
    placed = (
        P("grp", "voc"),
        P("voc"),
        P("grp", "voc"),
        P(None, ("grp", "voc")),
        P(None, ("grp", "voc")),
        P(),
        P(),
    )
    return jax.shard_map(
        local,
        mesh=mesh,
        in_specs=placed,
        out_specs=(P(), P("grp", "voc"), P("voc"), P(None, ("grp", "voc"))),
        check_vma=False,
    )
```

```python
import jax
import jax.numpy as jnp
from jax import lax
from jax.experimental import pallas as pl
from jax.experimental.pallas import tpu as pltpu
from jax.sharding import PartitionSpec as P

DS = 4096
SEQ = 2
VALID = 240
LANES = 256
EPSILON = 1e-06
GROUPS = 16
VOC = 16
ROWS = 24
HALF_S = 128
HALF_T = 160
HALF = HALF_S + HALF_T
VOC_DEV = 384
STATS = 8
SEND = 32
PER = 4
SPARE = 16
BF = jnp.bfloat16
F32 = jnp.float32
CORE_SWAP = [(i, i ^ 1) for i in range(GROUPS)]
TN = (((0,), (0,)), ((), ()))
NT = (((1,), (1,)), ((), ()))
NN = (((1,), (0,)), ((), ()))


def rounded(x):
    return lax.reduce_precision(x, 8, 7)


def dot(a, b, dims):
    return lax.dot_general(a, b, dims, preferred_element_type=F32)


def lane_tables(episode_source, lengths):
    episodes = lengths.shape[0]
    two = (lengths == 2).astype(jnp.int32)
    before = jnp.arange(episodes)[None, :] < jnp.arange(episodes)[:, None]
    rank = jnp.sum(jnp.where(before, two[None, :], 0), axis=1)
    lane = jnp.arange(LANES, dtype=jnp.int32)
    number = jnp.arange(episodes, dtype=jnp.int32)
    first = lane[None, :] == number[:, None]
    second = (two[:, None] == 1) & (lane[None, :] == episodes + rank[:, None])
    pick = first | second
    position = (lane >= episodes).astype(jnp.int32)
    inside = lane < VALID
    episode = jnp.sum(jnp.where(pick, number[:, None], 0), axis=0)
    source = jnp.sum(jnp.where(pick, episode_source[:, None], 0), axis=0)
    length = jnp.sum(jnp.where(pick, lengths[:, None], 0), axis=0)
    student_row = jnp.where(inside, episode * SEQ + position, -1)
    teacher_row = jnp.where(inside, source * SEQ + position, -1)
    weight = jnp.where(inside, 1.0 / jnp.maximum(length, 1).astype(F32), 0.0)
    return student_row[None], teacher_row[None], weight[None]


def own_core():
    return lax.rem(lax.axis_index("grp"), 2)


def lane_iota(shape):
    return lax.broadcasted_iota(jnp.int32, shape, len(shape) - 1)


def pack_kernel(student_in, teacher_in, out, student, teacher, sems):
    copies = [
        pltpu.make_async_copy(student_in, student, sems.at[0]),
        pltpu.make_async_copy(teacher_in, teacher, sems.at[1]),
    ]
    for copy in copies:
        copy.start()
    for copy in copies:
        copy.wait()
    for c in range(2):
        half = jnp.concatenate(
            [
                student[:, c * HALF_S : (c + 1) * HALF_S],
                teacher[:, c * HALF_T : (c + 1) * HALF_T],
            ],
            axis=1,
        )
        for z in range(GROUPS // 2):
            out[2 * z + c] = half


def spare_lanes():
    source = lax.broadcasted_iota(jnp.int32, (LANES, LANES), 0)
    lane = lane_iota((LANES, LANES))
    return jnp.where(lane == VALID + lax.rem(source, SPARE), 1.0, 0.0).astype(BF)


def spare_rows():
    row = lax.broadcasted_iota(jnp.int32, (SPARE, LANES), 0)
    return lax.div(lane_iota((SPARE, LANES)), SPARE) == row


def split(x, parts):
    out = []
    for _ in range(parts):
        out.append(x.astype(BF))
        x = x - out[-1].astype(F32)
    return out


def compact_kernel(held, student_row, teacher_row, gain, out):
    rows = jnp.concatenate([held[g].astype(F32) for g in range(GROUPS)], axis=0).astype(BF)
    ids = lax.broadcasted_iota(jnp.int32, (GROUPS * ROWS, LANES), 0)
    pick_s = jnp.where(ids == student_row[...], 1.0, 0.0).astype(BF)
    pick_t = jnp.where(ids == teacher_row[...], 1.0, 0.0).astype(BF)
    block_s = dot(rows[:, :HALF_S], pick_s, TN)
    block_t = dot(rows[:, HALF_S:], pick_t, TN).astype(BF)
    spread_gain = dot(gain[...].astype(BF), jnp.ones((16, LANES), BF), TN)
    squares = jnp.sum(block_s * block_s, axis=0, keepdims=True)
    parts = split(jnp.where(spare_rows(), squares, 0.0), 2)
    lanes = spare_lanes()
    spare = jnp.concatenate([dot(part, lanes, NN) for part in parts], axis=0)
    block_s = block_s * spread_gain
    block_s = jnp.concatenate([block_s[: 2 * SPARE] + spare, block_s[2 * SPARE :]], axis=0)
    block_s = block_s.astype(BF)
    for v in range(VOC):
        out[v, :HALF_S, :] = block_s
        out[v, HALF_S:, :] = block_t


def stack_rows(values):
    row = lax.broadcasted_iota(jnp.int32, (STATS, LANES), 0)
    out = jnp.zeros((STATS, LANES), F32)
    for k, value in enumerate(values):
        out = jnp.where(row == k, value, out)
    return out


def total(x):
    return jnp.sum(x, axis=0, keepdims=True)


def combined(stats):
    top_s, sum_s, top_t, sum_t, mean_d, mean_u, mean_du = [stats[:, k, :] for k in range(7)]
    all_s = jnp.max(top_s, axis=0, keepdims=True)
    all_t = jnp.max(top_t, axis=0, keepdims=True)
    shift_s = top_s - all_s
    shift_t = top_t - all_t
    scale_s = jnp.exp(shift_s)
    scale_t = jnp.exp(shift_t)
    shift_d = shift_s - shift_t
    return (
        all_s,
        total(scale_s * sum_s),
        all_t,
        total(scale_t * sum_t),
        total(scale_s * (mean_d + shift_d * sum_s)),
        total(scale_s * (mean_u + shift_s * sum_s)),
        total(
            scale_s
            * (mean_du + shift_s * mean_d + shift_d * mean_u + shift_s * shift_d * sum_s)
        ),
    )


def span_of(v, core, half):
    return pl.ds(pl.multiple_of(v * 2 * half + core * half, 32), half)


def logits_of(rows, student_head, teacher_head, core):
    student = jnp.zeros((VOC_DEV, LANES), F32)
    teacher = jnp.zeros((VOC_DEV, LANES), F32)
    squares = jnp.zeros((SPARE, LANES), F32)
    for j in range(0, VOC, PER):
        group = range(j, j + PER)
        head_s = jnp.concatenate([student_head[span_of(v, core, HALF_S), :] for v in group], axis=0)
        head_t = jnp.concatenate([teacher_head[span_of(v, core, HALF_T), :] for v in group], axis=0)
        rows_s = jnp.concatenate([rows[v, :HALF_S, :] for v in group], axis=0)
        rows_t = jnp.concatenate([rows[v, HALF_S:, :] for v in group], axis=0)
        student = student + dot(head_s, rows_s, TN)
        teacher = teacher + dot(head_t, rows_t, TN)
        for v in group:
            squares = squares + rows[v, :SPARE, :].astype(F32)
            squares = squares + rows[v, SPARE : 2 * SPARE, :].astype(F32)
    return student, teacher, squares


def forward_one(mine, student_head, teacher_head, student_out, teacher_out, squares_out):
    student, teacher, squares = logits_of(mine, student_head, teacher_head, own_core())
    student_out[...] = student
    teacher_out[...] = teacher
    squares_out[...] = squares


def forward_two(
    other, student_head, teacher_head, student_in, teacher_in, squares_in,
    exp_out, ratio_out, stats_out, tops_out, inverse_out,
):
    student, teacher, squares = logits_of(other, student_head, teacher_head, 1 - own_core())
    squares = squares + squares_in[...]
    squares = jnp.where(lane_iota((SPARE, LANES)) >= VALID, squares, 0.0)
    lanes = spare_lanes()
    by_row = sum(dot(part, lanes, NT) for part in split(squares, 3))
    squares = total(jnp.where(spare_rows(), by_row, 0.0))
    inverse = lax.rsqrt(squares / DS + EPSILON)
    inverse_out[...] = inverse
    student = (student + student_in[...]) * inverse
    teacher = teacher + teacher_in[...]

    top_s = jnp.max(student, axis=0, keepdims=True)
    top_t = jnp.max(teacher, axis=0, keepdims=True)
    below = student - top_s
    exp_s = jnp.exp(below)
    below_t = teacher - top_t
    ratio = below - below_t
    exp_out[...] = exp_s
    ratio_out[...] = ratio
    weighted = exp_s * ratio
    stats = stack_rows(
        [
            top_s,
            total(exp_s),
            top_t,
            total(jnp.exp(below_t)),
            total(weighted),
            total(exp_s * below),
            total(weighted * below),
        ]
    )
    tops_out[...] = stats
    for v in range(VOC):
        stats_out[v] = stats


def combine_kernel(stats, out):
    tile = stack_rows(combined(stats))
    for g in range(GROUPS):
        out[g] = tile


def terms_of(rows, student_head, grad, kept, core, out):
    source = lax.broadcasted_iota(jnp.int32, (LANES, LANES), 0)
    to_gain = jnp.where(
        (lane_iota((LANES, LANES)) == VALID) & (source < VALID), 1.0, 0.0
    ).astype(BF)
    for j in range(0, VOC, PER):
        group = range(j, j + PER)
        head = jnp.concatenate([student_head[span_of(v, core, HALF_S), :] for v in group], axis=0)
        term = dot(head, grad, NN)
        part = jnp.concatenate([rows[v, :HALF_S, :] for v in group], axis=0).astype(F32)
        term = term + dot((term * (part * kept)).astype(BF), to_gain, NN)
        term = term.astype(BF)
        for i, v in enumerate(group):
            out[v] = term[i * HALF_S : (i + 1) * HALF_S]


def backward_one(
    stats, tops, exp_in, ratio_in, weight, inverse, student_head, other,
    grad_out, scaled_out, away, pull_out, loss_out,
):
    all_s, total_s, all_t, total_t, sum_d, sum_u, sum_du = combined(stats)
    inside = lane_iota((1, LANES)) < VALID
    mean_d = sum_d / total_s
    mean_u = sum_u / total_s
    covariance = sum_du / total_s - mean_d * mean_u
    divergence = mean_d - jnp.log(total_s) + jnp.log(total_t)
    loss_out[...] = jnp.sum(
        jnp.where(inside, weight[...] * divergence, 0.0), axis=1, keepdims=True
    )
    pull_out[...] = weight[...] * covariance * inverse[...] * inverse[...] / DS
    shift_s = tops[0:1, :] - all_s
    shift_t = tops[2:3, :] - all_t
    factor = weight[...] * jnp.exp(shift_s) / total_s
    offset = shift_s - shift_t - mean_d
    grad = jnp.where(inside, factor * exp_in[...] * (ratio_in[...] + offset), 0.0)
    kept = jnp.where(inside, inverse[...], 0.0)
    scaled_out[...] = (grad * kept).astype(BF)
    grad = grad.astype(BF)
    grad_out[...] = grad
    terms_of(other, student_head, grad, kept, 1 - own_core(), away)


def backward_two(grad, inverse, student_head, mine, stay):
    kept = jnp.where(lane_iota((1, LANES)) < VALID, inverse[...], 0.0)
    terms_of(mine, student_head, grad[...], kept, own_core(), stay)


def head_kernel(mine, other, scaled, out):
    core = own_core()
    first = pl.program_id(0) * PER
    for rows, which in ((mine, core), (other, 1 - core)):
        block = jnp.concatenate([rows[first + i, :HALF_S, :] for i in range(PER)], axis=0)
        result = dot(block, scaled[...], NT).astype(BF)
        for i in range(PER):
            out[span_of(i, which, HALF_S), :] = result[i * HALF_S : (i + 1) * HALF_S]


def pair_kernel(stay, arrived, out):
    for v in range(VOC):
        out[v] = (stay[v].astype(F32) + arrived[v].astype(F32)).astype(BF)


def send_kernel(pieces, student_row, out):
    summed = pieces[0].astype(F32)
    for v in range(1, VOC):
        summed = summed + pieces[v].astype(F32)
    summed = summed.astype(BF)
    slot = lax.broadcasted_iota(jnp.int32, (SEND, LANES), 0)
    extra = (slot == ROWS) & (lane_iota((SEND, LANES)) == VALID)
    for g in range(GROUPS):
        pick = ((slot < ROWS) & (student_row[...] == slot + g * ROWS)) | extra
        out[g] = dot(jnp.where(pick, 1.0, 0.0).astype(BF), summed, NT).astype(BF)


def finish_kernel(pieces, hidden, gain, student_row, inverse, pull, grad_hidden, grad_gain):
    halves = []
    for c in range(2):
        summed = pieces[c].astype(F32)
        for z in range(1, GROUPS // 2):
            summed = summed + pieces[2 * z + c].astype(F32)
        halves.append(summed)
    summed = jnp.concatenate(halves, axis=1)
    grad_gain[...] = summed[ROWS : ROWS + 1] / gain[...]
    first = lax.axis_index("grp") * ROWS
    own = lax.broadcasted_iota(jnp.int32, (ROWS, LANES), 0) + first == student_row[...]
    own_rms = jnp.sum(jnp.where(own, inverse[...], 0.0), axis=1, keepdims=True)
    own_pull = jnp.sum(jnp.where(own, pull[...], 0.0), axis=1, keepdims=True)
    normed_grad = summed[:ROWS]
    result = own_rms * (normed_grad * gain[...]) - hidden[...].astype(F32) * own_pull
    grad_hidden[...] = result.astype(BF)


def shape(dims, dtype):
    return jax.ShapeDtypeStruct(dims, dtype)


def params(mib):
    return pltpu.CompilerParams(vmem_limit_bytes=mib * 1024 * 1024)


def cost(flops):
    return pl.CostEstimate(flops=flops, bytes_accessed=4 * 1024 * 1024, transcendentals=0)


def exchange(x, axis):
    return lax.all_to_all(x, axis, 0, 0, tiled=True)


ANY = pl.BlockSpec(memory_space=pl.ANY)
VMEM = pl.BlockSpec(memory_space=pltpu.VMEM)


def local(
    student_hidden, norm_gain, teacher_hidden, student_head, teacher_head, episode_source, lengths
):
    core = own_core()
    row = shape((1, LANES), F32)
    logits = shape((VOC_DEV, LANES), F32)
    half_rows = shape((VOC, HALF_S, LANES), BF)
    student_row, teacher_row, weight = lane_tables(episode_source, lengths)

    packed = pl.pallas_call(
        pack_kernel,
        out_shape=shape((GROUPS, ROWS, HALF), BF),
        in_specs=[ANY] * 2,
        scratch_shapes=[
            pltpu.VMEM((ROWS, 2 * HALF_S), BF),
            pltpu.VMEM((ROWS, 2 * HALF_T), BF),
            pltpu.SemaphoreType.DMA((2,)),
        ],
        compiler_params=params(4),
    )(student_hidden, teacher_hidden)
    held = exchange(packed, "grp")

    gain_half = lax.dynamic_slice_in_dim(norm_gain, core * HALF_S, HALF_S)
    gain_high = rounded(gain_half)
    gain_mid = rounded(gain_half - gain_high)
    gain_low = gain_half - gain_high - gain_mid
    gain_parts = jnp.concatenate(
        [jnp.stack([gain_high, gain_mid, gain_low]), jnp.zeros((13, HALF_S), F32)], axis=0
    )
    block = pl.pallas_call(
        compact_kernel, out_shape=shape((VOC, HALF, LANES), BF), compiler_params=params(8)
    )(held, student_row, teacher_row, gain_parts)
    mine = exchange(block, "voc")
    other = lax.ppermute(mine, "grp", CORE_SWAP)

    student, teacher, squares = pl.pallas_call(
        forward_one,
        out_shape=(logits, logits, shape((SPARE, LANES), F32)),
        compiler_params=params(12),
        cost_estimate=cost(VOC * HALF * VOC_DEV * LANES * 2),
    )(mine, student_head, teacher_head)
    exp_s, ratio, stats, tops, inverse = pl.pallas_call(
        forward_two,
        out_shape=(
            logits,
            logits,
            shape((VOC, STATS, LANES), F32),
            shape((STATS, LANES), F32),
            row,
        ),
        compiler_params=params(12),
        cost_estimate=cost(VOC * HALF * VOC_DEV * LANES * 2),
    )(other, student_head, teacher_head, student, teacher, squares)

    from_voc = exchange(stats, "voc")
    spread = pl.pallas_call(
        combine_kernel, out_shape=shape((GROUPS, STATS, LANES), F32), compiler_params=params(4)
    )(from_voc)
    from_grp = exchange(spread, "grp")

    grad, scaled, away, pull, loss = pl.pallas_call(
        backward_one,
        out_shape=(
            shape((VOC_DEV, LANES), BF),
            shape((VOC_DEV, LANES), BF),
            half_rows,
            row,
            shape((1, 1), F32),
        ),
        compiler_params=params(8),
        cost_estimate=cost(DS * VOC_DEV * LANES),
    )(from_grp, tops, exp_s, ratio, weight, inverse, student_head, other)
    arrived = lax.ppermute(away, "grp", CORE_SWAP)
    stay = pl.pallas_call(
        backward_two,
        out_shape=half_rows,
        compiler_params=params(8),
        cost_estimate=cost(DS * VOC_DEV * LANES),
    )(grad, inverse, student_head, mine)
    pair = pl.pallas_call(pair_kernel, out_shape=half_rows, compiler_params=params(8))(
        stay, arrived
    )
    pieces = exchange(pair, "voc")
    grad_head = pl.pallas_call(
        head_kernel,
        out_shape=shape((DS, VOC_DEV), BF),
        grid=(VOC // PER,),
        in_specs=[VMEM] * 3,
        out_specs=pl.BlockSpec((DS * PER // VOC, VOC_DEV), lambda i: (i, 0)),
        compiler_params=params(12),
        cost_estimate=cost(DS * VOC_DEV * LANES * 2),
    )(mine, other, scaled)
    outgoing = pl.pallas_call(
        send_kernel, out_shape=shape((GROUPS, SEND, HALF_S), BF), compiler_params=params(8)
    )(pieces, student_row)
    pieces = exchange(outgoing, "grp")
    grad_hidden, grad_gain = pl.pallas_call(
        finish_kernel, out_shape=(shape((ROWS, 2 * HALF_S), BF), row), compiler_params=params(4)
    )(pieces, student_hidden, norm_gain[None], student_row, inverse, pull)
    return (loss.reshape(()), grad_hidden, grad_gain.reshape(-1), grad_head)


def solution(mesh):
    placed = (
        P("grp", "voc"),
        P("voc"),
        P("grp", "voc"),
        P(None, ("grp", "voc")),
        P(None, ("grp", "voc")),
        P(),
        P(),
    )
    return jax.shard_map(
        local,
        mesh=mesh,
        in_specs=placed,
        out_specs=(P(), P("grp", "voc"), P("voc"), P(None, ("grp", "voc"))),
        check_vma=False,
    )
```

```python
import jax
import jax.numpy as jnp
from jax import lax
from jax.experimental import pallas as pl
from jax.experimental.pallas import tpu as pltpu
from jax.sharding import PartitionSpec as P

DS = 4096
SEQ = 2
VALID = 240
LANES = 256
EPSILON = 1e-06
GROUPS = 16
VOC = 16
ROWS = 24
HALF_S = 128
HALF_T = 160
HALF = HALF_S + HALF_T
VOC_DEV = 384
STATS = 8
SEND = 32
PACK = 56
TAIL = 32
PER = 4
SPARE = 16
SIDE = 4
BF = jnp.bfloat16
F32 = jnp.float32
CORE_SWAP = [(i, i ^ 1) for i in range(GROUPS)]
BOTH = ("grp", "voc")


def ring(phase, step):
    pairs = []
    for g in range(GROUPS):
        for v in range(VOC):
            y, x = divmod(v, SIDE)
            if (g % 2 == 0) == (phase == 1):
                x = (x + step) % SIDE
            else:
                y = (y + step) % SIDE
            pairs.append((g * VOC + v, g * VOC + y * SIDE + x))
    return pairs


TN = (((0,), (0,)), ((), ()))
NT = (((1,), (1,)), ((), ()))
NN = (((1,), (0,)), ((), ()))


def rounded(x):
    return lax.reduce_precision(x, 8, 7)


def dot(a, b, dims):
    return lax.dot_general(a, b, dims, preferred_element_type=F32)


def lane_tables(episode_source, lengths):
    episodes = lengths.shape[0]
    two = (lengths == 2).astype(jnp.int32)
    before = jnp.arange(episodes)[None, :] < jnp.arange(episodes)[:, None]
    rank = jnp.sum(jnp.where(before, two[None, :], 0), axis=1)
    lane = jnp.arange(LANES, dtype=jnp.int32)
    number = jnp.arange(episodes, dtype=jnp.int32)
    first = lane[None, :] == number[:, None]
    second = (two[:, None] == 1) & (lane[None, :] == episodes + rank[:, None])
    pick = first | second
    position = (lane >= episodes).astype(jnp.int32)
    inside = lane < VALID
    episode = jnp.sum(jnp.where(pick, number[:, None], 0), axis=0)
    source = jnp.sum(jnp.where(pick, episode_source[:, None], 0), axis=0)
    length = jnp.sum(jnp.where(pick, lengths[:, None], 0), axis=0)
    student_row = jnp.where(inside, episode * SEQ + position, -1)
    teacher_row = jnp.where(inside, source * SEQ + position, -1)
    weight = jnp.where(inside, 1.0 / jnp.maximum(length, 1).astype(F32), 0.0)
    return student_row[None], teacher_row[None], weight[None]


def own_core():
    return lax.rem(lax.axis_index("grp"), 2)


def lane_iota(shape):
    return lax.broadcasted_iota(jnp.int32, shape, len(shape) - 1)


def pack_kernel(student_in, teacher_in, out, student, teacher, in_sems):
    copies = [
        pltpu.make_async_copy(student_in, student, in_sems.at[0]),
        pltpu.make_async_copy(teacher_in, teacher, in_sems.at[1]),
    ]
    for copy in copies:
        copy.start()
    for copy in copies:
        copy.wait()
    for c in range(2):
        rows = teacher[:, c * HALF_T : (c + 1) * HALF_T].astype(F32)
        tail = rows[:, HALF_S:]
        tail = jnp.concatenate(
            [tail[:8], tail[8:16], tail[16:24], jnp.zeros((8, TAIL), F32)], axis=1
        )
        whole = jnp.concatenate(
            [student[:, c * HALF_S : (c + 1) * HALF_S].astype(F32), rows[:, :HALF_S], tail], axis=0
        )
        whole = whole.astype(BF)
        for z in range(GROUPS // 2):
            out[2 * z + c] = whole


def spare_lanes():
    source = lax.broadcasted_iota(jnp.int32, (LANES, LANES), 0)
    lane = lane_iota((LANES, LANES))
    return jnp.where(lane == VALID + lax.rem(source, SPARE), 1.0, 0.0).astype(BF)


def spare_rows():
    row = lax.broadcasted_iota(jnp.int32, (SPARE, LANES), 0)
    return lax.div(lane_iota((SPARE, LANES)), SPARE) == row


def split(x, parts):
    out = []
    for _ in range(parts):
        out.append(x.astype(BF))
        x = x - out[-1].astype(F32)
    return out


def compact_kernel(held, student_row, teacher_row, weight, gain, out, row_out, weight_out):
    row_out[...] = student_row[...]
    weight_out[...] = weight[...]
    blocks = [held[g].astype(F32) for g in range(GROUPS)]
    rows_s = jnp.concatenate([block[:ROWS] for block in blocks], axis=0).astype(BF)
    rows_t = jnp.concatenate([block[ROWS : 2 * ROWS] for block in blocks], axis=0).astype(BF)
    tails = jnp.concatenate([block[2 * ROWS :] for block in blocks], axis=0).astype(BF)
    ids = lax.broadcasted_iota(jnp.int32, (GROUPS * ROWS, LANES), 0)
    pick_s = jnp.where(ids == student_row[...], 1.0, 0.0).astype(BF)
    pick_t = jnp.where(ids == teacher_row[...], 1.0, 0.0).astype(BF)
    block_s = dot(rows_s, pick_s, TN)
    block_t = dot(rows_t, pick_t, TN).astype(BF)
    short = lax.broadcasted_iota(jnp.int32, (GROUPS * 8, LANES), 0)
    short = lax.div(short, 8) * ROWS + lax.rem(short, 8)
    tail = jnp.zeros((TAIL, LANES), F32)
    for k in range(3):
        pick = jnp.where(short + 8 * k == teacher_row[...], 1.0, 0.0).astype(BF)
        tail = tail + dot(tails, pick, TN)[k * TAIL : (k + 1) * TAIL]
    spread_gain = dot(gain[...].astype(BF), jnp.ones((16, LANES), BF), TN)
    squares = jnp.sum(block_s * block_s, axis=0, keepdims=True)
    parts = split(jnp.where(spare_rows(), squares, 0.0), 2)
    lanes = spare_lanes()
    spare = jnp.concatenate([dot(part, lanes, NN) for part in parts], axis=0)
    block_s = block_s * spread_gain
    block_s = jnp.concatenate([block_s[: 2 * SPARE] + spare, block_s[2 * SPARE :]], axis=0)
    out[:HALF_S, :] = block_s.astype(BF)
    out[HALF_S : 2 * HALF_S, :] = block_t
    out[2 * HALF_S :, :] = tail.astype(BF)


def stack_rows(values):
    row = lax.broadcasted_iota(jnp.int32, (STATS, LANES), 0)
    out = jnp.zeros((STATS, LANES), F32)
    for k, value in enumerate(values):
        out = jnp.where(row == k, value, out)
    return out


def total(x):
    return jnp.sum(x, axis=0, keepdims=True)


def combined(stats):
    top_s, sum_s, top_t, sum_t, mean_d, mean_u, mean_du = [stats[:, k, :] for k in range(7)]
    all_s = jnp.max(top_s, axis=0, keepdims=True)
    all_t = jnp.max(top_t, axis=0, keepdims=True)
    shift_s = top_s - all_s
    shift_t = top_t - all_t
    scale_s = jnp.exp(shift_s)
    scale_t = jnp.exp(shift_t)
    shift_d = shift_s - shift_t
    return (
        all_s,
        total(scale_s * sum_s),
        all_t,
        total(scale_t * sum_t),
        total(scale_s * (mean_d + shift_d * sum_s)),
        total(scale_s * (mean_u + shift_s * sum_s)),
        total(
            scale_s
            * (mean_du + shift_s * mean_d + shift_d * mean_u + shift_s * shift_d * sum_s)
        ),
    )


def span_of(v, core, half):
    return pl.ds(pl.multiple_of(v * 2 * half + core * half, 32), half)


def places(core):
    index = lax.axis_index("voc")
    x, y = lax.rem(index, SIDE), lax.div(index, SIDE)
    a = lax.select(core == 0, x, y)
    b = lax.select(core == 0, y, x)

    def place(j, k):
        u = lax.rem(a + SIDE - j, SIDE)
        w = lax.rem(b + SIDE - k, SIDE)
        return lax.select(core == 0, SIDE * w + u, SIDE * u + w)

    return place


def batches(refs, core):
    place = places(core)
    return [
        [(ref, j, place(j, k)) for j in range(SIDE)] for ref, k in zip(refs, (0, 1, 3, 2))
    ]


def logits_of(groups, student_head, teacher_head, core):
    student = jnp.zeros((VOC_DEV, LANES), F32)
    teacher = jnp.zeros((VOC_DEV, LANES), F32)
    squares = jnp.zeros((SPARE, LANES), F32)
    for group in groups:
        head_s = jnp.concatenate(
            [student_head[span_of(v, core, HALF_S), :] for _, _, v in group], axis=0
        )
        head_t = jnp.concatenate(
            [teacher_head[span_of(v, core, HALF_T), :] for _, _, v in group], axis=0
        )
        rows_s = jnp.concatenate([ref[j, :HALF_S, :] for ref, j, _ in group], axis=0)
        rows_t = jnp.concatenate([ref[j, HALF_S:, :] for ref, j, _ in group], axis=0)
        student = student + dot(head_s, rows_s, TN)
        teacher = teacher + dot(head_t, rows_t, TN)
        for ref, j, _ in group:
            squares = squares + ref[j, :SPARE, :].astype(F32)
            squares = squares + ref[j, SPARE : 2 * SPARE, :].astype(F32)
    return student, teacher, squares


def forward_near(
    a, u, d, student_head, teacher_head, student_out, teacher_out, squares_out, zero_out
):
    core = own_core()
    groups = batches((a, u, d), core)
    student, teacher, squares = logits_of(groups, student_head, teacher_head, core)
    student_out[...] = student
    teacher_out[...] = teacher
    squares_out[...] = squares
    zero_out[...] = jnp.zeros((1, LANES), F32)


def forward_mid(
    far, other_a, other_u, other_d, student_head, teacher_head,
    student_in, teacher_in, squares_in, student_out, teacher_out, squares_out,
):
    core = own_core()
    one = logits_of(batches((None, None, None, far), core)[3:], student_head, teacher_head, core)
    groups = batches((other_a, other_u, other_d), 1 - core)
    two = logits_of(groups, student_head, teacher_head, 1 - core)
    student_out[...] = one[0] + two[0] + student_in[...]
    teacher_out[...] = one[1] + two[1] + teacher_in[...]
    squares_out[...] = one[2] + two[2] + squares_in[...]


def forward_last(
    other_far, student_head, teacher_head, student_in, teacher_in, squares_in,
    exp_out, ratio_out, stats_out, tops_out, inverse_out,
):
    core = 1 - own_core()
    student, teacher, squares = logits_of(
        batches((None, None, None, other_far), core)[3:], student_head, teacher_head, core
    )
    squares = squares + squares_in[...]
    squares = jnp.where(lane_iota((SPARE, LANES)) >= VALID, squares, 0.0)
    lanes = spare_lanes()
    by_row = sum(dot(part, lanes, NT) for part in split(squares, 3))
    squares = total(jnp.where(spare_rows(), by_row, 0.0))
    inverse = lax.rsqrt(squares / DS + EPSILON)
    inverse_out[...] = inverse
    student = (student + student_in[...]) * inverse
    teacher = teacher + teacher_in[...]

    top_s = jnp.max(student, axis=0, keepdims=True)
    top_t = jnp.max(teacher, axis=0, keepdims=True)
    below = student - top_s
    exp_s = jnp.exp(below)
    below_t = teacher - top_t
    ratio = below - below_t
    exp_out[...] = exp_s
    ratio_out[...] = ratio
    weighted = exp_s * ratio
    stats = stack_rows(
        [
            top_s,
            total(exp_s),
            top_t,
            total(jnp.exp(below_t)),
            total(weighted),
            total(exp_s * below),
            total(weighted * below),
        ]
    )
    tops_out[...] = stats
    for v in range(VOC):
        stats_out[v] = stats


def combine_kernel(stats, out):
    tile = stack_rows(combined(stats))
    for g in range(GROUPS):
        out[g] = tile


def terms_of(groups, student_head, grad, core, out):
    for group in groups:
        head = jnp.concatenate(
            [student_head[span_of(v, core, HALF_S), :] for _, _, v in group], axis=0
        )
        term = dot(head, grad, NN).astype(BF)
        for i, (_, _, v) in enumerate(group):
            out[v] = term[i * HALF_S : (i + 1) * HALF_S]


def backward_one(
    stats, tops, exp_in, ratio_in, weight, inverse, student_head,
    grad_out, scaled_out, away, pull_out, loss_out,
):
    core = 1 - own_core()
    all_s, total_s, all_t, total_t, sum_d, sum_u, sum_du = combined(stats)
    inside = lane_iota((1, LANES)) < VALID
    mean_d = sum_d / total_s
    mean_u = sum_u / total_s
    covariance = sum_du / total_s - mean_d * mean_u
    divergence = mean_d - jnp.log(total_s) + jnp.log(total_t)
    loss_out[...] = jnp.sum(
        jnp.where(inside, weight[...] * divergence, 0.0), axis=1, keepdims=True
    )
    pull_out[...] = weight[...] * covariance * inverse[...] * inverse[...] / DS
    shift_s = tops[0:1, :] - all_s
    shift_t = tops[2:3, :] - all_t
    factor = weight[...] * jnp.exp(shift_s) / total_s
    offset = shift_s - shift_t - mean_d
    grad = jnp.where(inside, factor * exp_in[...] * (ratio_in[...] + offset), 0.0)
    kept = jnp.where(inside, inverse[...], 0.0)
    scaled_out[...] = (grad * kept).astype(BF)
    grad = grad.astype(BF)
    grad_out[...] = grad
    terms_of(batches((None,) * 4, core), student_head, grad, core, away)


def backward_two(*refs):
    mine, other = refs[:4], refs[4:8]
    grad, student_head, hidden, gain, student_row, inverse, pull = refs[8:15]
    stay, base_out, rows_out, sems = refs[15:]
    core = own_core()
    groups = batches(mine, core)
    copies = []
    for k, part in enumerate((groups, batches(other, 1 - core))):
        for group in part:
            for ref, j, v in group:
                n = len(copies)
                copies.append(
                    pltpu.make_async_copy(
                        ref.at[j, pl.ds(0, HALF_S)], rows_out.at[k, v], sems.at[n]
                    )
                )
                copies[n].start()
    first = lax.axis_index("grp") * ROWS
    own = lax.broadcasted_iota(jnp.int32, (ROWS, LANES), 0) + first == student_row[...]
    own_rms = jnp.sum(jnp.where(own, inverse[...], 0.0), axis=1, keepdims=True)
    own_pull = jnp.sum(jnp.where(own, pull[...], 0.0), axis=1, keepdims=True)
    base_out[:ROWS] = own_rms * gain[...]
    base_out[ROWS : 2 * ROWS] = hidden[...].astype(F32) * own_pull
    base_out[2 * ROWS :] = jnp.broadcast_to(1.0 / gain[...], (8, LANES))
    terms_of(groups, student_head, grad[...], core, stay)
    for copy in copies:
        copy.wait()


def head_kernel(source, scaled_in, out, rows, scaled, blocks, in_sems, scaled_sem, sems):
    waiting = []
    for k in range(2):
        for j in range(VOC // PER):
            waiting.append(
                pltpu.make_async_copy(
                    source.at[k, pl.ds(j * PER, PER)], rows.at[k, pl.ds(j * PER, PER)], in_sems.at[k, j]
                )
            )
    first = pltpu.make_async_copy(scaled_in, scaled, scaled_sem)
    first.start()
    for copy in waiting:
        copy.start()
    first.wait()
    copies = []
    for k, core in enumerate((own_core(), 1 - own_core())):
        for j in range(VOC // PER):
            waiting[k * (VOC // PER) + j].wait()
            block = rows[k, pl.ds(j * PER, PER)].reshape(PER * HALF_S, LANES)
            result = dot(block, scaled[...], NT).astype(BF)
            for i in range(PER):
                n = len(copies)
                blocks[n] = result[i * HALF_S : (i + 1) * HALF_S]
                copies.append(
                    pltpu.make_async_copy(
                        blocks.at[n], out.at[span_of(j * PER + i, core, HALF_S)], sems.at[n]
                    )
                )
                copies[n].start()
    for copy in copies:
        copy.wait()


def pair_kernel(stay, arrived, out):
    for v in range(VOC):
        out[v] = (stay[v].astype(F32) + arrived[v].astype(F32)).astype(BF)


def send_kernel(pieces, student_row, block, inverse, out):
    summed = pieces[0].astype(F32)
    for v in range(1, VOC):
        summed = summed + pieces[v].astype(F32)
    lane = lane_iota((HALF_S, LANES))
    inside = lane < VALID
    scaled = jnp.where(inside, block[:HALF_S, :].astype(F32) * inverse[...], 0.0)
    gain = jnp.sum(summed * scaled, axis=1, keepdims=True)
    summed = jnp.where(lane == VALID, gain, summed).astype(BF)
    slot = lax.broadcasted_iota(jnp.int32, (SEND, LANES), 0)
    extra = (slot == ROWS) & (lane_iota((SEND, LANES)) == VALID)
    picks = []
    for g in range(GROUPS):
        pick = ((slot < ROWS) & (student_row[...] == slot + g * ROWS)) | extra
        picks.append(jnp.where(pick, 1.0, 0.0).astype(BF))
    result = dot(jnp.concatenate(picks, axis=0), summed, NT).astype(BF)
    for g in range(GROUPS):
        out[g] = result[g * SEND : (g + 1) * SEND]


def finish_kernel(pieces_in, base_in, grad_hidden, grad_gain, pieces, base, sems):
    copies = [
        pltpu.make_async_copy(pieces_in, pieces, sems.at[0]),
        pltpu.make_async_copy(base_in, base, sems.at[1]),
    ]
    for copy in copies:
        copy.start()
    for copy in copies:
        copy.wait()
    halves = []
    for c in range(2):
        summed = pieces[c].astype(F32)
        for z in range(1, GROUPS // 2):
            summed = summed + pieces[2 * z + c].astype(F32)
        halves.append(summed)
    summed = jnp.concatenate(halves, axis=1)
    grad_gain[...] = summed[ROWS : ROWS + 1] * base[2 * ROWS : 2 * ROWS + 1]
    grad_hidden[...] = (summed[:ROWS] * base[:ROWS] - base[ROWS : 2 * ROWS]).astype(BF)


def shape(dims, dtype):
    return jax.ShapeDtypeStruct(dims, dtype)


def params(mib):
    return pltpu.CompilerParams(vmem_limit_bytes=mib * 1024 * 1024)


def in_hbm(x):
    return pltpu.with_memory_space_constraint(x, pltpu.HBM)


def cost(flops):
    return pl.CostEstimate(flops=flops, bytes_accessed=4 * 1024 * 1024, transcendentals=0)


def exchange(x, axis):
    return lax.all_to_all(x, axis, 0, 0, tiled=True)


HBM = pl.BlockSpec(memory_space=pltpu.HBM)
ANY = pl.BlockSpec(memory_space=pl.ANY)
VMEM = pl.BlockSpec(memory_space=pltpu.VMEM)


def local(
    student_hidden, norm_gain, teacher_hidden, student_head, teacher_head, episode_source, lengths
):
    core = own_core()
    row = shape((1, LANES), F32)
    logits = shape((VOC_DEV, LANES), F32)
    half_rows = shape((VOC, HALF_S, LANES), BF)
    student_row, teacher_row, weight = lane_tables(episode_source, lengths)

    packed = pl.pallas_call(
        pack_kernel,
        out_shape=pltpu.HBM((GROUPS, PACK, HALF_S), BF),
        in_specs=[HBM] * 2,
        out_specs=VMEM,
        scratch_shapes=[
            pltpu.VMEM((ROWS, 2 * HALF_S), BF),
            pltpu.VMEM((ROWS, 2 * HALF_T), BF),
            pltpu.SemaphoreType.DMA((2,)),
        ],
        compiler_params=params(4),
    )(in_hbm(student_hidden), in_hbm(teacher_hidden))
    held = exchange(packed, "grp")

    gain_half = lax.dynamic_slice_in_dim(norm_gain, core * HALF_S, HALF_S)
    gain_high = rounded(gain_half)
    gain_mid = rounded(gain_half - gain_high)
    gain_low = gain_half - gain_high - gain_mid
    gain_parts = jnp.concatenate(
        [jnp.stack([gain_high, gain_mid, gain_low]), jnp.zeros((13, HALF_S), F32)], axis=0
    )
    block, student_row, weight = pl.pallas_call(
        compact_kernel,
        out_shape=(shape((HALF, LANES), BF), shape((1, LANES), jnp.int32), row),
        compiler_params=params(8),
    )(held, student_row, teacher_row, weight, gain_parts)

    one = lax.ppermute(block, BOTH, ring(1, 1))
    three = lax.ppermute(block, BOTH, ring(1, 3))
    two = lax.ppermute(block, BOTH, ring(1, 2))
    a = jnp.stack([block, one, two, three])
    u = lax.ppermute(a, BOTH, ring(2, 1))
    d = lax.ppermute(a, BOTH, ring(2, 3))
    v = lax.ppermute(u[:2], BOTH, ring(2, 1))
    w = lax.ppermute(d[2:], BOTH, ring(2, 3))
    other = tuple(lax.ppermute(part, "grp", CORE_SWAP) for part in (a, u, d))

    partial = (logits, logits, shape((SPARE, LANES), F32))
    *sums, zero = pl.pallas_call(
        forward_near,
        out_shape=partial + (row,),
        compiler_params=params(12),
        cost_estimate=cost(12 * HALF * VOC_DEV * LANES * 2),
    )(a, u, d, student_head, teacher_head)
    far = jnp.concatenate([v, w], axis=0) + zero.astype(BF)
    mine = (a, u, d, far)
    other = other + (lax.ppermute(far, "grp", CORE_SWAP),)
    sums = pl.pallas_call(
        forward_mid,
        out_shape=partial,
        compiler_params=params(12),
        cost_estimate=cost(VOC * HALF * VOC_DEV * LANES * 2),
    )(far, *other[:3], student_head, teacher_head, *sums)
    exp_s, ratio, stats, tops, inverse = pl.pallas_call(
        forward_last,
        out_shape=(
            logits,
            logits,
            shape((VOC, STATS, LANES), F32),
            shape((STATS, LANES), F32),
            row,
        ),
        compiler_params=params(12),
        cost_estimate=cost(4 * HALF * VOC_DEV * LANES * 2),
    )(other[3], student_head, teacher_head, *sums)

    from_voc = exchange(stats, "voc")
    spread = pl.pallas_call(
        combine_kernel, out_shape=shape((GROUPS, STATS, LANES), F32), compiler_params=params(4)
    )(from_voc)
    from_grp = exchange(spread, "grp")

    grad, scaled, away, pull, loss = pl.pallas_call(
        backward_one,
        out_shape=(
            shape((VOC_DEV, LANES), BF),
            pltpu.HBM((VOC_DEV, LANES), BF),
            half_rows,
            row,
            shape((1, 1), F32),
        ),
        out_specs=(VMEM,) * 5,
        compiler_params=params(8),
        cost_estimate=cost(DS * VOC_DEV * LANES),
    )(from_grp, tops, exp_s, ratio, weight, inverse, student_head)
    arrived = lax.ppermute(away, "grp", CORE_SWAP)
    stay, base, rows = pl.pallas_call(
        backward_two,
        out_shape=(
            half_rows,
            pltpu.HBM((2 * ROWS + 8, LANES), F32),
            pltpu.HBM((2, VOC, HALF_S, LANES), BF),
        ),
        out_specs=(VMEM, VMEM, HBM),
        scratch_shapes=[pltpu.SemaphoreType.DMA((2 * VOC,))],
        compiler_params=params(8),
        cost_estimate=cost(DS * VOC_DEV * LANES),
    )(
        *mine, *other, grad, student_head,
        student_hidden, norm_gain[None], student_row, inverse, pull,
    )
    pair = pl.pallas_call(pair_kernel, out_shape=half_rows, compiler_params=params(8))(
        stay, arrived
    )
    pieces = exchange(pair, "voc")
    grad_head = pl.pallas_call(
        head_kernel,
        out_shape=shape((DS, VOC_DEV), BF),
        in_specs=[HBM] * 2,
        out_specs=HBM,
        scratch_shapes=[
            pltpu.VMEM((2, VOC, HALF_S, LANES), BF),
            pltpu.VMEM((VOC_DEV, LANES), BF),
            pltpu.VMEM((2 * VOC, HALF_S, VOC_DEV), BF),
            pltpu.SemaphoreType.DMA((2, VOC // PER)),
            pltpu.SemaphoreType.DMA,
            pltpu.SemaphoreType.DMA((2 * VOC,)),
        ],
        compiler_params=params(12),
        cost_estimate=cost(DS * VOC_DEV * LANES * 2),
    )(in_hbm(rows), in_hbm(scaled))
    outgoing = pl.pallas_call(
        send_kernel,
        out_shape=pltpu.HBM((GROUPS, SEND, HALF_S), BF),
        out_specs=VMEM,
        compiler_params=params(8),
    )(pieces, student_row, block, inverse)
    pieces = exchange(outgoing, "grp")
    grad_hidden, grad_gain = pl.pallas_call(
        finish_kernel,
        out_shape=(shape((ROWS, 2 * HALF_S), BF), row),
        in_specs=[ANY, HBM],
        scratch_shapes=[
            pltpu.VMEM((GROUPS, SEND, HALF_S), BF),
            pltpu.VMEM((2 * ROWS + 8, LANES), F32),
            pltpu.SemaphoreType.DMA((2,)),
        ],
        compiler_params=params(4),
    )(pieces, in_hbm(base))
    return (loss.reshape(()), grad_hidden, grad_gain.reshape(-1), grad_head)


def solution(mesh):
    placed = (
        P("grp", "voc"),
        P("voc"),
        P("grp", "voc"),
        P(None, ("grp", "voc")),
        P(None, ("grp", "voc")),
        P(),
        P(),
    )
    return jax.shard_map(
        local,
        mesh=mesh,
        in_specs=placed,
        out_specs=(P(), P("grp", "voc"), P("voc"), P(None, ("grp", "voc"))),
        check_vma=False,
    )
```

```python
import jax
import jax.numpy as jnp
from jax import lax
from jax.experimental import pallas as pl
from jax.experimental.pallas import tpu as pltpu
from jax.sharding import PartitionSpec as P

DS = 4096
SEQ = 2
VALID = 240
LANES = 256
EPSILON = 1e-06
GROUPS = 16
VOC = 16
ROWS = 24
HALF_S = 128
HALF_T = 160
HALF = HALF_S + HALF_T
VOC_DEV = 384
STATS = 8
SEND = 32
PACK = 56
TAIL = 32
PER = 4
SPARE = 16
SIDE = 4
BF = jnp.bfloat16
F32 = jnp.float32
CORE_SWAP = [(i, i ^ 1) for i in range(GROUPS)]
BOTH = ("grp", "voc")


def ring(phase, step):
    pairs = []
    for g in range(GROUPS):
        for v in range(VOC):
            y, x = divmod(v, SIDE)
            if (g % 2 == 0) == (phase == 1):
                x = (x + step) % SIDE
            else:
                y = (y + step) % SIDE
            pairs.append((g * VOC + v, g * VOC + y * SIDE + x))
    return pairs


TN = (((0,), (0,)), ((), ()))
NT = (((1,), (1,)), ((), ()))
NN = (((1,), (0,)), ((), ()))


def rounded(x):
    return lax.reduce_precision(x, 8, 7)


def dot(a, b, dims):
    return lax.dot_general(a, b, dims, preferred_element_type=F32)


def lane_tables(episode_source, lengths):
    episodes = lengths.shape[0]
    two = (lengths == 2).astype(jnp.int32)
    before = jnp.arange(episodes)[None, :] < jnp.arange(episodes)[:, None]
    rank = jnp.sum(jnp.where(before, two[None, :], 0), axis=1)
    lane = jnp.arange(LANES, dtype=jnp.int32)
    number = jnp.arange(episodes, dtype=jnp.int32)
    first = lane[None, :] == number[:, None]
    second = (two[:, None] == 1) & (lane[None, :] == episodes + rank[:, None])
    pick = first | second
    position = (lane >= episodes).astype(jnp.int32)
    inside = lane < VALID
    episode = jnp.sum(jnp.where(pick, number[:, None], 0), axis=0)
    source = jnp.sum(jnp.where(pick, episode_source[:, None], 0), axis=0)
    length = jnp.sum(jnp.where(pick, lengths[:, None], 0), axis=0)
    student_row = jnp.where(inside, episode * SEQ + position, -1)
    teacher_row = jnp.where(inside, source * SEQ + position, -1)
    weight = jnp.where(inside, 1.0 / jnp.maximum(length, 1).astype(F32), 0.0)
    return student_row[None], teacher_row[None], weight[None]


def own_core():
    return lax.rem(lax.axis_index("grp"), 2)


def lane_iota(shape):
    return lax.broadcasted_iota(jnp.int32, shape, len(shape) - 1)


def pack_kernel(student_in, teacher_in, out, student, teacher, in_sems):
    copies = [
        pltpu.make_async_copy(student_in, student, in_sems.at[0]),
        pltpu.make_async_copy(teacher_in, teacher, in_sems.at[1]),
    ]
    for copy in copies:
        copy.start()
    for copy in copies:
        copy.wait()
    for c in range(2):
        rows = teacher[:, c * HALF_T : (c + 1) * HALF_T].astype(F32)
        tail = rows[:, HALF_S:]
        tail = jnp.concatenate(
            [tail[:8], tail[8:16], tail[16:24], jnp.zeros((8, TAIL), F32)], axis=1
        )
        whole = jnp.concatenate(
            [student[:, c * HALF_S : (c + 1) * HALF_S].astype(F32), rows[:, :HALF_S], tail], axis=0
        )
        whole = whole.astype(BF)
        for z in range(GROUPS // 2):
            out[2 * z + c] = whole


def spare_lanes():
    source = lax.broadcasted_iota(jnp.int32, (LANES, LANES), 0)
    lane = lane_iota((LANES, LANES))
    return jnp.where(lane == VALID + lax.rem(source, SPARE), 1.0, 0.0).astype(BF)


def spare_rows():
    row = lax.broadcasted_iota(jnp.int32, (SPARE, LANES), 0)
    return lax.div(lane_iota((SPARE, LANES)), SPARE) == row


def split(x, parts):
    out = []
    for _ in range(parts):
        out.append(x.astype(BF))
        x = x - out[-1].astype(F32)
    return out


def compact_kernel(held, student_row, teacher_row, weight, gain, out, row_out, weight_out):
    row_out[...] = student_row[...]
    weight_out[...] = weight[...]
    blocks = [held[g].astype(F32) for g in range(GROUPS)]
    rows_s = jnp.concatenate([block[:ROWS] for block in blocks], axis=0).astype(BF)
    rows_t = jnp.concatenate([block[ROWS : 2 * ROWS] for block in blocks], axis=0).astype(BF)
    tails = jnp.concatenate([block[2 * ROWS :] for block in blocks], axis=0).astype(BF)
    ids = lax.broadcasted_iota(jnp.int32, (GROUPS * ROWS, LANES), 0)
    pick_s = jnp.where(ids == student_row[...], 1.0, 0.0).astype(BF)
    pick_t = jnp.where(ids == teacher_row[...], 1.0, 0.0).astype(BF)
    block_s = dot(rows_s, pick_s, TN)
    block_t = dot(rows_t, pick_t, TN).astype(BF)
    short = lax.broadcasted_iota(jnp.int32, (GROUPS * 8, LANES), 0)
    short = lax.div(short, 8) * ROWS + lax.rem(short, 8)
    tail = jnp.zeros((TAIL, LANES), F32)
    for k in range(3):
        pick = jnp.where(short + 8 * k == teacher_row[...], 1.0, 0.0).astype(BF)
        tail = tail + dot(tails, pick, TN)[k * TAIL : (k + 1) * TAIL]
    spread_gain = dot(gain[...].astype(BF), jnp.ones((16, LANES), BF), TN)
    squares = jnp.sum(block_s * block_s, axis=0, keepdims=True)
    parts = split(jnp.where(spare_rows(), squares, 0.0), 2)
    lanes = spare_lanes()
    spare = jnp.concatenate([dot(part, lanes, NN) for part in parts], axis=0)
    block_s = block_s * spread_gain
    block_s = jnp.concatenate([block_s[: 2 * SPARE] + spare, block_s[2 * SPARE :]], axis=0)
    out[:HALF_S, :] = block_s.astype(BF)
    out[HALF_S : 2 * HALF_S, :] = block_t
    out[2 * HALF_S :, :] = tail.astype(BF)


def stack_rows(values):
    row = lax.broadcasted_iota(jnp.int32, (STATS, LANES), 0)
    out = jnp.zeros((STATS, LANES), F32)
    for k, value in enumerate(values):
        out = jnp.where(row == k, value, out)
    return out


def total(x):
    return jnp.sum(x, axis=0, keepdims=True)


def combined(stats):
    top_s, sum_s, top_t, sum_t, mean_d, mean_u, mean_du = [stats[:, k, :] for k in range(7)]
    all_s = jnp.max(top_s, axis=0, keepdims=True)
    all_t = jnp.max(top_t, axis=0, keepdims=True)
    shift_s = top_s - all_s
    shift_t = top_t - all_t
    scale_s = jnp.exp(shift_s)
    scale_t = jnp.exp(shift_t)
    shift_d = shift_s - shift_t
    return (
        all_s,
        total(scale_s * sum_s),
        all_t,
        total(scale_t * sum_t),
        total(scale_s * (mean_d + shift_d * sum_s)),
        total(scale_s * (mean_u + shift_s * sum_s)),
        total(
            scale_s
            * (mean_du + shift_s * mean_d + shift_d * mean_u + shift_s * shift_d * sum_s)
        ),
    )


def span_of(v, core, half):
    return pl.ds(pl.multiple_of(v * 2 * half + core * half, 32), half)


def places(core):
    index = lax.axis_index("voc")
    x, y = lax.rem(index, SIDE), lax.div(index, SIDE)
    a = lax.select(core == 0, x, y)
    b = lax.select(core == 0, y, x)

    def place(j, k):
        u = lax.rem(a + SIDE - j, SIDE)
        w = lax.rem(b + SIDE - k, SIDE)
        return lax.select(core == 0, SIDE * w + u, SIDE * u + w)

    return place


def batches(refs, core):
    place = places(core)
    return [
        [(ref, j, place(j, k)) for j in range(SIDE)] for ref, k in zip(refs, (0, 1, 3, 2))
    ]


def logits_of(groups, student_head, teacher_head, core):
    student = jnp.zeros((VOC_DEV, LANES), F32)
    teacher = jnp.zeros((VOC_DEV, LANES), F32)
    squares = jnp.zeros((SPARE, LANES), F32)
    for group in groups:
        head_s = jnp.concatenate(
            [student_head[span_of(v, core, HALF_S), :] for _, _, v in group], axis=0
        )
        head_t = jnp.concatenate(
            [teacher_head[span_of(v, core, HALF_T), :] for _, _, v in group], axis=0
        )
        rows_s = jnp.concatenate([ref[j, :HALF_S, :] for ref, j, _ in group], axis=0)
        rows_t = jnp.concatenate([ref[j, HALF_S:, :] for ref, j, _ in group], axis=0)
        student = student + dot(head_s, rows_s, TN)
        teacher = teacher + dot(head_t, rows_t, TN)
        for ref, j, _ in group:
            squares = squares + ref[j, :SPARE, :].astype(F32)
            squares = squares + ref[j, SPARE : 2 * SPARE, :].astype(F32)
    return student, teacher, squares


def forward_near(
    a, u, d, student_head, teacher_head, student_out, teacher_out, squares_out, zero_out
):
    core = own_core()
    groups = batches((a, u, d), core)
    student, teacher, squares = logits_of(groups, student_head, teacher_head, core)
    student_out[...] = student
    teacher_out[...] = teacher
    squares_out[...] = squares
    zero_out[...] = jnp.zeros((1, LANES), F32)


def forward_mid(
    far, other_a, other_u, other_d, student_head, teacher_head,
    student_in, teacher_in, squares_in, student_out, teacher_out, squares_out,
):
    core = own_core()
    one = logits_of(batches((None, None, None, far), core)[3:], student_head, teacher_head, core)
    groups = batches((other_a, other_u, other_d), 1 - core)
    two = logits_of(groups, student_head, teacher_head, 1 - core)
    student_out[...] = one[0] + two[0] + student_in[...]
    teacher_out[...] = one[1] + two[1] + teacher_in[...]
    squares_out[...] = one[2] + two[2] + squares_in[...]


def forward_last(
    other_far, student_head, teacher_head, student_in, teacher_in, squares_in,
    exp_out, ratio_out, stats_out, tops_out, inverse_out,
):
    core = 1 - own_core()
    student, teacher, squares = logits_of(
        batches((None, None, None, other_far), core)[3:], student_head, teacher_head, core
    )
    squares = squares + squares_in[...]
    squares = jnp.where(lane_iota((SPARE, LANES)) >= VALID, squares, 0.0)
    lanes = spare_lanes()
    by_row = sum(dot(part, lanes, NT) for part in split(squares, 3))
    squares = total(jnp.where(spare_rows(), by_row, 0.0))
    inverse = lax.rsqrt(squares / DS + EPSILON)
    inverse_out[...] = inverse
    student = (student + student_in[...]) * inverse
    teacher = teacher + teacher_in[...]

    top_s = jnp.max(student, axis=0, keepdims=True)
    top_t = jnp.max(teacher, axis=0, keepdims=True)
    below = student - top_s
    exp_s = jnp.exp(below)
    below_t = teacher - top_t
    ratio = below - below_t
    exp_out[...] = exp_s
    ratio_out[...] = ratio
    weighted = exp_s * ratio
    stats = stack_rows(
        [
            top_s,
            total(exp_s),
            top_t,
            total(jnp.exp(below_t)),
            total(weighted),
            total(exp_s * below),
            total(weighted * below),
        ]
    )
    tops_out[...] = stats
    for v in range(VOC):
        stats_out[v] = stats


def combine_kernel(stats, out):
    tile = stack_rows(combined(stats))
    for g in range(GROUPS):
        out[g] = tile


def terms_of(groups, student_head, grad, core, out):
    for group in groups:
        head = jnp.concatenate(
            [student_head[span_of(v, core, HALF_S), :] for _, _, v in group], axis=0
        )
        term = dot(head, grad, NN).astype(BF)
        for i, (_, _, v) in enumerate(group):
            out[v] = term[i * HALF_S : (i + 1) * HALF_S]


def backward_one(
    stats, tops, exp_in, ratio_in, weight, inverse, student_head,
    grad_out, scaled_out, away, pull_out, loss_out,
):
    core = 1 - own_core()
    all_s, total_s, all_t, total_t, sum_d, sum_u, sum_du = combined(stats)
    inside = lane_iota((1, LANES)) < VALID
    mean_d = sum_d / total_s
    mean_u = sum_u / total_s
    covariance = sum_du / total_s - mean_d * mean_u
    divergence = mean_d - jnp.log(total_s) + jnp.log(total_t)
    loss_out[...] = jnp.sum(
        jnp.where(inside, weight[...] * divergence, 0.0), axis=1, keepdims=True
    )
    pull_out[...] = weight[...] * covariance * inverse[...] * inverse[...] / DS
    shift_s = tops[0:1, :] - all_s
    shift_t = tops[2:3, :] - all_t
    factor = weight[...] * jnp.exp(shift_s) / total_s
    offset = shift_s - shift_t - mean_d
    grad = jnp.where(inside, factor * exp_in[...] * (ratio_in[...] + offset), 0.0)
    kept = jnp.where(inside, inverse[...], 0.0)
    scaled_out[...] = (grad * kept).astype(BF)
    grad = grad.astype(BF)
    grad_out[...] = grad
    terms_of(batches((None,) * 4, core), student_head, grad, core, away)


def backward_two(*refs):
    mine, other = refs[:4], refs[4:8]
    grad, student_head, hidden, gain, student_row, inverse, pull = refs[8:15]
    stay, base_out, rows_out, sems = refs[15:]
    core = own_core()
    groups = batches(mine, core)
    copies = []
    for k, refs in enumerate((mine, other)):
        for j, ref in enumerate(refs):
            copies.append(
                pltpu.make_async_copy(
                    ref.at[:, pl.ds(0, HALF_S)],
                    rows_out.at[k, pl.ds(j * SIDE, SIDE)],
                    sems.at[k, j],
                )
            )
            copies[-1].start()
    first = lax.axis_index("grp") * ROWS
    own = lax.broadcasted_iota(jnp.int32, (ROWS, LANES), 0) + first == student_row[...]
    own_rms = jnp.sum(jnp.where(own, inverse[...], 0.0), axis=1, keepdims=True)
    own_pull = jnp.sum(jnp.where(own, pull[...], 0.0), axis=1, keepdims=True)
    base_out[:ROWS] = own_rms * gain[...]
    base_out[ROWS : 2 * ROWS] = hidden[...].astype(F32) * own_pull
    base_out[2 * ROWS :] = jnp.broadcast_to(1.0 / gain[...], (8, LANES))
    terms_of(groups, student_head, grad[...], core, stay)
    for copy in copies:
        copy.wait()


def head_kernel(source, scaled_in, out, rows, scaled, blocks, in_sems, scaled_sem, sems):
    waiting = []
    for k in range(2):
        for j in range(VOC // PER):
            waiting.append(
                pltpu.make_async_copy(
                    source.at[k, pl.ds(j * PER, PER)], rows.at[k, pl.ds(j * PER, PER)], in_sems.at[k, j]
                )
            )
    first = pltpu.make_async_copy(scaled_in, scaled, scaled_sem)
    first.start()
    for copy in waiting:
        copy.start()
    first.wait()
    copies = []
    for k, core in enumerate((own_core(), 1 - own_core())):
        groups = batches((None,) * 4, core)
        for j in range(VOC // PER):
            waiting[k * (VOC // PER) + j].wait()
            block = rows[k, pl.ds(j * PER, PER)].reshape(PER * HALF_S, LANES)
            result = dot(block, scaled[...], NT).astype(BF)
            for i, (_, _, v) in enumerate(groups[j]):
                n = len(copies)
                blocks[n] = result[i * HALF_S : (i + 1) * HALF_S]
                copies.append(
                    pltpu.make_async_copy(
                        blocks.at[n], out.at[span_of(v, core, HALF_S)], sems.at[n]
                    )
                )
                copies[n].start()
    for copy in copies:
        copy.wait()


def pair_kernel(stay, arrived, out):
    for v in range(VOC):
        out[v] = (stay[v].astype(F32) + arrived[v].astype(F32)).astype(BF)


def send_kernel(pieces, student_row, block, inverse, out):
    summed = pieces[0].astype(F32)
    for v in range(1, VOC):
        summed = summed + pieces[v].astype(F32)
    lane = lane_iota((HALF_S, LANES))
    inside = lane < VALID
    scaled = jnp.where(inside, block[:HALF_S, :].astype(F32) * inverse[...], 0.0)
    gain = jnp.sum(summed * scaled, axis=1, keepdims=True)
    summed = jnp.where(lane == VALID, gain, summed).astype(BF)
    slot = lax.broadcasted_iota(jnp.int32, (SEND, LANES), 0)
    extra = (slot == ROWS) & (lane_iota((SEND, LANES)) == VALID)
    picks = []
    for g in range(GROUPS):
        pick = ((slot < ROWS) & (student_row[...] == slot + g * ROWS)) | extra
        picks.append(jnp.where(pick, 1.0, 0.0).astype(BF))
    result = dot(jnp.concatenate(picks, axis=0), summed, NT).astype(BF)
    for g in range(GROUPS):
        out[g] = result[g * SEND : (g + 1) * SEND]


def finish_kernel(pieces_in, base_in, grad_hidden, grad_gain, pieces, base, sems):
    copies = [
        pltpu.make_async_copy(pieces_in, pieces, sems.at[0]),
        pltpu.make_async_copy(base_in, base, sems.at[1]),
    ]
    for copy in copies:
        copy.start()
    for copy in copies:
        copy.wait()
    halves = []
    for c in range(2):
        summed = pieces[c].astype(F32)
        for z in range(1, GROUPS // 2):
            summed = summed + pieces[2 * z + c].astype(F32)
        halves.append(summed)
    summed = jnp.concatenate(halves, axis=1)
    grad_gain[...] = summed[ROWS : ROWS + 1] * base[2 * ROWS : 2 * ROWS + 1]
    grad_hidden[...] = (summed[:ROWS] * base[:ROWS] - base[ROWS : 2 * ROWS]).astype(BF)


def shape(dims, dtype):
    return jax.ShapeDtypeStruct(dims, dtype)


def params(mib):
    return pltpu.CompilerParams(vmem_limit_bytes=mib * 1024 * 1024)


def in_hbm(x):
    return pltpu.with_memory_space_constraint(x, pltpu.HBM)


def cost(flops):
    return pl.CostEstimate(flops=flops, bytes_accessed=4 * 1024 * 1024, transcendentals=0)


def exchange(x, axis):
    return lax.all_to_all(x, axis, 0, 0, tiled=True)


HBM = pl.BlockSpec(memory_space=pltpu.HBM)
ANY = pl.BlockSpec(memory_space=pl.ANY)
VMEM = pl.BlockSpec(memory_space=pltpu.VMEM)


def local(
    student_hidden, norm_gain, teacher_hidden, student_head, teacher_head, episode_source, lengths
):
    core = own_core()
    row = shape((1, LANES), F32)
    logits = shape((VOC_DEV, LANES), F32)
    half_rows = shape((VOC, HALF_S, LANES), BF)
    student_row, teacher_row, weight = lane_tables(episode_source, lengths)

    packed = pl.pallas_call(
        pack_kernel,
        out_shape=pltpu.HBM((GROUPS, PACK, HALF_S), BF),
        in_specs=[HBM] * 2,
        out_specs=VMEM,
        scratch_shapes=[
            pltpu.VMEM((ROWS, 2 * HALF_S), BF),
            pltpu.VMEM((ROWS, 2 * HALF_T), BF),
            pltpu.SemaphoreType.DMA((2,)),
        ],
        compiler_params=params(4),
    )(in_hbm(student_hidden), in_hbm(teacher_hidden))
    held = exchange(packed, "grp")

    gain_half = lax.dynamic_slice_in_dim(norm_gain, core * HALF_S, HALF_S)
    gain_high = rounded(gain_half)
    gain_mid = rounded(gain_half - gain_high)
    gain_low = gain_half - gain_high - gain_mid
    gain_parts = jnp.concatenate(
        [jnp.stack([gain_high, gain_mid, gain_low]), jnp.zeros((13, HALF_S), F32)], axis=0
    )
    block, student_row, weight = pl.pallas_call(
        compact_kernel,
        out_shape=(shape((HALF, LANES), BF), shape((1, LANES), jnp.int32), row),
        compiler_params=params(8),
    )(held, student_row, teacher_row, weight, gain_parts)

    one = lax.ppermute(block, BOTH, ring(1, 1))
    three = lax.ppermute(block, BOTH, ring(1, 3))
    two = lax.ppermute(block, BOTH, ring(1, 2))
    first = jnp.stack([block, one])
    second = jnp.stack([two, three])
    u_first = lax.ppermute(first, BOTH, ring(2, 1))
    d_second = lax.ppermute(second, BOTH, ring(2, 3))
    u_second = lax.ppermute(second, BOTH, ring(2, 1))
    d_first = lax.ppermute(first, BOTH, ring(2, 3))
    v = lax.ppermute(u_first, BOTH, ring(2, 1))
    w = lax.ppermute(d_second, BOTH, ring(2, 3))
    a = jnp.concatenate([first, second], axis=0)
    u = jnp.concatenate([u_first, u_second], axis=0)
    d = jnp.concatenate([d_first, d_second], axis=0)
    other = tuple(lax.ppermute(part, "grp", CORE_SWAP) for part in (a, u, d))

    partial = (logits, logits, shape((SPARE, LANES), F32))
    *sums, zero = pl.pallas_call(
        forward_near,
        out_shape=partial + (row,),
        compiler_params=params(12),
        cost_estimate=cost(12 * HALF * VOC_DEV * LANES * 2),
    )(a, u, d, student_head, teacher_head)
    far = jnp.concatenate([v, w], axis=0) + zero.astype(BF)
    mine = (a, u, d, far)
    other = other + (lax.ppermute(far, "grp", CORE_SWAP),)
    sums = pl.pallas_call(
        forward_mid,
        out_shape=partial,
        compiler_params=params(12),
        cost_estimate=cost(VOC * HALF * VOC_DEV * LANES * 2),
    )(far, *other[:3], student_head, teacher_head, *sums)
    exp_s, ratio, stats, tops, inverse = pl.pallas_call(
        forward_last,
        out_shape=(
            logits,
            logits,
            shape((VOC, STATS, LANES), F32),
            shape((STATS, LANES), F32),
            row,
        ),
        compiler_params=params(12),
        cost_estimate=cost(4 * HALF * VOC_DEV * LANES * 2),
    )(other[3], student_head, teacher_head, *sums)

    from_voc = exchange(stats, "voc")
    spread = pl.pallas_call(
        combine_kernel, out_shape=shape((GROUPS, STATS, LANES), F32), compiler_params=params(4)
    )(from_voc)
    from_grp = exchange(spread, "grp")

    grad, scaled, away, pull, loss = pl.pallas_call(
        backward_one,
        out_shape=(
            shape((VOC_DEV, LANES), BF),
            pltpu.HBM((VOC_DEV, LANES), BF),
            half_rows,
            row,
            shape((1, 1), F32),
        ),
        out_specs=(VMEM,) * 5,
        compiler_params=params(8),
        cost_estimate=cost(DS * VOC_DEV * LANES),
    )(from_grp, tops, exp_s, ratio, weight, inverse, student_head)
    arrived = lax.ppermute(away, "grp", CORE_SWAP)
    stay, base, rows = pl.pallas_call(
        backward_two,
        out_shape=(
            half_rows,
            pltpu.HBM((2 * ROWS + 8, LANES), F32),
            pltpu.HBM((2, VOC, HALF_S, LANES), BF),
        ),
        out_specs=(VMEM, VMEM, HBM),
        scratch_shapes=[pltpu.SemaphoreType.DMA((2, SIDE))],
        compiler_params=params(8),
        cost_estimate=cost(DS * VOC_DEV * LANES),
    )(
        *mine, *other, grad, student_head,
        student_hidden, norm_gain[None], student_row, inverse, pull,
    )
    pair = pl.pallas_call(pair_kernel, out_shape=half_rows, compiler_params=params(8))(
        stay, arrived
    )
    pieces = exchange(pair, "voc")
    grad_head = pl.pallas_call(
        head_kernel,
        out_shape=shape((DS, VOC_DEV), BF),
        in_specs=[HBM] * 2,
        out_specs=HBM,
        scratch_shapes=[
            pltpu.VMEM((2, VOC, HALF_S, LANES), BF),
            pltpu.VMEM((VOC_DEV, LANES), BF),
            pltpu.VMEM((2 * VOC, HALF_S, VOC_DEV), BF),
            pltpu.SemaphoreType.DMA((2, VOC // PER)),
            pltpu.SemaphoreType.DMA,
            pltpu.SemaphoreType.DMA((2 * VOC,)),
        ],
        compiler_params=params(12),
        cost_estimate=cost(DS * VOC_DEV * LANES * 2),
    )(in_hbm(rows), in_hbm(scaled))
    outgoing = pl.pallas_call(
        send_kernel,
        out_shape=pltpu.HBM((GROUPS, SEND, HALF_S), BF),
        out_specs=VMEM,
        compiler_params=params(8),
    )(pieces, student_row, block, inverse)
    pieces = exchange(outgoing, "grp")
    grad_hidden, grad_gain = pl.pallas_call(
        finish_kernel,
        out_shape=(shape((ROWS, 2 * HALF_S), BF), row),
        in_specs=[ANY, HBM],
        scratch_shapes=[
            pltpu.VMEM((GROUPS, SEND, HALF_S), BF),
            pltpu.VMEM((2 * ROWS + 8, LANES), F32),
            pltpu.SemaphoreType.DMA((2,)),
        ],
        compiler_params=params(4),
    )(pieces, in_hbm(base))
    return (loss.reshape(()), grad_hidden, grad_gain.reshape(-1), grad_head)


def solution(mesh):
    placed = (
        P("grp", "voc"),
        P("voc"),
        P("grp", "voc"),
        P(None, ("grp", "voc")),
        P(None, ("grp", "voc")),
        P(),
        P(),
    )
    return jax.shard_map(
        local,
        mesh=mesh,
        in_specs=placed,
        out_specs=(P(), P("grp", "voc"), P("voc"), P(None, ("grp", "voc"))),
        check_vma=False,
    )
```

```python
import jax
import jax.numpy as jnp
from jax import lax
from jax.experimental import pallas as pl
from jax.experimental.pallas import tpu as pltpu
from jax.sharding import PartitionSpec as P

DS = 4096
SEQ = 2
VALID = 240
LANES = 256
EPSILON = 1e-06
GROUPS = 16
VOC = 16
ROWS = 24
HALF_S = 128
HALF_T = 160
HALF = HALF_S + HALF_T
VOC_DEV = 384
STATS = 8
SEND = 32
PACK = 56
TAIL = 32
PER = 4
SPARE = 16
SIDE = 4
BF = jnp.bfloat16
F32 = jnp.float32
CORE_SWAP = [(i, i ^ 1) for i in range(GROUPS)]
BOTH = ("grp", "voc")


def ring(phase, step):
    pairs = []
    for g in range(GROUPS):
        for v in range(VOC):
            y, x = divmod(v, SIDE)
            if (g % 2 == 0) == (phase == 1):
                x = (x + step) % SIDE
            else:
                y = (y + step) % SIDE
            pairs.append((g * VOC + v, g * VOC + y * SIDE + x))
    return pairs


TN = (((0,), (0,)), ((), ()))
NT = (((1,), (1,)), ((), ()))
NN = (((1,), (0,)), ((), ()))


def rounded(x):
    return lax.reduce_precision(x, 8, 7)


def dot(a, b, dims):
    return lax.dot_general(a, b, dims, preferred_element_type=F32)


def lane_tables(episode_source, lengths):
    episodes = lengths.shape[0]
    two = (lengths == 2).astype(jnp.int32)
    before = jnp.arange(episodes)[None, :] < jnp.arange(episodes)[:, None]
    rank = jnp.sum(jnp.where(before, two[None, :], 0), axis=1)
    lane = jnp.arange(LANES, dtype=jnp.int32)
    number = jnp.arange(episodes, dtype=jnp.int32)
    first = lane[None, :] == number[:, None]
    second = (two[:, None] == 1) & (lane[None, :] == episodes + rank[:, None])
    pick = first | second
    position = (lane >= episodes).astype(jnp.int32)
    inside = lane < VALID
    episode = jnp.sum(jnp.where(pick, number[:, None], 0), axis=0)
    source = jnp.sum(jnp.where(pick, episode_source[:, None], 0), axis=0)
    length = jnp.sum(jnp.where(pick, lengths[:, None], 0), axis=0)
    student_row = jnp.where(inside, episode * SEQ + position, -1)
    teacher_row = jnp.where(inside, source * SEQ + position, -1)
    weight = jnp.where(inside, 1.0 / jnp.maximum(length, 1).astype(F32), 0.0)
    return student_row[None], teacher_row[None], weight[None]


def own_core():
    return lax.rem(lax.axis_index("grp"), 2)


def lane_iota(shape):
    return lax.broadcasted_iota(jnp.int32, shape, len(shape) - 1)


def pack_kernel(student_in, teacher_in, out, student, teacher, in_sems):
    copies = [
        pltpu.make_async_copy(student_in, student, in_sems.at[0]),
        pltpu.make_async_copy(teacher_in, teacher, in_sems.at[1]),
    ]
    for copy in copies:
        copy.start()
    for copy in copies:
        copy.wait()
    for c in range(2):
        rows = teacher[:, c * HALF_T : (c + 1) * HALF_T].astype(F32)
        tail = rows[:, HALF_S:]
        tail = jnp.concatenate(
            [tail[:8], tail[8:16], tail[16:24], jnp.zeros((8, TAIL), F32)], axis=1
        )
        whole = jnp.concatenate(
            [student[:, c * HALF_S : (c + 1) * HALF_S].astype(F32), rows[:, :HALF_S], tail], axis=0
        )
        whole = whole.astype(BF)
        for z in range(GROUPS // 2):
            out[2 * z + c] = whole


def spare_lanes():
    source = lax.broadcasted_iota(jnp.int32, (LANES, LANES), 0)
    lane = lane_iota((LANES, LANES))
    return jnp.where(lane == VALID + lax.rem(source, SPARE), 1.0, 0.0).astype(BF)


def spare_rows():
    row = lax.broadcasted_iota(jnp.int32, (SPARE, LANES), 0)
    return lax.div(lane_iota((SPARE, LANES)), SPARE) == row


def split(x, parts):
    out = []
    for _ in range(parts):
        out.append(x.astype(BF))
        x = x - out[-1].astype(F32)
    return out


def compact_kernel(held, student_row, teacher_row, weight, gain, out, row_out, weight_out):
    row_out[...] = student_row[...]
    weight_out[...] = weight[...]
    blocks = [held[g].astype(F32) for g in range(GROUPS)]
    rows_s = jnp.concatenate([block[:ROWS] for block in blocks], axis=0).astype(BF)
    rows_t = jnp.concatenate([block[ROWS : 2 * ROWS] for block in blocks], axis=0).astype(BF)
    tails = jnp.concatenate([block[2 * ROWS :] for block in blocks], axis=0).astype(BF)
    ids = lax.broadcasted_iota(jnp.int32, (GROUPS * ROWS, LANES), 0)
    pick_s = jnp.where(ids == student_row[...], 1.0, 0.0).astype(BF)
    pick_t = jnp.where(ids == teacher_row[...], 1.0, 0.0).astype(BF)
    block_s = dot(rows_s, pick_s, TN)
    block_t = dot(rows_t, pick_t, TN).astype(BF)
    short = lax.broadcasted_iota(jnp.int32, (GROUPS * 8, LANES), 0)
    short = lax.div(short, 8) * ROWS + lax.rem(short, 8)
    tail = jnp.zeros((TAIL, LANES), F32)
    for k in range(3):
        pick = jnp.where(short + 8 * k == teacher_row[...], 1.0, 0.0).astype(BF)
        tail = tail + dot(tails, pick, TN)[k * TAIL : (k + 1) * TAIL]
    spread_gain = dot(gain[...].astype(BF), jnp.ones((16, LANES), BF), TN)
    squares = jnp.sum(block_s * block_s, axis=0, keepdims=True)
    parts = split(jnp.where(spare_rows(), squares, 0.0), 2)
    lanes = spare_lanes()
    spare = jnp.concatenate([dot(part, lanes, NN) for part in parts], axis=0)
    block_s = block_s * spread_gain
    block_s = jnp.concatenate([block_s[: 2 * SPARE] + spare, block_s[2 * SPARE :]], axis=0)
    out[:HALF_S, :] = block_s.astype(BF)
    out[HALF_S : 2 * HALF_S, :] = block_t
    out[2 * HALF_S :, :] = tail.astype(BF)


def stack_rows(values):
    row = lax.broadcasted_iota(jnp.int32, (STATS, LANES), 0)
    out = jnp.zeros((STATS, LANES), F32)
    for k, value in enumerate(values):
        out = jnp.where(row == k, value, out)
    return out


def total(x):
    return jnp.sum(x, axis=0, keepdims=True)


def combined(stats):
    top_s, sum_s, top_t, sum_t, mean_d, mean_u, mean_du = [stats[:, k, :] for k in range(7)]
    all_s = jnp.max(top_s, axis=0, keepdims=True)
    all_t = jnp.max(top_t, axis=0, keepdims=True)
    shift_s = top_s - all_s
    shift_t = top_t - all_t
    scale_s = jnp.exp(shift_s)
    scale_t = jnp.exp(shift_t)
    shift_d = shift_s - shift_t
    return (
        all_s,
        total(scale_s * sum_s),
        all_t,
        total(scale_t * sum_t),
        total(scale_s * (mean_d + shift_d * sum_s)),
        total(scale_s * (mean_u + shift_s * sum_s)),
        total(
            scale_s
            * (mean_du + shift_s * mean_d + shift_d * mean_u + shift_s * shift_d * sum_s)
        ),
    )


def span_of(v, core, half):
    return pl.ds(pl.multiple_of(v * 2 * half + core * half, 32), half)


def places(core):
    index = lax.axis_index("voc")
    x, y = lax.rem(index, SIDE), lax.div(index, SIDE)
    a = lax.select(core == 0, x, y)
    b = lax.select(core == 0, y, x)

    def place(j, k):
        u = lax.rem(a + SIDE - j, SIDE)
        w = lax.rem(b + SIDE - k, SIDE)
        return lax.select(core == 0, SIDE * w + u, SIDE * u + w)

    return place


def batches(refs, core):
    place = places(core)
    return [
        [(ref, j, place(j, k)) for j in range(SIDE)] for ref, k in zip(refs, (0, 1, 3, 2))
    ]


def logits_of(groups, student_head, teacher_head, core):
    student = jnp.zeros((VOC_DEV, LANES), F32)
    teacher = jnp.zeros((VOC_DEV, LANES), F32)
    squares = jnp.zeros((SPARE, LANES), F32)
    for group in groups:
        head_s = jnp.concatenate(
            [student_head[span_of(v, core, HALF_S), :] for _, _, v in group], axis=0
        )
        head_t = jnp.concatenate(
            [teacher_head[span_of(v, core, HALF_T), :] for _, _, v in group], axis=0
        )
        rows_s = jnp.concatenate([ref[j, :HALF_S, :] for ref, j, _ in group], axis=0)
        rows_t = jnp.concatenate([ref[j, HALF_S:, :] for ref, j, _ in group], axis=0)
        student = student + dot(head_s, rows_s, TN)
        teacher = teacher + dot(head_t, rows_t, TN)
        for ref, j, _ in group:
            squares = squares + ref[j, :SPARE, :].astype(F32)
            squares = squares + ref[j, SPARE : 2 * SPARE, :].astype(F32)
    return student, teacher, squares


def forward_own(
    a, u_first, d_second, student_head, teacher_in,
    student_out, teacher_out, squares_out, teacher_head, zero_out, sem,
):
    copy = pltpu.make_async_copy(teacher_in, teacher_head, sem)
    copy.start()
    zero_out[...] = jnp.zeros((1, LANES), F32)
    copy.wait()
    core = own_core()
    student, teacher, squares = logits_of(batches((a,), core), student_head, teacher_head, core)
    student_out[...] = student
    teacher_out[...] = teacher
    squares_out[...] = squares


def save_rows(refs, out, sems):
    copies = []
    for k, ref in enumerate(refs):
        copies.append(
            pltpu.make_async_copy(
                ref.at[:, pl.ds(0, HALF_S)], out.at[pl.ds(k * SIDE, SIDE)], sems.at[k]
            )
        )
        copies[k].start()
    return copies


def forward_near(
    a, u, d, student_head, teacher_head, student_sum, teacher_sum, squares_sum,
    student_out, teacher_out, squares_out, zero_out, rows_out, row_sems,
):
    core = own_core()
    saved = save_rows((a, u, d), rows_out, row_sems)
    groups = batches((None, u, d), core)[1:]
    student, teacher, squares = logits_of(groups, student_head, teacher_head, core)
    student_out[...] = student + student_sum[...]
    teacher_out[...] = teacher + teacher_sum[...]
    squares_out[...] = squares + squares_sum[...]
    zero_out[...] = jnp.zeros((1, LANES), F32)
    for copy in saved:
        copy.wait()


def forward_mid(
    far, other_a, other_u, other_d, student_head, teacher_head,
    student_sum, teacher_sum, squares_sum, student_out, teacher_out, squares_out,
):
    core = own_core()
    groups = batches((None, None, None, far), core)[3:]
    one = logits_of(groups, student_head, teacher_head, core)
    groups = batches((other_a, other_u, other_d), 1 - core)
    two = logits_of(groups, student_head, teacher_head, 1 - core)
    student_out[...] = one[0] + two[0] + student_sum[...]
    teacher_out[...] = one[1] + two[1] + teacher_sum[...]
    squares_out[...] = one[2] + two[2] + squares_sum[...]


def forward_last(
    other_far, student_head, teacher_head, student_in, teacher_in, squares_in,
    exp_out, ratio_out, stats_out, tops_out, inverse_out,
):
    core = 1 - own_core()
    student, teacher, squares = logits_of(
        batches((None, None, None, other_far), core)[3:], student_head, teacher_head, core
    )
    squares = squares + squares_in[...]
    squares = jnp.where(lane_iota((SPARE, LANES)) >= VALID, squares, 0.0)
    lanes = spare_lanes()
    by_row = sum(dot(part, lanes, NT) for part in split(squares, 3))
    squares = total(jnp.where(spare_rows(), by_row, 0.0))
    inverse = lax.rsqrt(squares / DS + EPSILON)
    inverse_out[...] = inverse
    student = (student + student_in[...]) * inverse
    teacher = teacher + teacher_in[...]

    top_s = jnp.max(student, axis=0, keepdims=True)
    top_t = jnp.max(teacher, axis=0, keepdims=True)
    below = student - top_s
    exp_s = jnp.exp(below)
    below_t = teacher - top_t
    ratio = below - below_t
    exp_out[...] = exp_s
    ratio_out[...] = ratio
    weighted = exp_s * ratio
    stats = stack_rows(
        [
            top_s,
            total(exp_s),
            top_t,
            total(jnp.exp(below_t)),
            total(weighted),
            total(exp_s * below),
            total(weighted * below),
        ]
    )
    tops_out[...] = stats
    for v in range(VOC):
        stats_out[v] = stats


def combine_kernel(stats, out):
    tile = stack_rows(combined(stats))
    for g in range(GROUPS):
        out[g] = tile


def terms_of(groups, student_head, grad, core, out):
    for group in groups:
        head = jnp.concatenate(
            [student_head[span_of(v, core, HALF_S), :] for _, _, v in group], axis=0
        )
        term = dot(head, grad, NN).astype(BF)
        for i, (_, _, v) in enumerate(group):
            out[v] = term[i * HALF_S : (i + 1) * HALF_S]


def backward_one(
    stats, tops, exp_in, ratio_in, weight, inverse, student_head,
    grad_out, scaled_out, away, pull_out, loss_out,
):
    core = 1 - own_core()
    all_s, total_s, all_t, total_t, sum_d, sum_u, sum_du = combined(stats)
    inside = lane_iota((1, LANES)) < VALID
    mean_d = sum_d / total_s
    mean_u = sum_u / total_s
    covariance = sum_du / total_s - mean_d * mean_u
    divergence = mean_d - jnp.log(total_s) + jnp.log(total_t)
    loss_out[...] = jnp.sum(
        jnp.where(inside, weight[...] * divergence, 0.0), axis=1, keepdims=True
    )
    pull_out[...] = weight[...] * covariance * inverse[...] * inverse[...] / DS
    shift_s = tops[0:1, :] - all_s
    shift_t = tops[2:3, :] - all_t
    factor = weight[...] * jnp.exp(shift_s) / total_s
    offset = shift_s - shift_t - mean_d
    grad = jnp.where(inside, factor * exp_in[...] * (ratio_in[...] + offset), 0.0)
    kept = jnp.where(inside, inverse[...], 0.0)
    scaled_out[...] = (grad * kept).astype(BF)
    grad = grad.astype(BF)
    grad_out[...] = grad
    terms_of(batches((None,) * 4, core), student_head, grad, core, away)


def backward_two(*refs):
    grad, student_head, hidden, gain, student_row, inverse, pull = refs[5:12]
    stay, base_out, rows_out, sems = refs[12:]
    saved = save_rows(refs[:5], rows_out, sems)
    core = own_core()
    first = lax.axis_index("grp") * ROWS
    own = lax.broadcasted_iota(jnp.int32, (ROWS, LANES), 0) + first == student_row[...]
    own_rms = jnp.sum(jnp.where(own, inverse[...], 0.0), axis=1, keepdims=True)
    own_pull = jnp.sum(jnp.where(own, pull[...], 0.0), axis=1, keepdims=True)
    base_out[:ROWS] = own_rms * gain[...]
    base_out[ROWS : 2 * ROWS] = hidden[...].astype(F32) * own_pull
    base_out[2 * ROWS :] = jnp.broadcast_to(1.0 / gain[...], (8, LANES))
    terms_of(batches((None,) * 4, core), student_head, grad[...], core, stay)
    for copy in saved:
        copy.wait()


def head_kernel(
    near, rest, scaled_in, out, rows, scaled, blocks, in_sems, scaled_sem, sems
):
    first = pltpu.make_async_copy(scaled_in, scaled, scaled_sem)
    first.start()
    waiting = []
    for n in range(2 * SIDE):
        source, start = (near, n) if n < 3 else (rest, n - 3)
        waiting.append(
            pltpu.make_async_copy(
                source.at[pl.ds(start * SIDE, SIDE)], rows.at[pl.ds(n * SIDE, SIDE)], in_sems.at[n]
            )
        )
        waiting[n].start()
    first.wait()
    copies = []
    for k, core in enumerate((own_core(), 1 - own_core())):
        groups = batches((None,) * 4, core)
        for j in range(SIDE):
            m = k * SIDE + j
            waiting[m].wait()
            block = rows[pl.ds(m * SIDE, SIDE)].reshape(SIDE * HALF_S, LANES)
            result = dot(block, scaled[...], NT).astype(BF)
            for i, (_, _, v) in enumerate(groups[j]):
                n = len(copies)
                blocks[n] = result[i * HALF_S : (i + 1) * HALF_S]
                copies.append(
                    pltpu.make_async_copy(
                        blocks.at[n], out.at[span_of(v, core, HALF_S)], sems.at[n]
                    )
                )
                copies[n].start()
    for copy in copies:
        copy.wait()


def pair_kernel(stay, arrived, out):
    for v in range(VOC):
        out[v] = (stay[v].astype(F32) + arrived[v].astype(F32)).astype(BF)


def send_kernel(pieces, student_row, block, inverse, out):
    summed = pieces[0].astype(F32)
    for v in range(1, VOC):
        summed = summed + pieces[v].astype(F32)
    lane = lane_iota((HALF_S, LANES))
    inside = lane < VALID
    scaled = jnp.where(inside, block[:HALF_S, :].astype(F32) * inverse[...], 0.0)
    gain = jnp.sum(summed * scaled, axis=1, keepdims=True)
    summed = jnp.where(lane == VALID, gain, summed).astype(BF)
    slot = lax.broadcasted_iota(jnp.int32, (SEND, LANES), 0)
    extra = (slot == ROWS) & (lane_iota((SEND, LANES)) == VALID)
    picks = []
    for g in range(GROUPS):
        pick = ((slot < ROWS) & (student_row[...] == slot + g * ROWS)) | extra
        picks.append(jnp.where(pick, 1.0, 0.0).astype(BF))
    result = dot(jnp.concatenate(picks, axis=0), summed, NT).astype(BF)
    for g in range(GROUPS):
        out[g] = result[g * SEND : (g + 1) * SEND]


def finish_kernel(pieces_in, base_in, grad_hidden, grad_gain, pieces, base, sems):
    copies = [
        pltpu.make_async_copy(pieces_in, pieces, sems.at[0]),
        pltpu.make_async_copy(base_in, base, sems.at[1]),
    ]
    for copy in copies:
        copy.start()
    for copy in copies:
        copy.wait()
    halves = []
    for c in range(2):
        summed = pieces[c].astype(F32)
        for z in range(1, GROUPS // 2):
            summed = summed + pieces[2 * z + c].astype(F32)
        halves.append(summed)
    summed = jnp.concatenate(halves, axis=1)
    grad_gain[...] = summed[ROWS : ROWS + 1] * base[2 * ROWS : 2 * ROWS + 1]
    grad_hidden[...] = (summed[:ROWS] * base[:ROWS] - base[ROWS : 2 * ROWS]).astype(BF)


def shape(dims, dtype):
    return jax.ShapeDtypeStruct(dims, dtype)


def params(mib):
    return pltpu.CompilerParams(vmem_limit_bytes=mib * 1024 * 1024)


def in_hbm(x):
    return pltpu.with_memory_space_constraint(x, pltpu.HBM)


def cost(flops):
    return pl.CostEstimate(flops=flops, bytes_accessed=4 * 1024 * 1024, transcendentals=0)


def exchange(x, axis):
    return lax.all_to_all(x, axis, 0, 0, tiled=True)


HBM = pl.BlockSpec(memory_space=pltpu.HBM)
ANY = pl.BlockSpec(memory_space=pl.ANY)
VMEM = pl.BlockSpec(memory_space=pltpu.VMEM)


def local(
    student_hidden, norm_gain, teacher_hidden, student_head, teacher_head, episode_source, lengths
):
    core = own_core()
    row = shape((1, LANES), F32)
    logits = shape((VOC_DEV, LANES), F32)
    half_rows = shape((VOC, HALF_S, LANES), BF)
    student_row, teacher_row, weight = lane_tables(episode_source, lengths)

    packed = pl.pallas_call(
        pack_kernel,
        out_shape=pltpu.HBM((GROUPS, PACK, HALF_S), BF),
        in_specs=[HBM] * 2,
        out_specs=VMEM,
        scratch_shapes=[
            pltpu.VMEM((ROWS, 2 * HALF_S), BF),
            pltpu.VMEM((ROWS, 2 * HALF_T), BF),
            pltpu.SemaphoreType.DMA((2,)),
        ],
        compiler_params=params(4),
    )(in_hbm(student_hidden), in_hbm(teacher_hidden))
    held = exchange(packed, "grp")

    gain_half = lax.dynamic_slice_in_dim(norm_gain, core * HALF_S, HALF_S)
    gain_high = rounded(gain_half)
    gain_mid = rounded(gain_half - gain_high)
    gain_low = gain_half - gain_high - gain_mid
    gain_parts = jnp.concatenate(
        [jnp.stack([gain_high, gain_mid, gain_low]), jnp.zeros((13, HALF_S), F32)], axis=0
    )
    block, student_row, weight = pl.pallas_call(
        compact_kernel,
        out_shape=(shape((HALF, LANES), BF), shape((1, LANES), jnp.int32), row),
        compiler_params=params(8),
    )(held, student_row, teacher_row, weight, gain_parts)

    one = lax.ppermute(block, BOTH, ring(1, 1))
    three = lax.ppermute(block, BOTH, ring(1, 3))
    two = lax.ppermute(block, BOTH, ring(1, 2))
    first = jnp.stack([block, one])
    second = jnp.stack([two, three])
    u_first = lax.ppermute(first, BOTH, ring(2, 1))
    d_second = lax.ppermute(second, BOTH, ring(2, 3))
    u_second = lax.ppermute(second, BOTH, ring(2, 1))
    d_first = lax.ppermute(first, BOTH, ring(2, 3))
    v = lax.ppermute(u_first, BOTH, ring(2, 1))
    w = lax.ppermute(d_second, BOTH, ring(2, 3))
    a = jnp.concatenate([first, second], axis=0)
    u = jnp.concatenate([u_first, u_second], axis=0)
    d = jnp.concatenate([d_first, d_second], axis=0)
    partial = (logits, logits, shape((SPARE, LANES), F32))

    def sems(count):
        return pltpu.SemaphoreType.DMA((count,))

    *sums, head_t, zero = pl.pallas_call(
        forward_own,
        out_shape=partial + (pltpu.VMEM(teacher_head.shape, BF), row),
        in_specs=[VMEM, ANY, ANY, VMEM, HBM],
        out_specs=(VMEM,) * 5,
        scratch_shapes=[pltpu.SemaphoreType.DMA],
        compiler_params=params(12),
        cost_estimate=cost(SIDE * HALF * VOC_DEV * LANES * 2),
    )(a, u_first, d_second, student_head, in_hbm(teacher_head))
    other = (lax.ppermute(a, "grp", CORE_SWAP),) + tuple(
        lax.ppermute(part + zero.astype(BF), "grp", CORE_SWAP) for part in (u, d)
    )
    *sums, zero, saved_near = pl.pallas_call(
        forward_near,
        out_shape=partial + (row, pltpu.HBM((3 * SIDE, HALF_S, LANES), BF)),
        out_specs=(VMEM,) * 4 + (HBM,),
        scratch_shapes=[sems(3)],
        compiler_params=params(12),
        cost_estimate=cost(2 * SIDE * HALF * VOC_DEV * LANES * 2),
    )(a, u, d, student_head, head_t, *sums)
    far = jnp.concatenate([v, w], axis=0) + zero.astype(BF)
    other_far = lax.ppermute(far, "grp", CORE_SWAP)
    sums = pl.pallas_call(
        forward_mid,
        out_shape=partial,
        compiler_params=params(12),
        cost_estimate=cost(VOC * HALF * VOC_DEV * LANES * 2),
    )(far, *other, student_head, head_t, *sums)
    exp_s, ratio, stats, tops, inverse = pl.pallas_call(
        forward_last,
        out_shape=(
            logits,
            logits,
            shape((VOC, STATS, LANES), F32),
            shape((STATS, LANES), F32),
            row,
        ),
        compiler_params=params(12),
        cost_estimate=cost(SIDE * HALF * VOC_DEV * LANES * 2),
    )(other_far, student_head, head_t, *sums)

    from_voc = exchange(stats, "voc")
    spread = pl.pallas_call(
        combine_kernel, out_shape=shape((GROUPS, STATS, LANES), F32), compiler_params=params(4)
    )(from_voc)
    from_grp = exchange(spread, "grp")

    grad, scaled, away, pull, loss = pl.pallas_call(
        backward_one,
        out_shape=(
            shape((VOC_DEV, LANES), BF),
            pltpu.HBM((VOC_DEV, LANES), BF),
            half_rows,
            row,
            shape((1, 1), F32),
        ),
        out_specs=(VMEM,) * 5,
        compiler_params=params(8),
        cost_estimate=cost(DS * VOC_DEV * LANES),
    )(from_grp, tops, exp_s, ratio, weight, inverse, student_head)
    arrived = lax.ppermute(away, "grp", CORE_SWAP)
    stay, base, saved_rest = pl.pallas_call(
        backward_two,
        out_shape=(
            half_rows,
            pltpu.HBM((2 * ROWS + 8, LANES), F32),
            pltpu.HBM((5 * SIDE, HALF_S, LANES), BF),
        ),
        out_specs=(VMEM, VMEM, HBM),
        scratch_shapes=[sems(5)],
        compiler_params=params(8),
        cost_estimate=cost(DS * VOC_DEV * LANES),
    )(
        far, *other, other_far, grad, student_head,
        student_hidden, norm_gain[None], student_row, inverse, pull,
    )
    pair = pl.pallas_call(pair_kernel, out_shape=half_rows, compiler_params=params(8))(
        stay, arrived
    )
    pieces = exchange(pair, "voc")
    grad_head = pl.pallas_call(
        head_kernel,
        out_shape=shape((DS, VOC_DEV), BF),
        in_specs=[HBM] * 3,
        out_specs=HBM,
        scratch_shapes=[
            pltpu.VMEM((2 * VOC, HALF_S, LANES), BF),
            pltpu.VMEM((VOC_DEV, LANES), BF),
            pltpu.VMEM((2 * VOC, HALF_S, VOC_DEV), BF),
            pltpu.SemaphoreType.DMA((2 * SIDE,)),
            pltpu.SemaphoreType.DMA,
            pltpu.SemaphoreType.DMA((2 * VOC,)),
        ],
        compiler_params=params(12),
        cost_estimate=cost(DS * VOC_DEV * LANES * 2),
    )(in_hbm(saved_near), in_hbm(saved_rest), in_hbm(scaled))
    outgoing = pl.pallas_call(
        send_kernel,
        out_shape=pltpu.HBM((GROUPS, SEND, HALF_S), BF),
        out_specs=VMEM,
        compiler_params=params(8),
    )(pieces, student_row, block, inverse)
    pieces = exchange(outgoing, "grp")
    grad_hidden, grad_gain = pl.pallas_call(
        finish_kernel,
        out_shape=(shape((ROWS, 2 * HALF_S), BF), row),
        in_specs=[ANY, HBM],
        scratch_shapes=[
            pltpu.VMEM((GROUPS, SEND, HALF_S), BF),
            pltpu.VMEM((2 * ROWS + 8, LANES), F32),
            pltpu.SemaphoreType.DMA((2,)),
        ],
        compiler_params=params(4),
    )(pieces, in_hbm(base))
    return (loss.reshape(()), grad_hidden, grad_gain.reshape(-1), grad_head)


def solution(mesh):
    placed = (
        P("grp", "voc"),
        P("voc"),
        P("grp", "voc"),
        P(None, ("grp", "voc")),
        P(None, ("grp", "voc")),
        P(),
        P(),
    )
    return jax.shard_map(
        local,
        mesh=mesh,
        in_specs=placed,
        out_specs=(P(), P("grp", "voc"), P("voc"), P(None, ("grp", "voc"))),
        check_vma=False,
    )
```

```python
import jax
import jax.numpy as jnp
from jax import lax
from jax.experimental import pallas as pl
from jax.experimental.pallas import tpu as pltpu
from jax.sharding import PartitionSpec as P

DS = 4096
SEQ = 2
VALID = 240
LANES = 256
EPSILON = 1e-06
GROUPS = 16
VOC = 16
ROWS = 24
HALF_S = 128
HALF_T = 160
HALF = HALF_S + HALF_T
VOC_DEV = 384
STATS = 8
SEND = 32
PACK = 56
TAIL = 32
PER = 4
SPARE = 16
SIDE = 4
BF = jnp.bfloat16
F32 = jnp.float32
CORE_SWAP = [(i, i ^ 1) for i in range(GROUPS)]
BOTH = ("grp", "voc")


def ring(phase, step):
    pairs = []
    for g in range(GROUPS):
        for v in range(VOC):
            y, x = divmod(v, SIDE)
            if (g % 2 == 0) == (phase == 1):
                x = (x + step) % SIDE
            else:
                y = (y + step) % SIDE
            pairs.append((g * VOC + v, g * VOC + y * SIDE + x))
    return pairs


TN = (((0,), (0,)), ((), ()))
NT = (((1,), (1,)), ((), ()))
NN = (((1,), (0,)), ((), ()))


def rounded(x):
    return lax.reduce_precision(x, 8, 7)


def dot(a, b, dims):
    return lax.dot_general(a, b, dims, preferred_element_type=F32)


def lane_tables(episode_source, lengths):
    episodes = lengths.shape[0]
    two = (lengths == 2).astype(jnp.int32)
    before = jnp.arange(episodes)[None, :] < jnp.arange(episodes)[:, None]
    rank = jnp.sum(jnp.where(before, two[None, :], 0), axis=1)
    lane = jnp.arange(LANES, dtype=jnp.int32)
    number = jnp.arange(episodes, dtype=jnp.int32)
    first = lane[None, :] == number[:, None]
    second = (two[:, None] == 1) & (lane[None, :] == episodes + rank[:, None])
    pick = first | second
    position = (lane >= episodes).astype(jnp.int32)
    inside = lane < VALID
    episode = jnp.sum(jnp.where(pick, number[:, None], 0), axis=0)
    source = jnp.sum(jnp.where(pick, episode_source[:, None], 0), axis=0)
    length = jnp.sum(jnp.where(pick, lengths[:, None], 0), axis=0)
    student_row = jnp.where(inside, episode * SEQ + position, -1)
    teacher_row = jnp.where(inside, source * SEQ + position, -1)
    weight = jnp.where(inside, 1.0 / jnp.maximum(length, 1).astype(F32), 0.0)
    return student_row[None], teacher_row[None], weight[None]


def own_core():
    return lax.rem(lax.axis_index("grp"), 2)


def lane_iota(shape):
    return lax.broadcasted_iota(jnp.int32, shape, len(shape) - 1)


def pack_kernel(student_in, teacher_in, out, student, teacher, in_sems):
    copies = [
        pltpu.make_async_copy(student_in, student, in_sems.at[0]),
        pltpu.make_async_copy(teacher_in, teacher, in_sems.at[1]),
    ]
    for copy in copies:
        copy.start()
    for copy in copies:
        copy.wait()
    for c in range(2):
        rows = teacher[:, c * HALF_T : (c + 1) * HALF_T].astype(F32)
        tail = rows[:, HALF_S:]
        tail = jnp.concatenate(
            [tail[:8], tail[8:16], tail[16:24], jnp.zeros((8, TAIL), F32)], axis=1
        )
        whole = jnp.concatenate(
            [student[:, c * HALF_S : (c + 1) * HALF_S].astype(F32), rows[:, :HALF_S], tail], axis=0
        )
        whole = whole.astype(BF)
        for z in range(GROUPS // 2):
            out[2 * z + c] = whole


def spare_lanes():
    source = lax.broadcasted_iota(jnp.int32, (LANES, LANES), 0)
    lane = lane_iota((LANES, LANES))
    return jnp.where(lane == VALID + lax.rem(source, SPARE), 1.0, 0.0).astype(BF)


def spare_rows():
    row = lax.broadcasted_iota(jnp.int32, (SPARE, LANES), 0)
    return lax.div(lane_iota((SPARE, LANES)), SPARE) == row


def split(x, parts):
    out = []
    for _ in range(parts):
        out.append(x.astype(BF))
        x = x - out[-1].astype(F32)
    return out


def compact_kernel(held, student_row, teacher_row, weight, gain, out, row_out, weight_out):
    row_out[...] = student_row[...]
    weight_out[...] = weight[...]
    blocks = [held[g].astype(F32) for g in range(GROUPS)]
    rows_s = jnp.concatenate([block[:ROWS] for block in blocks], axis=0).astype(BF)
    rows_t = jnp.concatenate([block[ROWS : 2 * ROWS] for block in blocks], axis=0).astype(BF)
    tails = jnp.concatenate([block[2 * ROWS :] for block in blocks], axis=0).astype(BF)
    ids = lax.broadcasted_iota(jnp.int32, (GROUPS * ROWS, LANES), 0)
    pick_s = jnp.where(ids == student_row[...], 1.0, 0.0).astype(BF)
    pick_t = jnp.where(ids == teacher_row[...], 1.0, 0.0).astype(BF)
    block_s = dot(rows_s, pick_s, TN)
    block_t = dot(rows_t, pick_t, TN).astype(BF)
    short = lax.broadcasted_iota(jnp.int32, (GROUPS * 8, LANES), 0)
    short = lax.div(short, 8) * ROWS + lax.rem(short, 8)
    tail = jnp.zeros((TAIL, LANES), F32)
    for k in range(3):
        pick = jnp.where(short + 8 * k == teacher_row[...], 1.0, 0.0).astype(BF)
        tail = tail + dot(tails, pick, TN)[k * TAIL : (k + 1) * TAIL]
    spread_gain = dot(gain[...].astype(BF), jnp.ones((16, LANES), BF), TN)
    squares = jnp.sum(block_s * block_s, axis=0, keepdims=True)
    parts = split(jnp.where(spare_rows(), squares, 0.0), 2)
    lanes = spare_lanes()
    spare = jnp.concatenate([dot(part, lanes, NN) for part in parts], axis=0)
    block_s = block_s * spread_gain
    block_s = jnp.concatenate([block_s[: 2 * SPARE] + spare, block_s[2 * SPARE :]], axis=0)
    out[:HALF_S, :] = block_s.astype(BF)
    out[HALF_S : 2 * HALF_S, :] = block_t
    out[2 * HALF_S :, :] = tail.astype(BF)


def stack_rows(values):
    row = lax.broadcasted_iota(jnp.int32, (STATS, LANES), 0)
    out = jnp.zeros((STATS, LANES), F32)
    for k, value in enumerate(values):
        out = jnp.where(row == k, value, out)
    return out


def total(x):
    return jnp.sum(x, axis=0, keepdims=True)


def combined(stats):
    top_s, sum_s, top_t, sum_t, mean_d, mean_u, mean_du = [stats[:, k, :] for k in range(7)]
    all_s = jnp.max(top_s, axis=0, keepdims=True)
    all_t = jnp.max(top_t, axis=0, keepdims=True)
    shift_s = top_s - all_s
    shift_t = top_t - all_t
    scale_s = jnp.exp(shift_s)
    scale_t = jnp.exp(shift_t)
    shift_d = shift_s - shift_t
    return (
        all_s,
        total(scale_s * sum_s),
        all_t,
        total(scale_t * sum_t),
        total(scale_s * (mean_d + shift_d * sum_s)),
        total(scale_s * (mean_u + shift_s * sum_s)),
        total(
            scale_s
            * (mean_du + shift_s * mean_d + shift_d * mean_u + shift_s * shift_d * sum_s)
        ),
    )


def span_of(v, core, half):
    return pl.ds(pl.multiple_of(v * 2 * half + core * half, 32), half)


def places(core):
    index = lax.axis_index("voc")
    x, y = lax.rem(index, SIDE), lax.div(index, SIDE)
    a = lax.select(core == 0, x, y)
    b = lax.select(core == 0, y, x)

    def place(j, k):
        u = lax.rem(a + SIDE - j, SIDE)
        w = lax.rem(b + SIDE - k, SIDE)
        return lax.select(core == 0, SIDE * w + u, SIDE * u + w)

    return place


def batches(refs, core):
    place = places(core)
    return [
        [(ref, j, place(j, k)) for j in range(SIDE)] for ref, k in zip(refs, (0, 1, 3, 2))
    ]


def logits_of(groups, student_head, teacher_head, core):
    student = jnp.zeros((VOC_DEV, LANES), F32)
    teacher = jnp.zeros((VOC_DEV, LANES), F32)
    squares = jnp.zeros((SPARE, LANES), F32)
    for group in groups:
        head_s = jnp.concatenate(
            [student_head[span_of(v, core, HALF_S), :] for _, _, v in group], axis=0
        )
        head_t = jnp.concatenate(
            [teacher_head[span_of(v, core, HALF_T), :] for _, _, v in group], axis=0
        )
        rows_s = jnp.concatenate([ref[j, :HALF_S, :] for ref, j, _ in group], axis=0)
        rows_t = jnp.concatenate([ref[j, HALF_S:, :] for ref, j, _ in group], axis=0)
        student = student + dot(head_s, rows_s, TN)
        teacher = teacher + dot(head_t, rows_t, TN)
        for ref, j, _ in group:
            squares = squares + ref[j, :SPARE, :].astype(F32)
            squares = squares + ref[j, SPARE : 2 * SPARE, :].astype(F32)
    return student, teacher, squares


def forward_own(
    a, u_first, d_second, student_head, teacher_in,
    student_out, teacher_out, squares_out, teacher_head, zero_out, sem,
):
    copy = pltpu.make_async_copy(teacher_in, teacher_head, sem)
    copy.start()
    zero_out[...] = jnp.zeros((1, LANES), F32)
    copy.wait()
    core = own_core()
    student, teacher, squares = logits_of(batches((a,), core), student_head, teacher_head, core)
    student_out[...] = student
    teacher_out[...] = teacher
    squares_out[...] = squares


def save_rows(refs, out, sems):
    copies = []
    for k, ref in enumerate(refs):
        copies.append(
            pltpu.make_async_copy(
                ref.at[:, pl.ds(0, HALF_S)], out.at[pl.ds(k * SIDE, SIDE)], sems.at[k]
            )
        )
        copies[k].start()
    return copies


def forward_near(
    a, u, d, student_head, teacher_head, student_sum, teacher_sum, squares_sum,
    student_out, teacher_out, squares_out, zero_out, rows_out, row_sems,
):
    core = own_core()
    saved = save_rows((a, u, d), rows_out, row_sems)
    groups = batches((None, u, d), core)[1:]
    student, teacher, squares = logits_of(groups, student_head, teacher_head, core)
    student_out[...] = student + student_sum[...]
    teacher_out[...] = teacher + teacher_sum[...]
    squares_out[...] = squares + squares_sum[...]
    zero_out[...] = jnp.zeros((1, LANES), F32)
    for copy in saved:
        copy.wait()


def forward_mid(
    far, other_a, other_u, other_d, student_head, teacher_head,
    student_sum, teacher_sum, squares_sum, student_out, teacher_out, squares_out,
):
    core = own_core()
    groups = batches((None, None, None, far), core)[3:]
    one = logits_of(groups, student_head, teacher_head, core)
    groups = batches((other_a, other_u, other_d), 1 - core)
    two = logits_of(groups, student_head, teacher_head, 1 - core)
    student_out[...] = one[0] + two[0] + student_sum[...]
    teacher_out[...] = one[1] + two[1] + teacher_sum[...]
    squares_out[...] = one[2] + two[2] + squares_sum[...]


def forward_last(
    other_far, student_head, teacher_head, student_in, teacher_in, squares_in,
    exp_out, ratio_out, stats_out, tops_out, inverse_out,
):
    core = 1 - own_core()
    student, teacher, squares = logits_of(
        batches((None, None, None, other_far), core)[3:], student_head, teacher_head, core
    )
    squares = squares + squares_in[...]
    squares = jnp.where(lane_iota((SPARE, LANES)) >= VALID, squares, 0.0)
    lanes = spare_lanes()
    by_row = sum(dot(part, lanes, NT) for part in split(squares, 3))
    squares = total(jnp.where(spare_rows(), by_row, 0.0))
    inverse = lax.rsqrt(squares / DS + EPSILON)
    inverse_out[...] = inverse
    student = (student + student_in[...]) * inverse
    teacher = teacher + teacher_in[...]

    top_s = jnp.max(student, axis=0, keepdims=True)
    top_t = jnp.max(teacher, axis=0, keepdims=True)
    below = student - top_s
    exp_s = jnp.exp(below)
    below_t = teacher - top_t
    ratio = below - below_t
    exp_out[...] = exp_s
    ratio_out[...] = ratio
    weighted = exp_s * ratio
    stats = stack_rows(
        [
            top_s,
            total(exp_s),
            top_t,
            total(jnp.exp(below_t)),
            total(weighted),
            total(exp_s * below),
            total(weighted * below),
        ]
    )
    tops_out[...] = stats
    for v in range(VOC):
        stats_out[v] = stats


def combine_kernel(stats, out):
    tile = stack_rows(combined(stats))
    for g in range(GROUPS):
        out[g] = tile


def terms_of(groups, student_head, grad, core, out):
    for group in groups:
        head = jnp.concatenate(
            [student_head[span_of(v, core, HALF_S), :] for _, _, v in group], axis=0
        )
        term = dot(head, grad, NN).astype(BF)
        for i, (_, _, v) in enumerate(group):
            out[v] = term[i * HALF_S : (i + 1) * HALF_S]


def backward_one(
    stats, tops, exp_in, ratio_in, weight, inverse, student_head,
    grad_out, scaled_out, away, pull_out, loss_out,
):
    core = 1 - own_core()
    all_s, total_s, all_t, total_t, sum_d, sum_u, sum_du = combined(stats)
    inside = lane_iota((1, LANES)) < VALID
    mean_d = sum_d / total_s
    mean_u = sum_u / total_s
    covariance = sum_du / total_s - mean_d * mean_u
    divergence = mean_d - jnp.log(total_s) + jnp.log(total_t)
    loss_out[...] = jnp.sum(
        jnp.where(inside, weight[...] * divergence, 0.0), axis=1, keepdims=True
    )
    pull_out[...] = weight[...] * covariance * inverse[...] * inverse[...] / DS
    shift_s = tops[0:1, :] - all_s
    shift_t = tops[2:3, :] - all_t
    factor = weight[...] * jnp.exp(shift_s) / total_s
    offset = shift_s - shift_t - mean_d
    grad = jnp.where(inside, factor * exp_in[...] * (ratio_in[...] + offset), 0.0)
    kept = jnp.where(inside, inverse[...], 0.0)
    scaled_out[...] = (grad * kept).astype(BF)
    grad = grad.astype(BF)
    grad_out[...] = grad
    terms_of(batches((None,) * 4, core), student_head, grad, core, away)


def backward_two(*refs):
    grad, student_head, hidden, gain, student_row, inverse, pull = refs[5:12]
    stay, base_out, rows_out, sems = refs[12:]
    saved = save_rows(refs[:5], rows_out, sems)
    core = own_core()
    first = lax.axis_index("grp") * ROWS
    own = lax.broadcasted_iota(jnp.int32, (ROWS, LANES), 0) + first == student_row[...]
    own_rms = jnp.sum(jnp.where(own, inverse[...], 0.0), axis=1, keepdims=True)
    own_pull = jnp.sum(jnp.where(own, pull[...], 0.0), axis=1, keepdims=True)
    base_out[:ROWS] = own_rms * gain[...]
    base_out[ROWS : 2 * ROWS] = hidden[...].astype(F32) * own_pull
    base_out[2 * ROWS :] = jnp.broadcast_to(1.0 / gain[...], (8, LANES))
    terms_of(batches((None,) * 4, core), student_head, grad[...], core, stay)
    for copy in saved:
        copy.wait()


def head_kernel(
    near, rest, scaled_in, out, rows, scaled, blocks, in_sems, scaled_sem, sems
):
    first = pltpu.make_async_copy(scaled_in, scaled, scaled_sem)
    first.start()
    waiting = []
    for n in range(2 * SIDE):
        source, start = (near, n) if n < 3 else (rest, n - 3)
        waiting.append(
            pltpu.make_async_copy(
                source.at[pl.ds(start * SIDE, SIDE)], rows.at[pl.ds(n * SIDE, SIDE)], in_sems.at[n]
            )
        )
        waiting[n].start()
    first.wait()
    copies = []
    for k, core in enumerate((own_core(), 1 - own_core())):
        groups = batches((None,) * 4, core)
        for j in range(SIDE):
            m = k * SIDE + j
            waiting[m].wait()
            block = rows[pl.ds(m * SIDE, SIDE)].reshape(SIDE * HALF_S, LANES)
            result = dot(block, scaled[...], NT).astype(BF)
            for i, (_, _, v) in enumerate(groups[j]):
                n = len(copies)
                blocks[n] = result[i * HALF_S : (i + 1) * HALF_S]
                copies.append(
                    pltpu.make_async_copy(
                        blocks.at[n], out.at[span_of(v, core, HALF_S)], sems.at[n]
                    )
                )
                copies[n].start()
    for copy in copies:
        copy.wait()


def pair_kernel(stay, arrived, out):
    for v in range(VOC):
        out[v] = (stay[v].astype(F32) + arrived[v].astype(F32)).astype(BF)


def send_kernel(pieces, student_row, block, inverse, out):
    summed = pieces[0].astype(F32)
    for v in range(1, VOC):
        summed = summed + pieces[v].astype(F32)
    lane = lane_iota((HALF_S, LANES))
    inside = lane < VALID
    scaled = jnp.where(inside, block[:HALF_S, :].astype(F32) * inverse[...], 0.0)
    gain = jnp.sum(summed * scaled, axis=1, keepdims=True)
    summed = jnp.where(lane == VALID, gain, summed).astype(BF)
    slot = lax.broadcasted_iota(jnp.int32, (SEND, LANES), 0)
    extra = (slot == ROWS) & (lane_iota((SEND, LANES)) == VALID)
    picks = []
    for g in range(GROUPS):
        pick = ((slot < ROWS) & (student_row[...] == slot + g * ROWS)) | extra
        picks.append(jnp.where(pick, 1.0, 0.0).astype(BF))
    result = dot(jnp.concatenate(picks, axis=0), summed, NT).astype(BF)
    for g in range(GROUPS):
        out[g] = result[g * SEND : (g + 1) * SEND]


def finish_kernel(pieces, base, grad_hidden, grad_gain):
    halves = []
    for c in range(2):
        summed = pieces[c].astype(F32)
        for z in range(1, GROUPS // 2):
            summed = summed + pieces[2 * z + c].astype(F32)
        halves.append(summed)
    summed = jnp.concatenate(halves, axis=1)
    grad_gain[...] = summed[ROWS : ROWS + 1] * base[2 * ROWS : 2 * ROWS + 1]
    grad_hidden[...] = (summed[:ROWS] * base[:ROWS] - base[ROWS : 2 * ROWS]).astype(BF)


def shape(dims, dtype):
    return jax.ShapeDtypeStruct(dims, dtype)


def params(mib):
    return pltpu.CompilerParams(vmem_limit_bytes=mib * 1024 * 1024)


def in_hbm(x):
    return pltpu.with_memory_space_constraint(x, pltpu.HBM)


def cost(flops):
    return pl.CostEstimate(flops=flops, bytes_accessed=4 * 1024 * 1024, transcendentals=0)


def exchange(x, axis):
    return lax.all_to_all(x, axis, 0, 0, tiled=True)


HBM = pl.BlockSpec(memory_space=pltpu.HBM)
ANY = pl.BlockSpec(memory_space=pl.ANY)
VMEM = pl.BlockSpec(memory_space=pltpu.VMEM)


def local(
    student_hidden, norm_gain, teacher_hidden, student_head, teacher_head, episode_source, lengths
):
    core = own_core()
    row = shape((1, LANES), F32)
    logits = shape((VOC_DEV, LANES), F32)
    half_rows = shape((VOC, HALF_S, LANES), BF)
    student_row, teacher_row, weight = lane_tables(episode_source, lengths)

    packed = pl.pallas_call(
        pack_kernel,
        out_shape=pltpu.HBM((GROUPS, PACK, HALF_S), BF),
        in_specs=[HBM] * 2,
        out_specs=VMEM,
        scratch_shapes=[
            pltpu.VMEM((ROWS, 2 * HALF_S), BF),
            pltpu.VMEM((ROWS, 2 * HALF_T), BF),
            pltpu.SemaphoreType.DMA((2,)),
        ],
        compiler_params=params(4),
    )(in_hbm(student_hidden), in_hbm(teacher_hidden))
    held = exchange(packed, "grp")

    gain_half = lax.dynamic_slice_in_dim(norm_gain, core * HALF_S, HALF_S)
    gain_high = rounded(gain_half)
    gain_mid = rounded(gain_half - gain_high)
    gain_low = gain_half - gain_high - gain_mid
    gain_parts = jnp.concatenate(
        [jnp.stack([gain_high, gain_mid, gain_low]), jnp.zeros((13, HALF_S), F32)], axis=0
    )
    block, student_row, weight = pl.pallas_call(
        compact_kernel,
        out_shape=(shape((HALF, LANES), BF), shape((1, LANES), jnp.int32), row),
        compiler_params=params(8),
    )(held, student_row, teacher_row, weight, gain_parts)

    one = lax.ppermute(block, BOTH, ring(1, 1))
    three = lax.ppermute(block, BOTH, ring(1, 3))
    two = lax.ppermute(block, BOTH, ring(1, 2))
    first = jnp.stack([block, one])
    second = jnp.stack([two, three])
    u_first = lax.ppermute(first, BOTH, ring(2, 1))
    d_second = lax.ppermute(second, BOTH, ring(2, 3))
    u_second = lax.ppermute(second, BOTH, ring(2, 1))
    d_first = lax.ppermute(first, BOTH, ring(2, 3))
    v = lax.ppermute(u_first, BOTH, ring(2, 1))
    w = lax.ppermute(d_second, BOTH, ring(2, 3))
    a = jnp.concatenate([first, second], axis=0)
    u = jnp.concatenate([u_first, u_second], axis=0)
    d = jnp.concatenate([d_first, d_second], axis=0)
    partial = (logits, logits, shape((SPARE, LANES), F32))

    def sems(count):
        return pltpu.SemaphoreType.DMA((count,))

    *sums, head_t, zero = pl.pallas_call(
        forward_own,
        out_shape=partial + (pltpu.VMEM(teacher_head.shape, BF), row),
        in_specs=[VMEM, ANY, ANY, VMEM, HBM],
        out_specs=(VMEM,) * 5,
        scratch_shapes=[pltpu.SemaphoreType.DMA],
        compiler_params=params(12),
        cost_estimate=cost(SIDE * HALF * VOC_DEV * LANES * 2),
    )(a, u_first, d_second, student_head, in_hbm(teacher_head))
    other = (lax.ppermute(a, "grp", CORE_SWAP),) + tuple(
        lax.ppermute(part + zero.astype(BF), "grp", CORE_SWAP) for part in (u, d)
    )
    *sums, zero, saved_near = pl.pallas_call(
        forward_near,
        out_shape=partial + (row, pltpu.HBM((3 * SIDE, HALF_S, LANES), BF)),
        out_specs=(VMEM,) * 4 + (HBM,),
        scratch_shapes=[sems(3)],
        compiler_params=params(12),
        cost_estimate=cost(2 * SIDE * HALF * VOC_DEV * LANES * 2),
    )(a, u, d, student_head, head_t, *sums)
    far = jnp.concatenate([v, w], axis=0) + zero.astype(BF)
    other_far = lax.ppermute(far, "grp", CORE_SWAP)
    sums = pl.pallas_call(
        forward_mid,
        out_shape=partial,
        compiler_params=params(12),
        cost_estimate=cost(VOC * HALF * VOC_DEV * LANES * 2),
    )(far, *other, student_head, head_t, *sums)
    exp_s, ratio, stats, tops, inverse = pl.pallas_call(
        forward_last,
        out_shape=(
            logits,
            logits,
            shape((VOC, STATS, LANES), F32),
            shape((STATS, LANES), F32),
            row,
        ),
        compiler_params=params(12),
        cost_estimate=cost(SIDE * HALF * VOC_DEV * LANES * 2),
    )(other_far, student_head, head_t, *sums)

    from_voc = exchange(stats, "voc")
    spread = pl.pallas_call(
        combine_kernel, out_shape=shape((GROUPS, STATS, LANES), F32), compiler_params=params(4)
    )(from_voc)
    from_grp = exchange(spread, "grp")

    grad, scaled, away, pull, loss = pl.pallas_call(
        backward_one,
        out_shape=(
            shape((VOC_DEV, LANES), BF),
            pltpu.HBM((VOC_DEV, LANES), BF),
            half_rows,
            row,
            shape((1, 1), F32),
        ),
        out_specs=(VMEM,) * 5,
        compiler_params=params(8),
        cost_estimate=cost(DS * VOC_DEV * LANES),
    )(from_grp, tops, exp_s, ratio, weight, inverse, student_head)
    arrived = lax.ppermute(away, "grp", CORE_SWAP)
    stay, base, saved_rest = pl.pallas_call(
        backward_two,
        out_shape=(
            half_rows,
            shape((2 * ROWS + 8, LANES), F32),
            pltpu.HBM((5 * SIDE, HALF_S, LANES), BF),
        ),
        out_specs=(VMEM, VMEM, HBM),
        scratch_shapes=[sems(5)],
        compiler_params=params(8),
        cost_estimate=cost(DS * VOC_DEV * LANES),
    )(
        far, *other, other_far, grad, student_head,
        student_hidden, norm_gain[None], student_row, inverse, pull,
    )
    pair = pl.pallas_call(pair_kernel, out_shape=half_rows, compiler_params=params(8))(
        stay, arrived
    )
    pieces = exchange(pair, "voc")
    grad_head = pl.pallas_call(
        head_kernel,
        out_shape=shape((DS, VOC_DEV), BF),
        in_specs=[HBM] * 3,
        out_specs=HBM,
        scratch_shapes=[
            pltpu.VMEM((2 * VOC, HALF_S, LANES), BF),
            pltpu.VMEM((VOC_DEV, LANES), BF),
            pltpu.VMEM((2 * VOC, HALF_S, VOC_DEV), BF),
            pltpu.SemaphoreType.DMA((2 * SIDE,)),
            pltpu.SemaphoreType.DMA,
            pltpu.SemaphoreType.DMA((2 * VOC,)),
        ],
        compiler_params=params(12),
        cost_estimate=cost(DS * VOC_DEV * LANES * 2),
    )(in_hbm(saved_near), in_hbm(saved_rest), in_hbm(scaled))
    outgoing = pl.pallas_call(
        send_kernel,
        out_shape=pltpu.HBM((GROUPS, SEND, HALF_S), BF),
        out_specs=VMEM,
        compiler_params=params(8),
    )(pieces, student_row, block, inverse)
    pieces = exchange(outgoing, "grp")
    grad_hidden, grad_gain = pl.pallas_call(
        finish_kernel,
        out_shape=(shape((ROWS, 2 * HALF_S), BF), row),
        compiler_params=params(4),
    )(pieces, base)
    return (loss.reshape(()), grad_hidden, grad_gain.reshape(-1), grad_head)


def solution(mesh):
    placed = (
        P("grp", "voc"),
        P("voc"),
        P("grp", "voc"),
        P(None, ("grp", "voc")),
        P(None, ("grp", "voc")),
        P(),
        P(),
    )
    return jax.shard_map(
        local,
        mesh=mesh,
        in_specs=placed,
        out_specs=(P(), P("grp", "voc"), P("voc"), P(None, ("grp", "voc"))),
        check_vma=False,
    )
```

```python
import jax
import jax.numpy as jnp
from jax import lax
from jax.experimental import pallas as pl
from jax.experimental.pallas import tpu as pltpu
from jax.sharding import PartitionSpec as P

DS = 4096
SEQ = 2
VALID = 240
LANES = 256
EPSILON = 1e-06
GROUPS = 16
VOC = 16
ROWS = 24
HALF_S = 128
HALF_T = 160
HALF = HALF_S + HALF_T
VOC_DEV = 384
STATS = 8
SEND = 32
PACK = 56
TAIL = 32
PER = 4
SPARE = 16
SIDE = 4
BF = jnp.bfloat16
F32 = jnp.float32
CORE_SWAP = [(i, i ^ 1) for i in range(GROUPS)]
BOTH = ("grp", "voc")


def ring(phase, step):
    pairs = []
    for g in range(GROUPS):
        for v in range(VOC):
            y, x = divmod(v, SIDE)
            if (g % 2 == 0) == (phase == 1):
                x = (x + step) % SIDE
            else:
                y = (y + step) % SIDE
            pairs.append((g * VOC + v, g * VOC + y * SIDE + x))
    return pairs


TN = (((0,), (0,)), ((), ()))
NT = (((1,), (1,)), ((), ()))
NN = (((1,), (0,)), ((), ()))


def dot(a, b, dims):
    return lax.dot_general(a, b, dims, preferred_element_type=F32)


def lane_tables(source, lengths):
    episodes = lengths.shape[1]
    here = lax.broadcasted_iota(jnp.int32, (episodes, episodes), 0)
    there = lane_iota((episodes, episodes))

    def column(mask, values):
        return jnp.sum(jnp.where(mask, values, 0.0), axis=1, keepdims=True)

    lengths = lengths.astype(F32)
    two = jnp.where(lengths == 2.0, 1.0, 0.0)
    rank = column(there < here, two)
    two = column(here == there, two)
    source = column(here == there, source.astype(F32))
    lengths = column(here == there, lengths)
    lane = lane_iota((episodes, LANES)).astype(F32)
    number = lax.broadcasted_iota(jnp.int32, (episodes, LANES), 0).astype(F32)
    pick = (lane == number) | ((two == 1.0) & (lane == episodes + rank))

    def of_lane(values):
        return jnp.sum(jnp.where(pick, values, 0.0), axis=0, keepdims=True)

    lane = lane_iota((1, LANES))
    inside = lane < VALID
    position = jnp.where(lane >= episodes, 1.0, 0.0)
    student_row = jnp.where(inside, of_lane(number) * SEQ + position, -1.0)
    teacher_row = jnp.where(inside, of_lane(source) * SEQ + position, -1.0)
    weight = jnp.where(inside, 1.0 / jnp.maximum(of_lane(lengths), 1.0), 0.0)
    return student_row.astype(jnp.int32), teacher_row.astype(jnp.int32), weight


def own_core():
    return lax.rem(lax.axis_index("grp"), 2)


def lane_iota(shape):
    return lax.broadcasted_iota(jnp.int32, shape, len(shape) - 1)


def pack_kernel(
    student_in, teacher_in, source_in, lengths_in, gain_in,
    out, student_row, teacher_row, weight, gain_out,
    student, teacher, source, lengths, gain, sems,
):
    pairs = (
        (source_in, source),
        (lengths_in, lengths),
        (gain_in, gain),
        (student_in, student),
        (teacher_in, teacher),
    )
    copies = []
    for n, (place, held) in enumerate(pairs):
        copies.append(pltpu.make_async_copy(place, held, sems.at[n]))
        copies[n].start()
    copies[0].wait()
    copies[1].wait()
    student_row[...], teacher_row[...], weight[...] = lane_tables(source[...], lengths[...])
    copies[2].wait()
    row = lax.broadcasted_iota(jnp.int32, (16, HALF_S), 0)
    own_gain = jnp.where(own_core() == 0, gain[:, :HALF_S], gain[:, HALF_S:])
    spread = jnp.zeros((16, HALF_S), F32)
    for k, part in enumerate(split(own_gain, 3)):
        spread = jnp.where(row == k, part.astype(F32), spread)
    gain_out[...] = spread
    copies[3].wait()
    copies[4].wait()
    for c in range(2):
        rows = teacher[:, c * HALF_T : (c + 1) * HALF_T].astype(F32)
        tail = rows[:, HALF_S:]
        tail = jnp.concatenate(
            [tail[:8], tail[8:16], tail[16:24], jnp.zeros((8, TAIL), F32)], axis=1
        )
        whole = jnp.concatenate(
            [student[:, c * HALF_S : (c + 1) * HALF_S].astype(F32), rows[:, :HALF_S], tail], axis=0
        )
        whole = whole.astype(BF)
        for z in range(GROUPS // 2):
            out[2 * z + c] = whole


def spare_lanes():
    source = lax.broadcasted_iota(jnp.int32, (LANES, LANES), 0)
    lane = lane_iota((LANES, LANES))
    return jnp.where(lane == VALID + lax.rem(source, SPARE), 1.0, 0.0).astype(BF)


def spare_rows():
    row = lax.broadcasted_iota(jnp.int32, (SPARE, LANES), 0)
    return lax.div(lane_iota((SPARE, LANES)), SPARE) == row


def split(x, parts):
    out = []
    for _ in range(parts):
        out.append(x.astype(BF))
        x = x - out[-1].astype(F32)
    return out


def compact_kernel(held, student_row, teacher_row, gain, out):
    blocks = [held[g].astype(F32) for g in range(GROUPS)]
    rows_s = jnp.concatenate([block[:ROWS] for block in blocks], axis=0).astype(BF)
    rows_t = jnp.concatenate([block[ROWS : 2 * ROWS] for block in blocks], axis=0).astype(BF)
    tails = jnp.concatenate([block[2 * ROWS :] for block in blocks], axis=0).astype(BF)
    ids = lax.broadcasted_iota(jnp.int32, (GROUPS * ROWS, LANES), 0)
    pick_s = jnp.where(ids == student_row[...], 1.0, 0.0).astype(BF)
    pick_t = jnp.where(ids == teacher_row[...], 1.0, 0.0).astype(BF)
    block_s = dot(rows_s, pick_s, TN)
    block_t = dot(rows_t, pick_t, TN).astype(BF)
    short = lax.broadcasted_iota(jnp.int32, (GROUPS * 8, LANES), 0)
    short = lax.div(short, 8) * ROWS + lax.rem(short, 8)
    tail = jnp.zeros((TAIL, LANES), F32)
    for k in range(3):
        pick = jnp.where(short + 8 * k == teacher_row[...], 1.0, 0.0).astype(BF)
        tail = tail + dot(tails, pick, TN)[k * TAIL : (k + 1) * TAIL]
    spread_gain = dot(gain[...].astype(BF), jnp.ones((16, LANES), BF), TN)
    squares = jnp.sum(block_s * block_s, axis=0, keepdims=True)
    parts = split(jnp.where(spare_rows(), squares, 0.0), 2)
    lanes = spare_lanes()
    spare = jnp.concatenate([dot(part, lanes, NN) for part in parts], axis=0)
    block_s = block_s * spread_gain
    block_s = jnp.concatenate([block_s[: 2 * SPARE] + spare, block_s[2 * SPARE :]], axis=0)
    out[:HALF_S, :] = block_s.astype(BF)
    out[HALF_S : 2 * HALF_S, :] = block_t
    out[2 * HALF_S :, :] = tail.astype(BF)


def stack_rows(values):
    row = lax.broadcasted_iota(jnp.int32, (STATS, LANES), 0)
    out = jnp.zeros((STATS, LANES), F32)
    for k, value in enumerate(values):
        out = jnp.where(row == k, value, out)
    return out


def total(x):
    return jnp.sum(x, axis=0, keepdims=True)


def combined(stats):
    top_s, sum_s, top_t, sum_t, mean_d, mean_u, mean_du = [stats[:, k, :] for k in range(7)]
    all_s = jnp.max(top_s, axis=0, keepdims=True)
    all_t = jnp.max(top_t, axis=0, keepdims=True)
    shift_s = top_s - all_s
    shift_t = top_t - all_t
    scale_s = jnp.exp(shift_s)
    scale_t = jnp.exp(shift_t)
    shift_d = shift_s - shift_t
    return (
        all_s,
        total(scale_s * sum_s),
        all_t,
        total(scale_t * sum_t),
        total(scale_s * (mean_d + shift_d * sum_s)),
        total(scale_s * (mean_u + shift_s * sum_s)),
        total(
            scale_s
            * (mean_du + shift_s * mean_d + shift_d * mean_u + shift_s * shift_d * sum_s)
        ),
    )


def span_of(v, core, half):
    return pl.ds(pl.multiple_of(v * 2 * half + core * half, 32), half)


def places(core):
    index = lax.axis_index("voc")
    x, y = lax.rem(index, SIDE), lax.div(index, SIDE)
    a = lax.select(core == 0, x, y)
    b = lax.select(core == 0, y, x)

    def place(j, k):
        u = lax.rem(a + SIDE - j, SIDE)
        w = lax.rem(b + SIDE - k, SIDE)
        return lax.select(core == 0, SIDE * w + u, SIDE * u + w)

    return place


def batches(refs, core):
    place = places(core)
    return [
        [(ref, j, place(j, k)) for j in range(SIDE)] for ref, k in zip(refs, (0, 1, 3, 2))
    ]


def logits_of(groups, student_head, teacher_head, core):
    student = jnp.zeros((VOC_DEV, LANES), F32)
    teacher = jnp.zeros((VOC_DEV, LANES), F32)
    squares = jnp.zeros((SPARE, LANES), F32)
    for group in groups:
        head_s = jnp.concatenate(
            [student_head[span_of(v, core, HALF_S), :] for _, _, v in group], axis=0
        )
        head_t = jnp.concatenate(
            [teacher_head[span_of(v, core, HALF_T), :] for _, _, v in group], axis=0
        )
        rows_s = jnp.concatenate([ref[j, :HALF_S, :] for ref, j, _ in group], axis=0)
        rows_t = jnp.concatenate([ref[j, HALF_S:, :] for ref, j, _ in group], axis=0)
        student = student + dot(head_s, rows_s, TN)
        teacher = teacher + dot(head_t, rows_t, TN)
        for ref, j, _ in group:
            squares = squares + ref[j, :SPARE, :].astype(F32)
            squares = squares + ref[j, SPARE : 2 * SPARE, :].astype(F32)
    return student, teacher, squares


def forward_own(
    a, u_first, d_second, student_head, teacher_in,
    student_out, teacher_out, squares_out, teacher_head, zero_out, sem,
):
    copy = pltpu.make_async_copy(teacher_in, teacher_head, sem)
    copy.start()
    zero_out[...] = jnp.zeros((1, LANES), F32)
    copy.wait()
    core = own_core()
    student, teacher, squares = logits_of(batches((a,), core), student_head, teacher_head, core)
    student_out[...] = student
    teacher_out[...] = teacher
    squares_out[...] = squares


def forward_near(
    u, d, student_head, teacher_head, student_sum, teacher_sum, squares_sum,
    student_out, teacher_out, squares_out, zero_out,
):
    core = own_core()
    groups = batches((None, u, d), core)[1:]
    student, teacher, squares = logits_of(groups, student_head, teacher_head, core)
    student_out[...] = student + student_sum[...]
    teacher_out[...] = teacher + teacher_sum[...]
    squares_out[...] = squares + squares_sum[...]
    zero_out[...] = jnp.zeros((1, LANES), F32)


def forward_mid(
    far, other_a, other_u, other_d, student_head, teacher_head,
    student_sum, teacher_sum, squares_sum, student_out, teacher_out, squares_out,
):
    core = own_core()
    groups = batches((None, None, None, far), core)[3:]
    one = logits_of(groups, student_head, teacher_head, core)
    groups = batches((other_a, other_u, other_d), 1 - core)
    two = logits_of(groups, student_head, teacher_head, 1 - core)
    student_out[...] = one[0] + two[0] + student_sum[...]
    teacher_out[...] = one[1] + two[1] + teacher_sum[...]
    squares_out[...] = one[2] + two[2] + squares_sum[...]


def forward_last(
    other_far, student_head, teacher_head, student_in, teacher_in, squares_in,
    exp_out, ratio_out, stats_out, tops_out, inverse_out,
):
    core = 1 - own_core()
    student, teacher, squares = logits_of(
        batches((None, None, None, other_far), core)[3:], student_head, teacher_head, core
    )
    squares = squares + squares_in[...]
    squares = jnp.where(lane_iota((SPARE, LANES)) >= VALID, squares, 0.0)
    lanes = spare_lanes()
    by_row = sum(dot(part, lanes, NT) for part in split(squares, 3))
    squares = total(jnp.where(spare_rows(), by_row, 0.0))
    inverse = lax.rsqrt(squares / DS + EPSILON)
    inverse_out[...] = inverse
    student = (student + student_in[...]) * inverse
    teacher = teacher + teacher_in[...]

    top_s = jnp.max(student, axis=0, keepdims=True)
    top_t = jnp.max(teacher, axis=0, keepdims=True)
    below = student - top_s
    exp_s = jnp.exp(below)
    below_t = teacher - top_t
    ratio = below - below_t
    exp_out[...] = exp_s
    ratio_out[...] = ratio
    weighted = exp_s * ratio
    stats = stack_rows(
        [
            top_s,
            total(exp_s),
            top_t,
            total(jnp.exp(below_t)),
            total(weighted),
            total(exp_s * below),
            total(weighted * below),
        ]
    )
    tops_out[...] = stats
    for v in range(VOC):
        stats_out[v] = stats


def combine_kernel(stats, out):
    tile = stack_rows(combined(stats))
    for g in range(GROUPS):
        out[g] = tile


def terms_of(groups, student_head, grad, core, out):
    for group in groups:
        head = jnp.concatenate(
            [student_head[span_of(v, core, HALF_S), :] for _, _, v in group], axis=0
        )
        term = dot(head, grad, NN).astype(BF)
        for i, (_, _, v) in enumerate(group):
            out[v] = term[i * HALF_S : (i + 1) * HALF_S]


def backward_one(
    stats, tops, exp_in, ratio_in, weight, inverse, student_head,
    grad_out, scaled_out, away, pull_out, loss_out,
):
    core = 1 - own_core()
    all_s, total_s, all_t, total_t, sum_d, sum_u, sum_du = combined(stats)
    inside = lane_iota((1, LANES)) < VALID
    mean_d = sum_d / total_s
    mean_u = sum_u / total_s
    covariance = sum_du / total_s - mean_d * mean_u
    divergence = mean_d - jnp.log(total_s) + jnp.log(total_t)
    loss_out[...] = jnp.sum(
        jnp.where(inside, weight[...] * divergence, 0.0), axis=1, keepdims=True
    )
    pull_out[...] = weight[...] * covariance * inverse[...] * inverse[...] / DS
    shift_s = tops[0:1, :] - all_s
    shift_t = tops[2:3, :] - all_t
    factor = weight[...] * jnp.exp(shift_s) / total_s
    offset = shift_s - shift_t - mean_d
    grad = jnp.where(inside, factor * exp_in[...] * (ratio_in[...] + offset), 0.0)
    kept = jnp.where(inside, inverse[...], 0.0)
    scaled_out[...] = (grad * kept).astype(BF)
    grad = grad.astype(BF)
    grad_out[...] = grad
    terms_of(batches((None,) * 4, core), student_head, grad, core, away)


def backward_two(
    grad, student_head, hidden, gain, student_row, inverse, pull, stay, base_out
):
    core = own_core()
    first = lax.axis_index("grp") * ROWS
    own = lax.broadcasted_iota(jnp.int32, (ROWS, LANES), 0) + first == student_row[...]
    own_rms = jnp.sum(jnp.where(own, inverse[...], 0.0), axis=1, keepdims=True)
    own_pull = jnp.sum(jnp.where(own, pull[...], 0.0), axis=1, keepdims=True)
    base_out[:ROWS] = own_rms * gain[...]
    base_out[ROWS : 2 * ROWS] = hidden[...].astype(F32) * own_pull
    base_out[2 * ROWS :] = jnp.broadcast_to(1.0 / gain[...], (8, LANES))
    terms_of(batches((None,) * 4, core), student_head, grad[...], core, stay)


def head_kernel(*refs):
    scaled, out, zero_out, blocks, sems = refs[8:]
    zero_out[...] = jnp.zeros((1, LANES), F32)
    copies = []
    for k, core in enumerate((own_core(), 1 - own_core())):
        for group in batches(refs[SIDE * k : SIDE * k + SIDE], core):
            block = jnp.concatenate([ref[j, :HALF_S, :] for ref, j, _ in group], axis=0)
            result = dot(block, scaled[...], NT).astype(BF)
            for i, (_, _, v) in enumerate(group):
                n = len(copies)
                blocks[n] = result[i * HALF_S : (i + 1) * HALF_S]
                copies.append(
                    pltpu.make_async_copy(
                        blocks.at[n], out.at[span_of(v, core, HALF_S)], sems.at[n]
                    )
                )
                copies[n].start()
    for copy in copies:
        copy.wait()


def pair_kernel(stay, arrived, zero, out):
    for v in range(VOC):
        out[v] = (stay[v].astype(F32) + arrived[v].astype(F32)).astype(BF)


def send_kernel(pieces, student_row, block, inverse, out):
    summed = pieces[0].astype(F32)
    for v in range(1, VOC):
        summed = summed + pieces[v].astype(F32)
    lane = lane_iota((HALF_S, LANES))
    inside = lane < VALID
    scaled = jnp.where(inside, block[:HALF_S, :].astype(F32) * inverse[...], 0.0)
    gain = jnp.sum(summed * scaled, axis=1, keepdims=True)
    summed = jnp.where(lane == VALID, gain, summed).astype(BF)
    slot = lax.broadcasted_iota(jnp.int32, (SEND, LANES), 0)
    extra = (slot == ROWS) & (lane_iota((SEND, LANES)) == VALID)
    picks = []
    for g in range(GROUPS):
        pick = ((slot < ROWS) & (student_row[...] == slot + g * ROWS)) | extra
        picks.append(jnp.where(pick, 1.0, 0.0).astype(BF))
    result = dot(jnp.concatenate(picks, axis=0), summed, NT).astype(BF)
    for g in range(GROUPS):
        out[g] = result[g * SEND : (g + 1) * SEND]


def finish_kernel(pieces, base, grad_hidden, grad_gain):
    halves = []
    for c in range(2):
        summed = pieces[c].astype(F32)
        for z in range(1, GROUPS // 2):
            summed = summed + pieces[2 * z + c].astype(F32)
        halves.append(summed)
    summed = jnp.concatenate(halves, axis=1)
    grad_gain[...] = summed[ROWS : ROWS + 1] * base[2 * ROWS : 2 * ROWS + 1]
    grad_hidden[...] = (summed[:ROWS] * base[:ROWS] - base[ROWS : 2 * ROWS]).astype(BF)


def shape(dims, dtype):
    return jax.ShapeDtypeStruct(dims, dtype)


def params(mib):
    return pltpu.CompilerParams(vmem_limit_bytes=mib * 1024 * 1024)


def in_hbm(x):
    return pltpu.with_memory_space_constraint(x, pltpu.HBM)


def cost(flops):
    return pl.CostEstimate(flops=flops, bytes_accessed=4 * 1024 * 1024, transcendentals=0)


def exchange(x, axis):
    return lax.all_to_all(x, axis, 0, 0, tiled=True)


HBM = pl.BlockSpec(memory_space=pltpu.HBM)
ANY = pl.BlockSpec(memory_space=pl.ANY)
VMEM = pl.BlockSpec(memory_space=pltpu.VMEM)


def local(
    student_hidden, norm_gain, teacher_hidden, student_head, teacher_head, episode_source, lengths
):
    row = shape((1, LANES), F32)
    logits = shape((VOC_DEV, LANES), F32)
    half_rows = shape((VOC, HALF_S, LANES), BF)

    table = shape((1, LANES), jnp.int32)
    episodes = lengths.shape[0]
    packed, student_row, teacher_row, weight, gain_parts = pl.pallas_call(
        pack_kernel,
        out_shape=(
            shape((GROUPS, PACK, HALF_S), BF), table, table, row, shape((16, HALF_S), F32)
        ),
        in_specs=[HBM] * 5,
        out_specs=(VMEM,) * 5,
        scratch_shapes=[
            pltpu.VMEM((ROWS, 2 * HALF_S), BF),
            pltpu.VMEM((ROWS, 2 * HALF_T), BF),
            pltpu.VMEM((1, episodes), jnp.int32),
            pltpu.VMEM((1, episodes), jnp.int32),
            pltpu.VMEM((1, 2 * HALF_S), F32),
            pltpu.SemaphoreType.DMA((5,)),
        ],
        compiler_params=params(4),
    )(
        in_hbm(student_hidden), in_hbm(teacher_hidden),
        in_hbm(episode_source[None]), in_hbm(lengths[None]), in_hbm(norm_gain[None]),
    )
    held = exchange(packed, "grp")
    block = pl.pallas_call(
        compact_kernel, out_shape=shape((HALF, LANES), BF), compiler_params=params(8)
    )(held, student_row, teacher_row, gain_parts)

    one = lax.ppermute(block, BOTH, ring(1, 1))
    three = lax.ppermute(block, BOTH, ring(1, 3))
    two = lax.ppermute(block, BOTH, ring(1, 2))
    first = jnp.stack([block, one])
    second = jnp.stack([two, three])
    u_first = lax.ppermute(first, BOTH, ring(2, 1))
    d_second = lax.ppermute(second, BOTH, ring(2, 3))
    u_second = lax.ppermute(second, BOTH, ring(2, 1))
    d_first = lax.ppermute(first, BOTH, ring(2, 3))
    v = lax.ppermute(u_first, BOTH, ring(2, 1))
    w = lax.ppermute(d_second, BOTH, ring(2, 3))
    a = jnp.concatenate([first, second], axis=0)
    u = jnp.concatenate([u_first, u_second], axis=0)
    d = jnp.concatenate([d_first, d_second], axis=0)
    partial = (logits, logits, shape((SPARE, LANES), F32))

    def sems(count):
        return pltpu.SemaphoreType.DMA((count,))

    *sums, head_t, zero = pl.pallas_call(
        forward_own,
        out_shape=partial + (pltpu.VMEM(teacher_head.shape, BF), row),
        in_specs=[VMEM, ANY, ANY, VMEM, HBM],
        out_specs=(VMEM,) * 5,
        scratch_shapes=[pltpu.SemaphoreType.DMA],
        compiler_params=params(12),
        cost_estimate=cost(SIDE * HALF * VOC_DEV * LANES * 2),
    )(a, u_first, d_second, student_head, in_hbm(teacher_head))
    other = (lax.ppermute(a, "grp", CORE_SWAP),) + tuple(
        lax.ppermute(part + zero.astype(BF), "grp", CORE_SWAP) for part in (u, d)
    )
    *sums, zero = pl.pallas_call(
        forward_near,
        out_shape=partial + (row,),
        compiler_params=params(12),
        cost_estimate=cost(2 * SIDE * HALF * VOC_DEV * LANES * 2),
    )(u, d, student_head, head_t, *sums)
    far = jnp.concatenate([v, w], axis=0) + zero.astype(BF)
    other_far = lax.ppermute(far, "grp", CORE_SWAP)
    sums = pl.pallas_call(
        forward_mid,
        out_shape=partial,
        compiler_params=params(12),
        cost_estimate=cost(VOC * HALF * VOC_DEV * LANES * 2),
    )(far, *other, student_head, head_t, *sums)
    exp_s, ratio, stats, tops, inverse = pl.pallas_call(
        forward_last,
        out_shape=(
            logits,
            logits,
            shape((VOC, STATS, LANES), F32),
            shape((STATS, LANES), F32),
            row,
        ),
        compiler_params=params(12),
        cost_estimate=cost(SIDE * HALF * VOC_DEV * LANES * 2),
    )(other_far, student_head, head_t, *sums)

    from_voc = exchange(stats, "voc")
    spread = pl.pallas_call(
        combine_kernel, out_shape=shape((GROUPS, STATS, LANES), F32), compiler_params=params(4)
    )(from_voc)
    from_grp = exchange(spread, "grp")

    grad, scaled, away, pull, loss = pl.pallas_call(
        backward_one,
        out_shape=(
            shape((VOC_DEV, LANES), BF),
            shape((VOC_DEV, LANES), BF),
            half_rows,
            row,
            shape((1, 1), F32),
        ),
        out_specs=(VMEM,) * 5,
        compiler_params=params(8),
        cost_estimate=cost(DS * VOC_DEV * LANES),
    )(from_grp, tops, exp_s, ratio, weight, inverse, student_head)
    arrived = lax.ppermute(away, "grp", CORE_SWAP)
    stay, base = pl.pallas_call(
        backward_two,
        out_shape=(half_rows, shape((2 * ROWS + 8, LANES), F32)),
        compiler_params=params(8),
        cost_estimate=cost(DS * VOC_DEV * LANES),
    )(grad, student_head, student_hidden, norm_gain[None], student_row, inverse, pull)
    grad_head, zero = pl.pallas_call(
        head_kernel,
        out_shape=(shape((DS, VOC_DEV), BF), row),
        out_specs=(HBM, VMEM),
        scratch_shapes=[pltpu.VMEM((2 * VOC, HALF_S, VOC_DEV), BF), sems(2 * VOC)],
        compiler_params=params(12),
        cost_estimate=cost(DS * VOC_DEV * LANES * 2),
    )(a, u, d, far, *other, other_far, scaled)
    pair = pl.pallas_call(pair_kernel, out_shape=half_rows, compiler_params=params(8))(
        stay, arrived, zero
    )
    pieces = exchange(pair, "voc")
    outgoing = pl.pallas_call(
        send_kernel,
        out_shape=shape((GROUPS, SEND, HALF_S), BF),
        compiler_params=params(8),
    )(pieces, student_row, block, inverse)
    pieces = exchange(outgoing, "grp")
    grad_hidden, grad_gain = pl.pallas_call(
        finish_kernel,
        out_shape=(shape((ROWS, 2 * HALF_S), BF), row),
        compiler_params=params(4),
    )(pieces, base)
    return (loss.reshape(()), grad_hidden, grad_gain.reshape(-1), grad_head)


def solution(mesh):
    placed = (
        P("grp", "voc"),
        P("voc"),
        P("grp", "voc"),
        P(None, ("grp", "voc")),
        P(None, ("grp", "voc")),
        P(),
        P(),
    )
    return jax.shard_map(
        local,
        mesh=mesh,
        in_specs=placed,
        out_specs=(P(), P("grp", "voc"), P("voc"), P(None, ("grp", "voc"))),
        check_vma=False,
    )
```

```python
import jax
import jax.numpy as jnp
from jax import lax
from jax.experimental import pallas as pl
from jax.experimental.pallas import tpu as pltpu
from jax.sharding import PartitionSpec as P

DS = 4096
SEQ = 2
VALID = 240
LANES = 256
EPSILON = 1e-06
LARGEST = 3e38
GROUPS = 16
VOC = 16
ROWS = 24
HALF_S = 128
HALF_T = 160
HALF = HALF_S + HALF_T
VOC_DEV = 384
STATS = 8
SEND = 32
PACK = 56
TAIL = 32
PER = 4
SPARE = 16
SIDE = 4
BF = jnp.bfloat16
F32 = jnp.float32
CORE_SWAP = [(i, i ^ 1) for i in range(GROUPS)]
BOTH = ("grp", "voc")


def ring(phase, step):
    pairs = []
    for g in range(GROUPS):
        for v in range(VOC):
            y, x = divmod(v, SIDE)
            if (g % 2 == 0) == (phase == 1):
                x = (x + step) % SIDE
            else:
                y = (y + step) % SIDE
            pairs.append((g * VOC + v, g * VOC + y * SIDE + x))
    return pairs


TN = (((0,), (0,)), ((), ()))
NT = (((1,), (1,)), ((), ()))
NN = (((1,), (0,)), ((), ()))


def dot(a, b, dims):
    return lax.dot_general(a, b, dims, preferred_element_type=F32)


def lane_tables(source, lengths):
    episodes = lengths.shape[1]
    here = lax.broadcasted_iota(jnp.int32, (episodes, episodes), 0)
    there = lane_iota((episodes, episodes))

    def column(mask, values):
        return jnp.sum(jnp.where(mask, values, 0.0), axis=1, keepdims=True)

    lengths = lengths.astype(F32)
    two = jnp.where(lengths == 2.0, 1.0, 0.0)
    rank = column(there < here, two)
    two = column(here == there, two)
    source = column(here == there, source.astype(F32))
    lengths = column(here == there, lengths)
    lane = lane_iota((episodes, LANES)).astype(F32)
    number = lax.broadcasted_iota(jnp.int32, (episodes, LANES), 0).astype(F32)
    pick = (lane == number) | ((two == 1.0) & (lane == episodes + rank))

    def of_lane(values):
        return jnp.sum(jnp.where(pick, values, 0.0), axis=0, keepdims=True)

    lane = lane_iota((1, LANES))
    inside = lane < VALID
    position = jnp.where(lane >= episodes, 1.0, 0.0)
    student_row = jnp.where(inside, of_lane(number) * SEQ + position, -1.0)
    teacher_row = jnp.where(inside, of_lane(source) * SEQ + position, -1.0)
    weight = jnp.where(inside, 1.0 / jnp.maximum(of_lane(lengths), 1.0), 0.0)
    return student_row.astype(jnp.int32), teacher_row.astype(jnp.int32), weight


def own_core():
    return lax.rem(lax.axis_index("grp"), 2)


def lane_iota(shape):
    return lax.broadcasted_iota(jnp.int32, shape, len(shape) - 1)


def pack_kernel(
    student_in, teacher_in, source_in, lengths_in, gain_in,
    out, student_row, teacher_row, weight, gain_out,
    student, teacher, source, lengths, gain, sems,
):
    pairs = (
        (source_in, source),
        (lengths_in, lengths),
        (gain_in, gain),
        (student_in, student),
        (teacher_in, teacher),
    )
    copies = []
    for n, (place, held) in enumerate(pairs):
        copies.append(pltpu.make_async_copy(place, held, sems.at[n]))
        copies[n].start()
    copies[0].wait()
    copies[1].wait()
    student_row[...], teacher_row[...], weight[...] = lane_tables(source[...], lengths[...])
    copies[2].wait()
    row = lax.broadcasted_iota(jnp.int32, (16, HALF_S), 0)
    own_gain = jnp.where(own_core() == 0, gain[:, :HALF_S], gain[:, HALF_S:])
    spread = jnp.zeros((16, HALF_S), F32)
    for k, part in enumerate(split(own_gain, 3)):
        spread = jnp.where(row == k, part.astype(F32), spread)
    gain_out[...] = spread
    copies[3].wait()
    copies[4].wait()
    for c in range(2):
        rows = teacher[:, c * HALF_T : (c + 1) * HALF_T].astype(F32)
        tail = rows[:, HALF_S:]
        tail = jnp.concatenate(
            [tail[:8], tail[8:16], tail[16:24], jnp.zeros((8, TAIL), F32)], axis=1
        )
        whole = jnp.concatenate(
            [student[:, c * HALF_S : (c + 1) * HALF_S].astype(F32), rows[:, :HALF_S], tail], axis=0
        )
        whole = whole.astype(BF)
        for z in range(GROUPS // 2):
            out[2 * z + c] = whole


def spare_lanes():
    source = lax.broadcasted_iota(jnp.int32, (LANES, LANES), 0)
    lane = lane_iota((LANES, LANES))
    return jnp.where(lane == VALID + lax.rem(source, SPARE), 1.0, 0.0).astype(BF)


def spare_rows():
    row = lax.broadcasted_iota(jnp.int32, (SPARE, LANES), 0)
    return lax.div(lane_iota((SPARE, LANES)), SPARE) == row


def split(x, parts):
    out = []
    for _ in range(parts):
        out.append(x.astype(BF))
        x = x - out[-1].astype(F32)
    return out


def compact_kernel(held, student_row, teacher_row, gain, out):
    blocks = [held[g].astype(F32) for g in range(GROUPS)]
    rows_s = jnp.concatenate([block[:ROWS] for block in blocks], axis=0).astype(BF)
    rows_t = jnp.concatenate([block[ROWS : 2 * ROWS] for block in blocks], axis=0).astype(BF)
    tails = jnp.concatenate([block[2 * ROWS :] for block in blocks], axis=0).astype(BF)
    ids = lax.broadcasted_iota(jnp.int32, (GROUPS * ROWS, LANES), 0)
    pick_s = jnp.where(ids == student_row[...], 1.0, 0.0).astype(BF)
    pick_t = jnp.where(ids == teacher_row[...], 1.0, 0.0).astype(BF)
    block_s = dot(rows_s, pick_s, TN)
    block_t = dot(rows_t, pick_t, TN).astype(BF)
    short = lax.broadcasted_iota(jnp.int32, (GROUPS * 8, LANES), 0)
    short = lax.div(short, 8) * ROWS + lax.rem(short, 8)
    tail = jnp.zeros((TAIL, LANES), F32)
    for k in range(3):
        pick = jnp.where(short + 8 * k == teacher_row[...], 1.0, 0.0).astype(BF)
        tail = tail + dot(tails, pick, TN)[k * TAIL : (k + 1) * TAIL]
    spread_gain = dot(gain[...].astype(BF), jnp.ones((16, LANES), BF), TN)
    squares = jnp.minimum(jnp.sum(block_s * block_s, axis=0, keepdims=True), LARGEST)
    parts = split(jnp.where(spare_rows(), squares, 0.0), 2)
    lanes = spare_lanes()
    spare = jnp.concatenate([dot(part, lanes, NN) for part in parts], axis=0)
    block_s = block_s * spread_gain
    block_s = jnp.concatenate([block_s[: 2 * SPARE] + spare, block_s[2 * SPARE :]], axis=0)
    out[:HALF_S, :] = block_s.astype(BF)
    out[HALF_S : 2 * HALF_S, :] = block_t
    out[2 * HALF_S :, :] = tail.astype(BF)


def stack_rows(values):
    row = lax.broadcasted_iota(jnp.int32, (STATS, LANES), 0)
    out = jnp.zeros((STATS, LANES), F32)
    for k, value in enumerate(values):
        out = jnp.where(row == k, value, out)
    return out


def total(x):
    return jnp.sum(x, axis=0, keepdims=True)


def combined(stats):
    top_s, sum_s, top_t, sum_t, mean_d, mean_u, mean_du = [stats[:, k, :] for k in range(7)]
    all_s = jnp.max(top_s, axis=0, keepdims=True)
    all_t = jnp.max(top_t, axis=0, keepdims=True)
    shift_s = top_s - all_s
    shift_t = top_t - all_t
    scale_s = jnp.exp(shift_s)
    scale_t = jnp.exp(shift_t)
    shift_d = shift_s - shift_t
    return (
        all_s,
        total(scale_s * sum_s),
        all_t,
        total(scale_t * sum_t),
        total(scale_s * (mean_d + shift_d * sum_s)),
        total(scale_s * (mean_u + shift_s * sum_s)),
        total(
            scale_s
            * (mean_du + shift_s * mean_d + shift_d * mean_u + shift_s * shift_d * sum_s)
        ),
    )


def span_of(v, core, half):
    return pl.ds(pl.multiple_of(v * 2 * half + core * half, 32), half)


def places(core):
    index = lax.axis_index("voc")
    x, y = lax.rem(index, SIDE), lax.div(index, SIDE)
    a = lax.select(core == 0, x, y)
    b = lax.select(core == 0, y, x)

    def place(j, k):
        u = lax.rem(a + SIDE - j, SIDE)
        w = lax.rem(b + SIDE - k, SIDE)
        return lax.select(core == 0, SIDE * w + u, SIDE * u + w)

    return place


def batches(refs, core):
    place = places(core)
    return [
        [(ref, j, place(j, k)) for j in range(SIDE)] for ref, k in zip(refs, (0, 1, 3, 2))
    ]


def logits_of(groups, student_head, teacher_head, core):
    student = jnp.zeros((VOC_DEV, LANES), F32)
    teacher = jnp.zeros((VOC_DEV, LANES), F32)
    squares = jnp.zeros((SPARE, LANES), F32)
    for group in groups:
        head_s = jnp.concatenate(
            [student_head[span_of(v, core, HALF_S), :] for _, _, v in group], axis=0
        )
        head_t = jnp.concatenate(
            [teacher_head[span_of(v, core, HALF_T), :] for _, _, v in group], axis=0
        )
        rows_s = jnp.concatenate([ref[j, :HALF_S, :] for ref, j, _ in group], axis=0)
        rows_t = jnp.concatenate([ref[j, HALF_S:, :] for ref, j, _ in group], axis=0)
        student = student + dot(head_s, rows_s, TN)
        teacher = teacher + dot(head_t, rows_t, TN)
        for ref, j, _ in group:
            squares = squares + ref[j, :SPARE, :].astype(F32)
            squares = squares + ref[j, SPARE : 2 * SPARE, :].astype(F32)
    return student, teacher, squares


def forward_own(
    a, u_first, d_second, student_head, teacher_in,
    student_out, teacher_out, squares_out, teacher_head, zero_out, sem,
):
    copy = pltpu.make_async_copy(teacher_in, teacher_head, sem)
    copy.start()
    zero_out[...] = jnp.zeros((1, LANES), F32)
    copy.wait()
    core = own_core()
    student, teacher, squares = logits_of(batches((a,), core), student_head, teacher_head, core)
    student_out[...] = student
    teacher_out[...] = teacher
    squares_out[...] = squares


def forward_near(
    u, d, student_head, teacher_head, student_sum, teacher_sum, squares_sum,
    student_out, teacher_out, squares_out, zero_out,
):
    core = own_core()
    groups = batches((None, u, d), core)[1:]
    student, teacher, squares = logits_of(groups, student_head, teacher_head, core)
    student_out[...] = student + student_sum[...]
    teacher_out[...] = teacher + teacher_sum[...]
    squares_out[...] = squares + squares_sum[...]
    zero_out[...] = jnp.zeros((1, LANES), F32)


def forward_mid(
    far, other_a, other_u, other_d, student_head, teacher_head,
    student_sum, teacher_sum, squares_sum, student_out, teacher_out, squares_out,
):
    core = own_core()
    groups = batches((None, None, None, far), core)[3:]
    one = logits_of(groups, student_head, teacher_head, core)
    groups = batches((other_a, other_u, other_d), 1 - core)
    two = logits_of(groups, student_head, teacher_head, 1 - core)
    student_out[...] = one[0] + two[0] + student_sum[...]
    teacher_out[...] = one[1] + two[1] + teacher_sum[...]
    squares_out[...] = one[2] + two[2] + squares_sum[...]


def forward_last(
    other_far, student_head, teacher_head, student_in, teacher_in, squares_in,
    exp_out, ratio_out, stats_out, tops_out, inverse_out,
):
    core = 1 - own_core()
    student, teacher, squares = logits_of(
        batches((None, None, None, other_far), core)[3:], student_head, teacher_head, core
    )
    squares = squares + squares_in[...]
    squares = jnp.where(lane_iota((SPARE, LANES)) >= VALID, squares, 0.0)
    lanes = spare_lanes()
    by_row = sum(dot(part, lanes, NT) for part in split(squares, 3))
    squares = total(jnp.where(spare_rows(), by_row, 0.0))
    inverse = lax.rsqrt(squares / DS + EPSILON)
    inverse_out[...] = inverse
    student = (student + student_in[...]) * inverse
    teacher = teacher + teacher_in[...]

    top_s = jnp.max(student, axis=0, keepdims=True)
    top_t = jnp.max(teacher, axis=0, keepdims=True)
    below = student - top_s
    exp_s = jnp.exp(below)
    below_t = teacher - top_t
    ratio = below - below_t
    exp_out[...] = exp_s
    ratio_out[...] = ratio
    weighted = exp_s * ratio
    stats = stack_rows(
        [
            top_s,
            total(exp_s),
            top_t,
            total(jnp.exp(below_t)),
            total(weighted),
            total(exp_s * below),
            total(weighted * below),
        ]
    )
    tops_out[...] = stats
    for v in range(VOC):
        stats_out[v] = stats


def combine_kernel(stats, out):
    tile = stack_rows(combined(stats))
    for g in range(GROUPS):
        out[g] = tile


def terms_of(groups, student_head, grad, core, out):
    for group in groups:
        head = jnp.concatenate(
            [student_head[span_of(v, core, HALF_S), :] for _, _, v in group], axis=0
        )
        term = dot(head, grad, NN).astype(BF)
        for i, (_, _, v) in enumerate(group):
            out[v] = term[i * HALF_S : (i + 1) * HALF_S]


def backward_one(
    stats, tops, exp_in, ratio_in, weight, inverse, student_head,
    grad_out, scaled_out, away, pull_out, loss_out,
):
    core = 1 - own_core()
    all_s, total_s, all_t, total_t, sum_d, sum_u, sum_du = combined(stats)
    inside = lane_iota((1, LANES)) < VALID
    mean_d = sum_d / total_s
    mean_u = sum_u / total_s
    covariance = sum_du / total_s - mean_d * mean_u
    divergence = mean_d - jnp.log(total_s) + jnp.log(total_t)
    loss_out[...] = jnp.sum(
        jnp.where(inside, weight[...] * divergence, 0.0), axis=1, keepdims=True
    )
    pull_out[...] = weight[...] * covariance * inverse[...] * inverse[...] / DS
    shift_s = tops[0:1, :] - all_s
    shift_t = tops[2:3, :] - all_t
    factor = weight[...] * jnp.exp(shift_s) / total_s
    offset = shift_s - shift_t - mean_d
    grad = jnp.where(inside, factor * exp_in[...] * (ratio_in[...] + offset), 0.0)
    kept = jnp.where(inside, inverse[...], 0.0)
    scaled_out[...] = (grad * kept).astype(BF)
    grad = grad.astype(BF)
    grad_out[...] = grad
    terms_of(batches((None,) * 4, core), student_head, grad, core, away)


def backward_two(
    grad, student_head, hidden, gain, student_row, inverse, pull, stay, base_out
):
    core = own_core()
    first = lax.axis_index("grp") * ROWS
    own = lax.broadcasted_iota(jnp.int32, (ROWS, LANES), 0) + first == student_row[...]
    own_rms = jnp.sum(jnp.where(own, inverse[...], 0.0), axis=1, keepdims=True)
    own_pull = jnp.sum(jnp.where(own, pull[...], 0.0), axis=1, keepdims=True)
    base_out[:ROWS] = own_rms * gain[...]
    base_out[ROWS : 2 * ROWS] = hidden[...].astype(F32) * own_pull
    base_out[2 * ROWS :] = jnp.broadcast_to(1.0 / gain[...], (8, LANES))
    terms_of(batches((None,) * 4, core), student_head, grad[...], core, stay)


def head_kernel(*refs):
    scaled, out, zero_out, blocks, sems = refs[8:]
    zero_out[...] = jnp.zeros((1, LANES), F32)
    copies = []
    for k, core in enumerate((own_core(), 1 - own_core())):
        for group in batches(refs[SIDE * k : SIDE * k + SIDE], core):
            block = jnp.concatenate([ref[j, :HALF_S, :] for ref, j, _ in group], axis=0)
            result = dot(block, scaled[...], NT).astype(BF)
            for i, (_, _, v) in enumerate(group):
                n = len(copies)
                blocks[n] = result[i * HALF_S : (i + 1) * HALF_S]
                copies.append(
                    pltpu.make_async_copy(
                        blocks.at[n], out.at[span_of(v, core, HALF_S)], sems.at[n]
                    )
                )
                copies[n].start()
    for copy in copies:
        copy.wait()


def pair_kernel(stay, arrived, zero, out):
    for v in range(VOC):
        out[v] = (stay[v].astype(F32) + arrived[v].astype(F32)).astype(BF)


def send_kernel(pieces, student_row, block, inverse, out):
    summed = pieces[0].astype(F32)
    for v in range(1, VOC):
        summed = summed + pieces[v].astype(F32)
    lane = lane_iota((HALF_S, LANES))
    inside = lane < VALID
    scaled = jnp.where(inside, block[:HALF_S, :].astype(F32) * inverse[...], 0.0)
    gain = jnp.sum(summed * scaled, axis=1, keepdims=True)
    summed = jnp.where(lane == VALID, gain, summed).astype(BF)
    slot = lax.broadcasted_iota(jnp.int32, (SEND, LANES), 0)
    extra = (slot == ROWS) & (lane_iota((SEND, LANES)) == VALID)
    picks = []
    for g in range(GROUPS):
        pick = ((slot < ROWS) & (student_row[...] == slot + g * ROWS)) | extra
        picks.append(jnp.where(pick, 1.0, 0.0).astype(BF))
    result = dot(jnp.concatenate(picks, axis=0), summed, NT).astype(BF)
    for g in range(GROUPS):
        out[g] = result[g * SEND : (g + 1) * SEND]


def finish_kernel(pieces, base, grad_hidden, grad_gain):
    halves = []
    for c in range(2):
        summed = pieces[c].astype(F32)
        for z in range(1, GROUPS // 2):
            summed = summed + pieces[2 * z + c].astype(F32)
        halves.append(summed)
    summed = jnp.concatenate(halves, axis=1)
    grad_gain[...] = summed[ROWS : ROWS + 1] * base[2 * ROWS : 2 * ROWS + 1]
    grad_hidden[...] = (summed[:ROWS] * base[:ROWS] - base[ROWS : 2 * ROWS]).astype(BF)


def shape(dims, dtype):
    return jax.ShapeDtypeStruct(dims, dtype)


def params(mib):
    return pltpu.CompilerParams(vmem_limit_bytes=mib * 1024 * 1024)


def in_hbm(x):
    return pltpu.with_memory_space_constraint(x, pltpu.HBM)


def cost(flops):
    return pl.CostEstimate(flops=flops, bytes_accessed=4 * 1024 * 1024, transcendentals=0)


def exchange(x, axis):
    return lax.all_to_all(x, axis, 0, 0, tiled=True)


HBM = pl.BlockSpec(memory_space=pltpu.HBM)
ANY = pl.BlockSpec(memory_space=pl.ANY)
VMEM = pl.BlockSpec(memory_space=pltpu.VMEM)


def local(
    student_hidden, norm_gain, teacher_hidden, student_head, teacher_head, episode_source, lengths
):
    row = shape((1, LANES), F32)
    logits = shape((VOC_DEV, LANES), F32)
    half_rows = shape((VOC, HALF_S, LANES), BF)

    table = shape((1, LANES), jnp.int32)
    episodes = lengths.shape[0]
    packed, student_row, teacher_row, weight, gain_parts = pl.pallas_call(
        pack_kernel,
        out_shape=(
            shape((GROUPS, PACK, HALF_S), BF), table, table, row, shape((16, HALF_S), F32)
        ),
        in_specs=[HBM] * 5,
        out_specs=(VMEM,) * 5,
        scratch_shapes=[
            pltpu.VMEM((ROWS, 2 * HALF_S), BF),
            pltpu.VMEM((ROWS, 2 * HALF_T), BF),
            pltpu.VMEM((1, episodes), jnp.int32),
            pltpu.VMEM((1, episodes), jnp.int32),
            pltpu.VMEM((1, 2 * HALF_S), F32),
            pltpu.SemaphoreType.DMA((5,)),
        ],
        compiler_params=params(4),
    )(
        in_hbm(student_hidden), in_hbm(teacher_hidden),
        in_hbm(episode_source[None]), in_hbm(lengths[None]), in_hbm(norm_gain[None]),
    )
    held = exchange(packed, "grp")
    block = pl.pallas_call(
        compact_kernel, out_shape=shape((HALF, LANES), BF), compiler_params=params(8)
    )(held, student_row, teacher_row, gain_parts)

    one = lax.ppermute(block, BOTH, ring(1, 1))
    three = lax.ppermute(block, BOTH, ring(1, 3))
    two = lax.ppermute(block, BOTH, ring(1, 2))
    first = jnp.stack([block, one])
    second = jnp.stack([two, three])
    u_first = lax.ppermute(first, BOTH, ring(2, 1))
    d_second = lax.ppermute(second, BOTH, ring(2, 3))
    u_second = lax.ppermute(second, BOTH, ring(2, 1))
    d_first = lax.ppermute(first, BOTH, ring(2, 3))
    v = lax.ppermute(u_first, BOTH, ring(2, 1))
    w = lax.ppermute(d_second, BOTH, ring(2, 3))
    a = jnp.concatenate([first, second], axis=0)
    u = jnp.concatenate([u_first, u_second], axis=0)
    d = jnp.concatenate([d_first, d_second], axis=0)
    partial = (logits, logits, shape((SPARE, LANES), F32))

    def sems(count):
        return pltpu.SemaphoreType.DMA((count,))

    *sums, head_t, zero = pl.pallas_call(
        forward_own,
        out_shape=partial + (pltpu.VMEM(teacher_head.shape, BF), row),
        in_specs=[VMEM, ANY, ANY, VMEM, HBM],
        out_specs=(VMEM,) * 5,
        scratch_shapes=[pltpu.SemaphoreType.DMA],
        compiler_params=params(12),
        cost_estimate=cost(SIDE * HALF * VOC_DEV * LANES * 2),
    )(a, u_first, d_second, student_head, in_hbm(teacher_head))
    other = (lax.ppermute(a, "grp", CORE_SWAP),) + tuple(
        lax.ppermute(part + zero.astype(BF), "grp", CORE_SWAP) for part in (u, d)
    )
    *sums, zero = pl.pallas_call(
        forward_near,
        out_shape=partial + (row,),
        compiler_params=params(12),
        cost_estimate=cost(2 * SIDE * HALF * VOC_DEV * LANES * 2),
    )(u, d, student_head, head_t, *sums)
    far = jnp.concatenate([v, w], axis=0) + zero.astype(BF)
    other_far = lax.ppermute(far, "grp", CORE_SWAP)
    sums = pl.pallas_call(
        forward_mid,
        out_shape=partial,
        compiler_params=params(12),
        cost_estimate=cost(VOC * HALF * VOC_DEV * LANES * 2),
    )(far, *other, student_head, head_t, *sums)
    exp_s, ratio, stats, tops, inverse = pl.pallas_call(
        forward_last,
        out_shape=(
            logits,
            logits,
            shape((VOC, STATS, LANES), F32),
            shape((STATS, LANES), F32),
            row,
        ),
        compiler_params=params(12),
        cost_estimate=cost(SIDE * HALF * VOC_DEV * LANES * 2),
    )(other_far, student_head, head_t, *sums)

    from_voc = exchange(stats, "voc")
    spread = pl.pallas_call(
        combine_kernel, out_shape=shape((GROUPS, STATS, LANES), F32), compiler_params=params(4)
    )(from_voc)
    from_grp = exchange(spread, "grp")

    grad, scaled, away, pull, loss = pl.pallas_call(
        backward_one,
        out_shape=(
            shape((VOC_DEV, LANES), BF),
            shape((VOC_DEV, LANES), BF),
            half_rows,
            row,
            shape((1, 1), F32),
        ),
        out_specs=(VMEM,) * 5,
        compiler_params=params(8),
        cost_estimate=cost(DS * VOC_DEV * LANES),
    )(from_grp, tops, exp_s, ratio, weight, inverse, student_head)
    arrived = lax.ppermute(away, "grp", CORE_SWAP)
    stay, base = pl.pallas_call(
        backward_two,
        out_shape=(half_rows, shape((2 * ROWS + 8, LANES), F32)),
        compiler_params=params(8),
        cost_estimate=cost(DS * VOC_DEV * LANES),
    )(grad, student_head, student_hidden, norm_gain[None], student_row, inverse, pull)
    grad_head, zero = pl.pallas_call(
        head_kernel,
        out_shape=(shape((DS, VOC_DEV), BF), row),
        out_specs=(HBM, VMEM),
        scratch_shapes=[pltpu.VMEM((2 * VOC, HALF_S, VOC_DEV), BF), sems(2 * VOC)],
        compiler_params=params(12),
        cost_estimate=cost(DS * VOC_DEV * LANES * 2),
    )(a, u, d, far, *other, other_far, scaled)
    pair = pl.pallas_call(pair_kernel, out_shape=half_rows, compiler_params=params(8))(
        stay, arrived, zero
    )
    pieces = exchange(pair, "voc")
    outgoing = pl.pallas_call(
        send_kernel,
        out_shape=shape((GROUPS, SEND, HALF_S), BF),
        compiler_params=params(8),
    )(pieces, student_row, block, inverse)
    pieces = exchange(outgoing, "grp")
    grad_hidden, grad_gain = pl.pallas_call(
        finish_kernel,
        out_shape=(shape((ROWS, 2 * HALF_S), BF), row),
        compiler_params=params(4),
    )(pieces, base)
    return (loss.reshape(()), grad_hidden, grad_gain.reshape(-1), grad_head)


def solution(mesh):
    placed = (
        P("grp", "voc"),
        P("voc"),
        P("grp", "voc"),
        P(None, ("grp", "voc")),
        P(None, ("grp", "voc")),
        P(),
        P(),
    )
    return jax.shard_map(
        local,
        mesh=mesh,
        in_specs=placed,
        out_specs=(P(), P("grp", "voc"), P("voc"), P(None, ("grp", "voc"))),
        check_vma=False,
    )
```

```python
import jax
import jax.numpy as jnp
from jax import lax
from jax.experimental import pallas as pl
from jax.experimental.pallas import tpu as pltpu
from jax.sharding import PartitionSpec as P

DS = 4096
SEQ = 2
VALID = 240
LANES = 256
EPSILON = 1e-06
LARGEST = 3e38
GROUPS = 16
VOC = 16
ROWS = 24
HALF_S = 128
HALF_T = 160
HALF = HALF_S + HALF_T
VOC_DEV = 384
STATS = 8
SEND = 32
PACK = 56
TAIL = 32
PER = 4
SPARE = 16
SIDE = 4
BF = jnp.bfloat16
F32 = jnp.float32
CORE_SWAP = [(i, i ^ 1) for i in range(GROUPS)]
BOTH = ("grp", "voc")


def ring(phase, step):
    pairs = []
    for g in range(GROUPS):
        for v in range(VOC):
            y, x = divmod(v, SIDE)
            if (g % 2 == 0) == (phase == 1):
                x = (x + step) % SIDE
            else:
                y = (y + step) % SIDE
            pairs.append((g * VOC + v, g * VOC + y * SIDE + x))
    return pairs


TN = (((0,), (0,)), ((), ()))
NT = (((1,), (1,)), ((), ()))
NN = (((1,), (0,)), ((), ()))


def dot(a, b, dims):
    return lax.dot_general(a, b, dims, preferred_element_type=F32)


def lane_tables(source, lengths):
    episodes = lengths.shape[1]
    here = lax.broadcasted_iota(jnp.int32, (episodes, episodes), 0)
    there = lane_iota((episodes, episodes))

    def column(mask, values):
        return jnp.sum(jnp.where(mask, values, 0.0), axis=1, keepdims=True)

    lengths = lengths.astype(F32)
    two = jnp.where(lengths == 2.0, 1.0, 0.0)
    rank = column(there < here, two)
    two = column(here == there, two)
    source = column(here == there, source.astype(F32))
    lengths = column(here == there, lengths)
    lane = lane_iota((episodes, LANES)).astype(F32)
    number = lax.broadcasted_iota(jnp.int32, (episodes, LANES), 0).astype(F32)
    pick = (lane == number) | ((two == 1.0) & (lane == episodes + rank))

    def of_lane(values):
        return jnp.sum(jnp.where(pick, values, 0.0), axis=0, keepdims=True)

    lane = lane_iota((1, LANES))
    inside = lane < VALID
    position = jnp.where(lane >= episodes, 1.0, 0.0)
    student_row = jnp.where(inside, of_lane(number) * SEQ + position, -1.0)
    teacher_row = jnp.where(inside, of_lane(source) * SEQ + position, -1.0)
    weight = jnp.where(inside, 1.0 / jnp.maximum(of_lane(lengths), 1.0), 0.0)
    return student_row.astype(jnp.int32), teacher_row.astype(jnp.int32), weight


def own_core():
    return lax.rem(lax.axis_index("grp"), 2)


def lane_iota(shape):
    return lax.broadcasted_iota(jnp.int32, shape, len(shape) - 1)


def pack_kernel(
    student_in, teacher_in, source_in, lengths_in, gain_in,
    out, student_row, teacher_row, weight, gain_out,
    student, teacher, source, lengths, gain, sems,
):
    pairs = (
        (source_in, source),
        (lengths_in, lengths),
        (gain_in, gain),
        (student_in, student),
        (teacher_in, teacher),
    )
    copies = []
    for n, (place, held) in enumerate(pairs):
        copies.append(pltpu.make_async_copy(place, held, sems.at[n]))
        copies[n].start()
    copies[0].wait()
    copies[1].wait()
    student_row[...], teacher_row[...], weight[...] = lane_tables(source[...], lengths[...])
    copies[2].wait()
    row = lax.broadcasted_iota(jnp.int32, (16, HALF_S), 0)
    own_gain = jnp.where(own_core() == 0, gain[:, :HALF_S], gain[:, HALF_S:])
    spread = jnp.zeros((16, HALF_S), F32)
    for k, part in enumerate(split(own_gain, 3)):
        spread = jnp.where(row == k, part.astype(F32), spread)
    gain_out[...] = spread
    copies[3].wait()
    copies[4].wait()
    for c in range(2):
        rows = teacher[:, c * HALF_T : (c + 1) * HALF_T].astype(F32)
        tail = rows[:, HALF_S:]
        tail = jnp.concatenate(
            [tail[:8], tail[8:16], tail[16:24], jnp.zeros((8, TAIL), F32)], axis=1
        )
        whole = jnp.concatenate(
            [student[:, c * HALF_S : (c + 1) * HALF_S].astype(F32), rows[:, :HALF_S], tail], axis=0
        )
        whole = whole.astype(BF)
        for z in range(GROUPS // 2):
            out[2 * z + c] = whole


def spare_lanes():
    source = lax.broadcasted_iota(jnp.int32, (LANES, LANES), 0)
    lane = lane_iota((LANES, LANES))
    return jnp.where(lane == VALID + lax.rem(source, SPARE), 1.0, 0.0).astype(BF)


def spare_rows():
    row = lax.broadcasted_iota(jnp.int32, (SPARE, LANES), 0)
    return lax.div(lane_iota((SPARE, LANES)), SPARE) == row


def split(x, parts):
    out = []
    for _ in range(parts):
        out.append(x.astype(BF))
        x = x - out[-1].astype(F32)
    return out


def compact_kernel(held, student_row, teacher_row, gain, out):
    blocks = [held[g].astype(F32) for g in range(GROUPS)]
    rows_s = jnp.concatenate([block[:ROWS] for block in blocks], axis=0).astype(BF)
    rows_t = jnp.concatenate([block[ROWS : 2 * ROWS] for block in blocks], axis=0).astype(BF)
    tails = jnp.concatenate([block[2 * ROWS :] for block in blocks], axis=0).astype(BF)
    ids = lax.broadcasted_iota(jnp.int32, (GROUPS * ROWS, LANES), 0)
    pick_s = jnp.where(ids == student_row[...], 1.0, 0.0).astype(BF)
    pick_t = jnp.where(ids == teacher_row[...], 1.0, 0.0).astype(BF)
    block_s = dot(rows_s, pick_s, TN)
    block_t = dot(rows_t, pick_t, TN).astype(BF)
    short = lax.broadcasted_iota(jnp.int32, (GROUPS * 8, LANES), 0)
    short = lax.div(short, 8) * ROWS + lax.rem(short, 8)
    tail = jnp.zeros((TAIL, LANES), F32)
    for k in range(3):
        pick = jnp.where(short + 8 * k == teacher_row[...], 1.0, 0.0).astype(BF)
        tail = tail + dot(tails, pick, TN)[k * TAIL : (k + 1) * TAIL]
    spread_gain = dot(gain[...].astype(BF), jnp.ones((16, LANES), BF), TN)
    squares = jnp.minimum(jnp.sum(block_s * block_s, axis=0, keepdims=True), LARGEST)
    parts = split(jnp.where(spare_rows(), squares, 0.0), 2)
    lanes = spare_lanes()
    spare = jnp.concatenate([dot(part, lanes, NN) for part in parts], axis=0)
    block_s = block_s * spread_gain
    block_s = jnp.concatenate([block_s[: 2 * SPARE] + spare, block_s[2 * SPARE :]], axis=0)
    out[:HALF_S, :] = block_s.astype(BF)
    out[HALF_S : 2 * HALF_S, :] = block_t
    out[2 * HALF_S :, :] = tail.astype(BF)


def stack_rows(values):
    row = lax.broadcasted_iota(jnp.int32, (STATS, LANES), 0)
    out = jnp.zeros((STATS, LANES), F32)
    for k, value in enumerate(values):
        out = jnp.where(row == k, value, out)
    return out


def total(x):
    return jnp.sum(x, axis=0, keepdims=True)


def combined(stats):
    top_s, sum_s, top_t, sum_t, mean_d, mean_u, mean_du = [stats[:, k, :] for k in range(7)]
    all_s = jnp.max(top_s, axis=0, keepdims=True)
    all_t = jnp.max(top_t, axis=0, keepdims=True)
    shift_s = top_s - all_s
    shift_t = top_t - all_t
    scale_s = jnp.exp(shift_s)
    scale_t = jnp.exp(shift_t)
    shift_d = shift_s - shift_t
    return (
        all_s,
        total(scale_s * sum_s),
        all_t,
        total(scale_t * sum_t),
        total(scale_s * (mean_d + shift_d * sum_s)),
        total(scale_s * (mean_u + shift_s * sum_s)),
        total(
            scale_s
            * (mean_du + shift_s * mean_d + shift_d * mean_u + shift_s * shift_d * sum_s)
        ),
    )


def span_of(v, core, half):
    return pl.ds(pl.multiple_of(v * 2 * half + core * half, 32), half)


def places(core):
    index = lax.axis_index("voc")
    x, y = lax.rem(index, SIDE), lax.div(index, SIDE)
    a = lax.select(core == 0, x, y)
    b = lax.select(core == 0, y, x)

    def place(j, k):
        u = lax.rem(a + SIDE - j, SIDE)
        w = lax.rem(b + SIDE - k, SIDE)
        return lax.select(core == 0, SIDE * w + u, SIDE * u + w)

    return place


def batches(refs, core):
    place = places(core)
    return [
        [(ref, j, place(j, k)) for j in range(SIDE)] for ref, k in zip(refs, (0, 1, 3, 2))
    ]


def logits_of(groups, student_head, teacher_head, core):
    student = jnp.zeros((VOC_DEV, LANES), F32)
    teacher = jnp.zeros((VOC_DEV, LANES), F32)
    squares = jnp.zeros((SPARE, LANES), F32)
    for group in groups:
        head_s = jnp.concatenate(
            [student_head[span_of(v, core, HALF_S), :] for _, _, v in group], axis=0
        )
        head_t = jnp.concatenate(
            [teacher_head[span_of(v, core, HALF_T), :] for _, _, v in group], axis=0
        )
        rows_s = jnp.concatenate([ref[j, :HALF_S, :] for ref, j, _ in group], axis=0)
        rows_t = jnp.concatenate([ref[j, HALF_S:, :] for ref, j, _ in group], axis=0)
        student = student + dot(head_s, rows_s, TN)
        teacher = teacher + dot(head_t, rows_t, TN)
        for ref, j, _ in group:
            squares = squares + ref[j, :SPARE, :].astype(F32)
            squares = squares + ref[j, SPARE : 2 * SPARE, :].astype(F32)
    return student, teacher, squares


def forward_own(
    a, u_first, d_second, student_head, teacher_in,
    student_out, teacher_out, squares_out, teacher_head, zero_out, sem,
):
    copy = pltpu.make_async_copy(teacher_in, teacher_head, sem)
    copy.start()
    zero_out[...] = jnp.zeros((1, LANES), F32)
    copy.wait()
    core = own_core()
    student, teacher, squares = logits_of(batches((a,), core), student_head, teacher_head, core)
    student_out[...] = student
    teacher_out[...] = teacher
    squares_out[...] = squares


def forward_near(
    u, d, student_head, teacher_head, student_sum, teacher_sum, squares_sum,
    student_out, teacher_out, squares_out, zero_out,
):
    core = own_core()
    groups = batches((None, u, d), core)[1:]
    student, teacher, squares = logits_of(groups, student_head, teacher_head, core)
    student_out[...] = student + student_sum[...]
    teacher_out[...] = teacher + teacher_sum[...]
    squares_out[...] = squares + squares_sum[...]
    zero_out[...] = jnp.zeros((1, LANES), F32)


def forward_mid(
    far, other_a, other_u, other_d, student_head, teacher_head,
    student_sum, teacher_sum, squares_sum, student_out, teacher_out, squares_out,
):
    core = own_core()
    groups = batches((None, None, None, far), core)[3:]
    one = logits_of(groups, student_head, teacher_head, core)
    groups = batches((other_a, other_u, other_d), 1 - core)
    two = logits_of(groups, student_head, teacher_head, 1 - core)
    student_out[...] = one[0] + two[0] + student_sum[...]
    teacher_out[...] = one[1] + two[1] + teacher_sum[...]
    squares_out[...] = one[2] + two[2] + squares_sum[...]


def forward_last(
    other_far, student_head, teacher_head, student_in, teacher_in, squares_in,
    exp_out, ratio_out, stats_out, tops_out, inverse_out,
):
    core = 1 - own_core()
    student, teacher, squares = logits_of(
        batches((None, None, None, other_far), core)[3:], student_head, teacher_head, core
    )
    squares = squares + squares_in[...]
    squares = jnp.where(lane_iota((SPARE, LANES)) >= VALID, squares, 0.0)
    lanes = spare_lanes()
    by_row = sum(dot(part, lanes, NT) for part in split(squares, 3))
    squares = total(jnp.where(spare_rows(), by_row, 0.0))
    inverse = lax.rsqrt(squares / DS + EPSILON)
    inverse_out[...] = inverse
    student = (student + student_in[...]) * inverse
    teacher = teacher + teacher_in[...]

    top_s = jnp.max(student, axis=0, keepdims=True)
    top_t = jnp.max(teacher, axis=0, keepdims=True)
    below = student - top_s
    exp_s = jnp.exp(below)
    below_t = teacher - top_t
    ratio = below - below_t
    exp_out[...] = exp_s
    ratio_out[...] = ratio
    weighted = exp_s * ratio
    stats = stack_rows(
        [
            top_s,
            total(exp_s),
            top_t,
            total(jnp.exp(below_t)),
            total(weighted),
            total(exp_s * below),
            total(weighted * below),
        ]
    )
    tops_out[...] = stats
    for v in range(VOC):
        stats_out[v] = stats


def combine_kernel(stats, out):
    tile = stack_rows(combined(stats))
    for g in range(GROUPS):
        out[g] = tile


def terms_of(groups, student_head, grad, core, out):
    for group in groups:
        head = jnp.concatenate(
            [student_head[span_of(v, core, HALF_S), :] for _, _, v in group], axis=0
        )
        term = dot(head, grad, NN).astype(BF)
        for i, (_, _, v) in enumerate(group):
            out[v] = term[i * HALF_S : (i + 1) * HALF_S]


def backward_one(
    stats, tops, exp_in, ratio_in, weight, inverse, student_head,
    grad_out, scaled_out, away, pull_out, loss_out,
):
    core = 1 - own_core()
    all_s, total_s, all_t, total_t, sum_d, sum_u, sum_du = combined(stats)
    inside = lane_iota((1, LANES)) < VALID
    mean_d = sum_d / total_s
    mean_u = sum_u / total_s
    covariance = sum_du / total_s - mean_d * mean_u
    divergence = mean_d - jnp.log(total_s) + jnp.log(total_t)
    loss_out[...] = jnp.sum(
        jnp.where(inside, weight[...] * divergence, 0.0), axis=1, keepdims=True
    )
    pull_out[...] = weight[...] * covariance * inverse[...] * inverse[...] / DS
    shift_s = tops[0:1, :] - all_s
    shift_t = tops[2:3, :] - all_t
    factor = weight[...] * jnp.exp(shift_s) / total_s
    offset = shift_s - shift_t - mean_d
    grad = jnp.where(inside, factor * exp_in[...] * (ratio_in[...] + offset), 0.0)
    kept = jnp.where(inside, inverse[...], 0.0)
    scaled_out[...] = (grad * kept).astype(BF)
    grad = grad.astype(BF)
    grad_out[...] = grad
    terms_of(batches((None,) * 4, core), student_head, grad, core, away)


def backward_two(*refs):
    scaled, grad, student_head, hidden, gain, student_row, inverse, pull = refs[8:16]
    stay, base_out, out, blocks, sems = refs[16:]
    core = own_core()
    copies = []
    for k, side in enumerate((core, 1 - core)):
        for group in batches(refs[SIDE * k : SIDE * k + SIDE], side):
            block = jnp.concatenate([ref[j, :HALF_S, :] for ref, j, _ in group], axis=0)
            result = dot(block, scaled[...], NT).astype(BF)
            for i, (_, _, v) in enumerate(group):
                n = len(copies)
                blocks[n] = result[i * HALF_S : (i + 1) * HALF_S]
                copies.append(
                    pltpu.make_async_copy(
                        blocks.at[n], out.at[span_of(v, side, HALF_S)], sems.at[n]
                    )
                )
                copies[n].start()
    first = lax.axis_index("grp") * ROWS
    own = lax.broadcasted_iota(jnp.int32, (ROWS, LANES), 0) + first == student_row[...]
    own_rms = jnp.sum(jnp.where(own, inverse[...], 0.0), axis=1, keepdims=True)
    own_pull = jnp.sum(jnp.where(own, pull[...], 0.0), axis=1, keepdims=True)
    base_out[:ROWS] = own_rms * gain[...]
    base_out[ROWS : 2 * ROWS] = hidden[...].astype(F32) * own_pull
    base_out[2 * ROWS :] = jnp.broadcast_to(1.0 / gain[...], (8, LANES))
    terms_of(batches((None,) * 4, core), student_head, grad[...], core, stay)
    for copy in copies:
        copy.wait()


def pair_kernel(stay, arrived, out):
    for v in range(VOC):
        out[v] = (stay[v].astype(F32) + arrived[v].astype(F32)).astype(BF)


def send_kernel(pieces, student_row, block, inverse, out):
    summed = pieces[0].astype(F32)
    for v in range(1, VOC):
        summed = summed + pieces[v].astype(F32)
    lane = lane_iota((HALF_S, LANES))
    inside = lane < VALID
    scaled = jnp.where(inside, block[:HALF_S, :].astype(F32) * inverse[...], 0.0)
    gain = jnp.sum(summed * scaled, axis=1, keepdims=True)
    summed = jnp.where(lane == VALID, gain, summed).astype(BF)
    slot = lax.broadcasted_iota(jnp.int32, (SEND, LANES), 0)
    extra = (slot == ROWS) & (lane_iota((SEND, LANES)) == VALID)
    picks = []
    for g in range(GROUPS):
        pick = ((slot < ROWS) & (student_row[...] == slot + g * ROWS)) | extra
        picks.append(jnp.where(pick, 1.0, 0.0).astype(BF))
    result = dot(jnp.concatenate(picks, axis=0), summed, NT).astype(BF)
    for g in range(GROUPS):
        out[g] = result[g * SEND : (g + 1) * SEND]


def finish_kernel(pieces, base, grad_hidden, grad_gain):
    halves = []
    for c in range(2):
        summed = pieces[c].astype(F32)
        for z in range(1, GROUPS // 2):
            summed = summed + pieces[2 * z + c].astype(F32)
        halves.append(summed)
    summed = jnp.concatenate(halves, axis=1)
    grad_gain[...] = summed[ROWS : ROWS + 1] * base[2 * ROWS : 2 * ROWS + 1]
    grad_hidden[...] = (summed[:ROWS] * base[:ROWS] - base[ROWS : 2 * ROWS]).astype(BF)


def shape(dims, dtype):
    return jax.ShapeDtypeStruct(dims, dtype)


def params(mib):
    return pltpu.CompilerParams(vmem_limit_bytes=mib * 1024 * 1024)


def in_hbm(x):
    return pltpu.with_memory_space_constraint(x, pltpu.HBM)


def cost(flops):
    return pl.CostEstimate(flops=flops, bytes_accessed=4 * 1024 * 1024, transcendentals=0)


def exchange(x, axis):
    return lax.all_to_all(x, axis, 0, 0, tiled=True)


HBM = pl.BlockSpec(memory_space=pltpu.HBM)
ANY = pl.BlockSpec(memory_space=pl.ANY)
VMEM = pl.BlockSpec(memory_space=pltpu.VMEM)


def local(
    student_hidden, norm_gain, teacher_hidden, student_head, teacher_head, episode_source, lengths
):
    row = shape((1, LANES), F32)
    logits = shape((VOC_DEV, LANES), F32)
    half_rows = shape((VOC, HALF_S, LANES), BF)

    table = shape((1, LANES), jnp.int32)
    episodes = lengths.shape[0]
    packed, student_row, teacher_row, weight, gain_parts = pl.pallas_call(
        pack_kernel,
        out_shape=(
            shape((GROUPS, PACK, HALF_S), BF), table, table, row, shape((16, HALF_S), F32)
        ),
        in_specs=[HBM] * 5,
        out_specs=(VMEM,) * 5,
        scratch_shapes=[
            pltpu.VMEM((ROWS, 2 * HALF_S), BF),
            pltpu.VMEM((ROWS, 2 * HALF_T), BF),
            pltpu.VMEM((1, episodes), jnp.int32),
            pltpu.VMEM((1, episodes), jnp.int32),
            pltpu.VMEM((1, 2 * HALF_S), F32),
            pltpu.SemaphoreType.DMA((5,)),
        ],
        compiler_params=params(4),
    )(
        in_hbm(student_hidden), in_hbm(teacher_hidden),
        in_hbm(episode_source[None]), in_hbm(lengths[None]), in_hbm(norm_gain[None]),
    )
    held = exchange(packed, "grp")
    block = pl.pallas_call(
        compact_kernel, out_shape=shape((HALF, LANES), BF), compiler_params=params(8)
    )(held, student_row, teacher_row, gain_parts)

    one = lax.ppermute(block, BOTH, ring(1, 1))
    three = lax.ppermute(block, BOTH, ring(1, 3))
    two = lax.ppermute(block, BOTH, ring(1, 2))
    first = jnp.stack([block, one])
    second = jnp.stack([two, three])
    u_first = lax.ppermute(first, BOTH, ring(2, 1))
    d_second = lax.ppermute(second, BOTH, ring(2, 3))
    u_second = lax.ppermute(second, BOTH, ring(2, 1))
    d_first = lax.ppermute(first, BOTH, ring(2, 3))
    v = lax.ppermute(u_first, BOTH, ring(2, 1))
    w = lax.ppermute(d_second, BOTH, ring(2, 3))
    a = jnp.concatenate([first, second], axis=0)
    u = jnp.concatenate([u_first, u_second], axis=0)
    d = jnp.concatenate([d_first, d_second], axis=0)
    partial = (logits, logits, shape((SPARE, LANES), F32))

    def sems(count):
        return pltpu.SemaphoreType.DMA((count,))

    *sums, head_t, zero = pl.pallas_call(
        forward_own,
        out_shape=partial + (pltpu.VMEM(teacher_head.shape, BF), row),
        in_specs=[VMEM, ANY, ANY, VMEM, HBM],
        out_specs=(VMEM,) * 5,
        scratch_shapes=[pltpu.SemaphoreType.DMA],
        compiler_params=params(12),
        cost_estimate=cost(SIDE * HALF * VOC_DEV * LANES * 2),
    )(a, u_first, d_second, student_head, in_hbm(teacher_head))
    other = (lax.ppermute(a, "grp", CORE_SWAP),) + tuple(
        lax.ppermute(part + zero.astype(BF), "grp", CORE_SWAP) for part in (u, d)
    )
    *sums, zero = pl.pallas_call(
        forward_near,
        out_shape=partial + (row,),
        compiler_params=params(12),
        cost_estimate=cost(2 * SIDE * HALF * VOC_DEV * LANES * 2),
    )(u, d, student_head, head_t, *sums)
    far = jnp.concatenate([v, w], axis=0) + zero.astype(BF)
    other_far = lax.ppermute(far, "grp", CORE_SWAP)
    sums = pl.pallas_call(
        forward_mid,
        out_shape=partial,
        compiler_params=params(12),
        cost_estimate=cost(VOC * HALF * VOC_DEV * LANES * 2),
    )(far, *other, student_head, head_t, *sums)
    exp_s, ratio, stats, tops, inverse = pl.pallas_call(
        forward_last,
        out_shape=(
            logits,
            logits,
            shape((VOC, STATS, LANES), F32),
            shape((STATS, LANES), F32),
            row,
        ),
        compiler_params=params(12),
        cost_estimate=cost(SIDE * HALF * VOC_DEV * LANES * 2),
    )(other_far, student_head, head_t, *sums)

    from_voc = exchange(stats, "voc")
    spread = pl.pallas_call(
        combine_kernel, out_shape=shape((GROUPS, STATS, LANES), F32), compiler_params=params(4)
    )(from_voc)
    from_grp = exchange(spread, "grp")

    grad, scaled, away, pull, loss = pl.pallas_call(
        backward_one,
        out_shape=(
            shape((VOC_DEV, LANES), BF),
            shape((VOC_DEV, LANES), BF),
            half_rows,
            row,
            shape((1, 1), F32),
        ),
        out_specs=(VMEM,) * 5,
        compiler_params=params(8),
        cost_estimate=cost(DS * VOC_DEV * LANES),
    )(from_grp, tops, exp_s, ratio, weight, inverse, student_head)
    arrived = lax.ppermute(away, "grp", CORE_SWAP)
    stay, base, grad_head = pl.pallas_call(
        backward_two,
        out_shape=(
            half_rows,
            shape((2 * ROWS + 8, LANES), F32),
            shape((DS, VOC_DEV), BF),
        ),
        out_specs=(VMEM, VMEM, HBM),
        scratch_shapes=[pltpu.VMEM((2 * VOC, HALF_S, VOC_DEV), BF), sems(2 * VOC)],
        compiler_params=params(12),
        cost_estimate=cost(DS * VOC_DEV * LANES * 3),
    )(
        a, u, d, far, *other, other_far, scaled, grad, student_head,
        student_hidden, norm_gain[None], student_row, inverse, pull,
    )
    pair = pl.pallas_call(pair_kernel, out_shape=half_rows, compiler_params=params(8))(
        stay, arrived
    )
    pieces = exchange(pair, "voc")
    outgoing = pl.pallas_call(
        send_kernel,
        out_shape=shape((GROUPS, SEND, HALF_S), BF),
        compiler_params=params(8),
    )(pieces, student_row, block, inverse)
    pieces = exchange(outgoing, "grp")
    grad_hidden, grad_gain = pl.pallas_call(
        finish_kernel,
        out_shape=(shape((ROWS, 2 * HALF_S), BF), row),
        compiler_params=params(4),
    )(pieces, base)
    return (loss.reshape(()), grad_hidden, grad_gain.reshape(-1), grad_head)


def solution(mesh):
    placed = (
        P("grp", "voc"),
        P("voc"),
        P("grp", "voc"),
        P(None, ("grp", "voc")),
        P(None, ("grp", "voc")),
        P(),
        P(),
    )
    return jax.shard_map(
        local,
        mesh=mesh,
        in_specs=placed,
        out_specs=(P(), P("grp", "voc"), P("voc"), P(None, ("grp", "voc"))),
        check_vma=False,
    )
```

```python
import jax
import jax.numpy as jnp
from jax import lax
from jax.experimental import pallas as pl
from jax.experimental.pallas import tpu as pltpu
from jax.sharding import PartitionSpec as P

DS = 4096
SEQ = 2
VALID = 240
LANES = 256
EPSILON = 1e-06
LARGEST = 3e38
GROUPS = 16
VOC = 16
ROWS = 24
HALF_S = 128
HALF_T = 160
HALF = HALF_S + HALF_T
VOC_DEV = 384
STATS = 8
SEND = 32
PACK = 56
TAIL = 32
PER = 4
SPARE = 16
SIDE = 4
BF = jnp.bfloat16
F32 = jnp.float32
CORE_SWAP = [(i, i ^ 1) for i in range(GROUPS)]
BOTH = ("grp", "voc")


def ring(phase, step):
    pairs = []
    for g in range(GROUPS):
        for v in range(VOC):
            y, x = divmod(v, SIDE)
            if (g % 2 == 0) == (phase == 1):
                x = (x + step) % SIDE
            else:
                y = (y + step) % SIDE
            pairs.append((g * VOC + v, g * VOC + y * SIDE + x))
    return pairs


TN = (((0,), (0,)), ((), ()))
NT = (((1,), (1,)), ((), ()))
NN = (((1,), (0,)), ((), ()))


def dot(a, b, dims):
    return lax.dot_general(a, b, dims, preferred_element_type=F32)


def lane_tables(source, lengths):
    episodes = lengths.shape[1]
    here = lax.broadcasted_iota(jnp.int32, (episodes, episodes), 0)
    there = lane_iota((episodes, episodes))

    def column(mask, values):
        return jnp.sum(jnp.where(mask, values, 0.0), axis=1, keepdims=True)

    lengths = lengths.astype(F32)
    two = jnp.where(lengths == 2.0, 1.0, 0.0)
    rank = column(there < here, two)
    two = column(here == there, two)
    source = column(here == there, source.astype(F32))
    lengths = column(here == there, lengths)
    lane = lane_iota((episodes, LANES)).astype(F32)
    number = lax.broadcasted_iota(jnp.int32, (episodes, LANES), 0).astype(F32)
    pick = (lane == number) | ((two == 1.0) & (lane == episodes + rank))

    def of_lane(values):
        return jnp.sum(jnp.where(pick, values, 0.0), axis=0, keepdims=True)

    lane = lane_iota((1, LANES))
    inside = lane < VALID
    position = jnp.where(lane >= episodes, 1.0, 0.0)
    student_row = jnp.where(inside, of_lane(number) * SEQ + position, -1.0)
    teacher_row = jnp.where(inside, of_lane(source) * SEQ + position, -1.0)
    weight = jnp.where(inside, 1.0 / jnp.maximum(of_lane(lengths), 1.0), 0.0)
    return student_row.astype(jnp.int32), teacher_row.astype(jnp.int32), weight


def own_core():
    return lax.rem(lax.axis_index("grp"), 2)


def lane_iota(shape):
    return lax.broadcasted_iota(jnp.int32, shape, len(shape) - 1)


def pack_kernel(
    student, teacher, source_in, lengths_in, gain_in,
    out, student_row, teacher_row, weight, gain_out,
    source, lengths, gain, sems,
):
    pairs = ((source_in, source), (lengths_in, lengths), (gain_in, gain))
    copies = []
    for n, (place, held) in enumerate(pairs):
        copies.append(pltpu.make_async_copy(place, held, sems.at[n]))
        copies[n].start()
    copies[0].wait()
    copies[1].wait()
    student_row[...], teacher_row[...], weight[...] = lane_tables(source[...], lengths[...])
    copies[2].wait()
    row = lax.broadcasted_iota(jnp.int32, (16, HALF_S), 0)
    own_gain = jnp.where(own_core() == 0, gain[:, :HALF_S], gain[:, HALF_S:])
    spread = jnp.zeros((16, HALF_S), F32)
    for k, part in enumerate(split(own_gain, 3)):
        spread = jnp.where(row == k, part.astype(F32), spread)
    gain_out[...] = spread
    for c in range(2):
        rows = teacher[:, c * HALF_T : (c + 1) * HALF_T].astype(F32)
        tail = rows[:, HALF_S:]
        tail = jnp.concatenate(
            [tail[:8], tail[8:16], tail[16:24], jnp.zeros((8, TAIL), F32)], axis=1
        )
        whole = jnp.concatenate(
            [student[:, c * HALF_S : (c + 1) * HALF_S].astype(F32), rows[:, :HALF_S], tail], axis=0
        )
        whole = whole.astype(BF)
        for z in range(GROUPS // 2):
            out[2 * z + c] = whole


def spare_lanes():
    source = lax.broadcasted_iota(jnp.int32, (LANES, LANES), 0)
    lane = lane_iota((LANES, LANES))
    return jnp.where(lane == VALID + lax.rem(source, SPARE), 1.0, 0.0).astype(BF)


def spare_rows():
    row = lax.broadcasted_iota(jnp.int32, (SPARE, LANES), 0)
    return lax.div(lane_iota((SPARE, LANES)), SPARE) == row


def split(x, parts):
    out = []
    for _ in range(parts):
        out.append(x.astype(BF))
        x = x - out[-1].astype(F32)
    return out


def compact_kernel(held, student_row, teacher_row, gain, out):
    blocks = [held[g].astype(F32) for g in range(GROUPS)]
    rows_s = jnp.concatenate([block[:ROWS] for block in blocks], axis=0).astype(BF)
    rows_t = jnp.concatenate([block[ROWS : 2 * ROWS] for block in blocks], axis=0).astype(BF)
    tails = jnp.concatenate([block[2 * ROWS :] for block in blocks], axis=0).astype(BF)
    ids = lax.broadcasted_iota(jnp.int32, (GROUPS * ROWS, LANES), 0)
    pick_s = jnp.where(ids == student_row[...], 1.0, 0.0).astype(BF)
    pick_t = jnp.where(ids == teacher_row[...], 1.0, 0.0).astype(BF)
    block_s = dot(rows_s, pick_s, TN)
    block_t = dot(rows_t, pick_t, TN).astype(BF)
    short = lax.broadcasted_iota(jnp.int32, (GROUPS * 8, LANES), 0)
    short = lax.div(short, 8) * ROWS + lax.rem(short, 8)
    tail = jnp.zeros((TAIL, LANES), F32)
    for k in range(3):
        pick = jnp.where(short + 8 * k == teacher_row[...], 1.0, 0.0).astype(BF)
        tail = tail + dot(tails, pick, TN)[k * TAIL : (k + 1) * TAIL]
    spread_gain = dot(gain[...].astype(BF), jnp.ones((16, LANES), BF), TN)
    squares = jnp.minimum(jnp.sum(block_s * block_s, axis=0, keepdims=True), LARGEST)
    parts = split(jnp.where(spare_rows(), squares, 0.0), 2)
    lanes = spare_lanes()
    spare = jnp.concatenate([dot(part, lanes, NN) for part in parts], axis=0)
    block_s = block_s * spread_gain
    block_s = jnp.concatenate([block_s[: 2 * SPARE] + spare, block_s[2 * SPARE :]], axis=0)
    out[:HALF_S, :] = block_s.astype(BF)
    out[HALF_S : 2 * HALF_S, :] = block_t
    out[2 * HALF_S :, :] = tail.astype(BF)


def stack_rows(values):
    row = lax.broadcasted_iota(jnp.int32, (STATS, LANES), 0)
    out = jnp.zeros((STATS, LANES), F32)
    for k, value in enumerate(values):
        out = jnp.where(row == k, value, out)
    return out


def total(x):
    return jnp.sum(x, axis=0, keepdims=True)


def combined(stats):
    top_s, sum_s, top_t, sum_t, mean_d, mean_u, mean_du = [stats[:, k, :] for k in range(7)]
    all_s = jnp.max(top_s, axis=0, keepdims=True)
    all_t = jnp.max(top_t, axis=0, keepdims=True)
    shift_s = top_s - all_s
    shift_t = top_t - all_t
    scale_s = jnp.exp(shift_s)
    scale_t = jnp.exp(shift_t)
    shift_d = shift_s - shift_t
    return (
        all_s,
        total(scale_s * sum_s),
        all_t,
        total(scale_t * sum_t),
        total(scale_s * (mean_d + shift_d * sum_s)),
        total(scale_s * (mean_u + shift_s * sum_s)),
        total(
            scale_s
            * (mean_du + shift_s * mean_d + shift_d * mean_u + shift_s * shift_d * sum_s)
        ),
    )


def span_of(v, core, half):
    return pl.ds(pl.multiple_of(v * 2 * half + core * half, 32), half)


def places(core):
    index = lax.axis_index("voc")
    x, y = lax.rem(index, SIDE), lax.div(index, SIDE)
    a = lax.select(core == 0, x, y)
    b = lax.select(core == 0, y, x)

    def place(j, k):
        u = lax.rem(a + SIDE - j, SIDE)
        w = lax.rem(b + SIDE - k, SIDE)
        return lax.select(core == 0, SIDE * w + u, SIDE * u + w)

    return place


def batches(refs, core):
    place = places(core)
    return [
        [(ref, j, place(j, k)) for j in range(SIDE)] for ref, k in zip(refs, (0, 1, 3, 2))
    ]


def logits_of(groups, student_head, teacher_head, core):
    student = jnp.zeros((VOC_DEV, LANES), F32)
    teacher = jnp.zeros((VOC_DEV, LANES), F32)
    squares = jnp.zeros((SPARE, LANES), F32)
    for group in groups:
        head_s = jnp.concatenate(
            [student_head[span_of(v, core, HALF_S), :] for _, _, v in group], axis=0
        )
        head_t = jnp.concatenate(
            [teacher_head[span_of(v, core, HALF_T), :] for _, _, v in group], axis=0
        )
        rows_s = jnp.concatenate([ref[j, :HALF_S, :] for ref, j, _ in group], axis=0)
        rows_t = jnp.concatenate([ref[j, HALF_S:, :] for ref, j, _ in group], axis=0)
        student = student + dot(head_s, rows_s, TN)
        teacher = teacher + dot(head_t, rows_t, TN)
        for ref, j, _ in group:
            squares = squares + ref[j, :SPARE, :].astype(F32)
            squares = squares + ref[j, SPARE : 2 * SPARE, :].astype(F32)
    return student, teacher, squares


def forward_own(
    a, u_first, d_second, student_head, teacher_in,
    student_out, teacher_out, squares_out, teacher_head, zero_out, sem,
):
    copy = pltpu.make_async_copy(teacher_in, teacher_head, sem)
    copy.start()
    zero_out[...] = jnp.zeros((1, LANES), F32)
    copy.wait()
    core = own_core()
    student, teacher, squares = logits_of(batches((a,), core), student_head, teacher_head, core)
    student_out[...] = student
    teacher_out[...] = teacher
    squares_out[...] = squares


def forward_near(
    u, d, student_head, teacher_head, student_sum, teacher_sum, squares_sum,
    student_out, teacher_out, squares_out, zero_out,
):
    core = own_core()
    groups = batches((None, u, d), core)[1:]
    student, teacher, squares = logits_of(groups, student_head, teacher_head, core)
    student_out[...] = student + student_sum[...]
    teacher_out[...] = teacher + teacher_sum[...]
    squares_out[...] = squares + squares_sum[...]
    zero_out[...] = jnp.zeros((1, LANES), F32)


def forward_mid(
    far, other_a, other_u, other_d, student_head, teacher_head,
    student_sum, teacher_sum, squares_sum, student_out, teacher_out, squares_out,
):
    core = own_core()
    groups = batches((None, None, None, far), core)[3:]
    one = logits_of(groups, student_head, teacher_head, core)
    groups = batches((other_a, other_u, other_d), 1 - core)
    two = logits_of(groups, student_head, teacher_head, 1 - core)
    student_out[...] = one[0] + two[0] + student_sum[...]
    teacher_out[...] = one[1] + two[1] + teacher_sum[...]
    squares_out[...] = one[2] + two[2] + squares_sum[...]


def forward_last(
    other_far, student_head, teacher_head, student_in, teacher_in, squares_in,
    exp_out, ratio_out, stats_out, tops_out, inverse_out,
):
    core = 1 - own_core()
    student, teacher, squares = logits_of(
        batches((None, None, None, other_far), core)[3:], student_head, teacher_head, core
    )
    squares = squares + squares_in[...]
    squares = jnp.where(lane_iota((SPARE, LANES)) >= VALID, squares, 0.0)
    lanes = spare_lanes()
    by_row = sum(dot(part, lanes, NT) for part in split(squares, 3))
    squares = total(jnp.where(spare_rows(), by_row, 0.0))
    inverse = lax.rsqrt(squares / DS + EPSILON)
    inverse_out[...] = inverse
    student = (student + student_in[...]) * inverse
    teacher = teacher + teacher_in[...]

    top_s = jnp.max(student, axis=0, keepdims=True)
    top_t = jnp.max(teacher, axis=0, keepdims=True)
    below = student - top_s
    exp_s = jnp.exp(below)
    below_t = teacher - top_t
    ratio = below - below_t
    exp_out[...] = exp_s
    ratio_out[...] = ratio
    weighted = exp_s * ratio
    stats = stack_rows(
        [
            top_s,
            total(exp_s),
            top_t,
            total(jnp.exp(below_t)),
            total(weighted),
            total(exp_s * below),
            total(weighted * below),
        ]
    )
    tops_out[...] = stats
    for v in range(VOC):
        stats_out[v] = stats


def combine_kernel(stats, out):
    tile = stack_rows(combined(stats))
    for g in range(GROUPS):
        out[g] = tile


def terms_of(groups, student_head, grad, core, out):
    for group in groups:
        head = jnp.concatenate(
            [student_head[span_of(v, core, HALF_S), :] for _, _, v in group], axis=0
        )
        term = dot(head, grad, NN).astype(BF)
        for i, (_, _, v) in enumerate(group):
            out[v] = term[i * HALF_S : (i + 1) * HALF_S]


def backward_one(
    stats, tops, exp_in, ratio_in, weight, inverse, student_head,
    grad_out, scaled_out, away, pull_out, loss_out,
):
    core = 1 - own_core()
    all_s, total_s, all_t, total_t, sum_d, sum_u, sum_du = combined(stats)
    inside = lane_iota((1, LANES)) < VALID
    mean_d = sum_d / total_s
    mean_u = sum_u / total_s
    covariance = sum_du / total_s - mean_d * mean_u
    divergence = mean_d - jnp.log(total_s) + jnp.log(total_t)
    loss_out[...] = jnp.sum(
        jnp.where(inside, weight[...] * divergence, 0.0), axis=1, keepdims=True
    )
    pull_out[...] = weight[...] * covariance * inverse[...] * inverse[...] / DS
    shift_s = tops[0:1, :] - all_s
    shift_t = tops[2:3, :] - all_t
    factor = weight[...] * jnp.exp(shift_s) / total_s
    offset = shift_s - shift_t - mean_d
    grad = jnp.where(inside, factor * exp_in[...] * (ratio_in[...] + offset), 0.0)
    kept = jnp.where(inside, inverse[...], 0.0)
    scaled_out[...] = (grad * kept).astype(BF)
    grad = grad.astype(BF)
    grad_out[...] = grad
    terms_of(batches((None,) * 4, core), student_head, grad, core, away)


def backward_two(*refs):
    scaled, grad, student_head, hidden, gain, student_row, inverse, pull = refs[8:16]
    stay, base_out, out, blocks, sems = refs[16:]
    core = own_core()
    copies = []
    for k, side in enumerate((core, 1 - core)):
        for group in batches(refs[SIDE * k : SIDE * k + SIDE], side):
            block = jnp.concatenate([ref[j, :HALF_S, :] for ref, j, _ in group], axis=0)
            result = dot(block, scaled[...], NT).astype(BF)
            for i, (_, _, v) in enumerate(group):
                n = len(copies)
                blocks[n] = result[i * HALF_S : (i + 1) * HALF_S]
                copies.append(
                    pltpu.make_async_copy(
                        blocks.at[n], out.at[span_of(v, side, HALF_S)], sems.at[n]
                    )
                )
                copies[n].start()
    first = lax.axis_index("grp") * ROWS
    own = lax.broadcasted_iota(jnp.int32, (ROWS, LANES), 0) + first == student_row[...]
    own_rms = jnp.sum(jnp.where(own, inverse[...], 0.0), axis=1, keepdims=True)
    own_pull = jnp.sum(jnp.where(own, pull[...], 0.0), axis=1, keepdims=True)
    base_out[:ROWS] = own_rms * gain[...]
    base_out[ROWS : 2 * ROWS] = hidden[...].astype(F32) * own_pull
    base_out[2 * ROWS :] = jnp.broadcast_to(1.0 / gain[...], (8, LANES))
    terms_of(batches((None,) * 4, core), student_head, grad[...], core, stay)
    for copy in copies:
        copy.wait()


def pair_kernel(stay, arrived, out):
    for v in range(VOC):
        out[v] = (stay[v].astype(F32) + arrived[v].astype(F32)).astype(BF)


def send_kernel(pieces, student_row, block, inverse, out):
    summed = pieces[0].astype(F32)
    for v in range(1, VOC):
        summed = summed + pieces[v].astype(F32)
    lane = lane_iota((HALF_S, LANES))
    inside = lane < VALID
    scaled = jnp.where(inside, block[:HALF_S, :].astype(F32) * inverse[...], 0.0)
    gain = jnp.sum(summed * scaled, axis=1, keepdims=True)
    summed = jnp.where(lane == VALID, gain, summed).astype(BF)
    slot = lax.broadcasted_iota(jnp.int32, (SEND, LANES), 0)
    extra = (slot == ROWS) & (lane_iota((SEND, LANES)) == VALID)
    picks = []
    for g in range(GROUPS):
        pick = ((slot < ROWS) & (student_row[...] == slot + g * ROWS)) | extra
        picks.append(jnp.where(pick, 1.0, 0.0).astype(BF))
    result = dot(jnp.concatenate(picks, axis=0), summed, NT).astype(BF)
    for g in range(GROUPS):
        out[g] = result[g * SEND : (g + 1) * SEND]


def finish_kernel(pieces, base, grad_hidden, grad_gain):
    halves = []
    for c in range(2):
        summed = pieces[c].astype(F32)
        for z in range(1, GROUPS // 2):
            summed = summed + pieces[2 * z + c].astype(F32)
        halves.append(summed)
    summed = jnp.concatenate(halves, axis=1)
    grad_gain[...] = summed[ROWS : ROWS + 1] * base[2 * ROWS : 2 * ROWS + 1]
    grad_hidden[...] = (summed[:ROWS] * base[:ROWS] - base[ROWS : 2 * ROWS]).astype(BF)


def shape(dims, dtype):
    return jax.ShapeDtypeStruct(dims, dtype)


def params(mib):
    return pltpu.CompilerParams(vmem_limit_bytes=mib * 1024 * 1024)


def in_hbm(x):
    return pltpu.with_memory_space_constraint(x, pltpu.HBM)


def cost(flops):
    return pl.CostEstimate(flops=flops, bytes_accessed=4 * 1024 * 1024, transcendentals=0)


def exchange(x, axis):
    return lax.all_to_all(x, axis, 0, 0, tiled=True)


HBM = pl.BlockSpec(memory_space=pltpu.HBM)
ANY = pl.BlockSpec(memory_space=pl.ANY)
VMEM = pl.BlockSpec(memory_space=pltpu.VMEM)


def local(
    student_hidden, norm_gain, teacher_hidden, student_head, teacher_head, episode_source, lengths
):
    row = shape((1, LANES), F32)
    logits = shape((VOC_DEV, LANES), F32)
    half_rows = shape((VOC, HALF_S, LANES), BF)

    table = shape((1, LANES), jnp.int32)
    episodes = lengths.shape[0]
    packed, student_row, teacher_row, weight, gain_parts = pl.pallas_call(
        pack_kernel,
        out_shape=(
            shape((GROUPS, PACK, HALF_S), BF), table, table, row, shape((16, HALF_S), F32)
        ),
        in_specs=[VMEM] * 2 + [HBM] * 3,
        out_specs=(VMEM,) * 5,
        scratch_shapes=[
            pltpu.VMEM((1, episodes), jnp.int32),
            pltpu.VMEM((1, episodes), jnp.int32),
            pltpu.VMEM((1, 2 * HALF_S), F32),
            pltpu.SemaphoreType.DMA((3,)),
        ],
        compiler_params=params(4),
    )(
        in_hbm(student_hidden), in_hbm(teacher_hidden),
        in_hbm(episode_source[None]), in_hbm(lengths[None]), in_hbm(norm_gain[None]),
    )
    held = exchange(packed, "grp")
    block = pl.pallas_call(
        compact_kernel, out_shape=shape((HALF, LANES), BF), compiler_params=params(8)
    )(held, student_row, teacher_row, gain_parts)

    one = lax.ppermute(block, BOTH, ring(1, 1))
    three = lax.ppermute(block, BOTH, ring(1, 3))
    two = lax.ppermute(block, BOTH, ring(1, 2))
    first = jnp.stack([block, one])
    second = jnp.stack([two, three])
    u_first = lax.ppermute(first, BOTH, ring(2, 1))
    d_second = lax.ppermute(second, BOTH, ring(2, 3))
    u_second = lax.ppermute(second, BOTH, ring(2, 1))
    d_first = lax.ppermute(first, BOTH, ring(2, 3))
    v = lax.ppermute(u_first, BOTH, ring(2, 1))
    w = lax.ppermute(d_second, BOTH, ring(2, 3))
    a = jnp.concatenate([first, second], axis=0)
    u = jnp.concatenate([u_first, u_second], axis=0)
    d = jnp.concatenate([d_first, d_second], axis=0)
    partial = (logits, logits, shape((SPARE, LANES), F32))

    def sems(count):
        return pltpu.SemaphoreType.DMA((count,))

    *sums, head_t, zero = pl.pallas_call(
        forward_own,
        out_shape=partial + (pltpu.VMEM(teacher_head.shape, BF), row),
        in_specs=[VMEM, ANY, ANY, VMEM, HBM],
        out_specs=(VMEM,) * 5,
        scratch_shapes=[pltpu.SemaphoreType.DMA],
        compiler_params=params(12),
        cost_estimate=cost(SIDE * HALF * VOC_DEV * LANES * 2),
    )(a, u_first, d_second, student_head, in_hbm(teacher_head))
    other = (lax.ppermute(a, "grp", CORE_SWAP),) + tuple(
        lax.ppermute(part + zero.astype(BF), "grp", CORE_SWAP) for part in (u, d)
    )
    *sums, zero = pl.pallas_call(
        forward_near,
        out_shape=partial + (row,),
        compiler_params=params(12),
        cost_estimate=cost(2 * SIDE * HALF * VOC_DEV * LANES * 2),
    )(u, d, student_head, head_t, *sums)
    far = jnp.concatenate([v, w], axis=0) + zero.astype(BF)
    other_far = lax.ppermute(far, "grp", CORE_SWAP)
    sums = pl.pallas_call(
        forward_mid,
        out_shape=partial,
        compiler_params=params(12),
        cost_estimate=cost(VOC * HALF * VOC_DEV * LANES * 2),
    )(far, *other, student_head, head_t, *sums)
    exp_s, ratio, stats, tops, inverse = pl.pallas_call(
        forward_last,
        out_shape=(
            logits,
            logits,
            shape((VOC, STATS, LANES), F32),
            shape((STATS, LANES), F32),
            row,
        ),
        compiler_params=params(12),
        cost_estimate=cost(SIDE * HALF * VOC_DEV * LANES * 2),
    )(other_far, student_head, head_t, *sums)

    from_voc = exchange(stats, "voc")
    spread = pl.pallas_call(
        combine_kernel, out_shape=shape((GROUPS, STATS, LANES), F32), compiler_params=params(4)
    )(from_voc)
    from_grp = exchange(spread, "grp")

    grad, scaled, away, pull, loss = pl.pallas_call(
        backward_one,
        out_shape=(
            shape((VOC_DEV, LANES), BF),
            shape((VOC_DEV, LANES), BF),
            half_rows,
            row,
            shape((1, 1), F32),
        ),
        out_specs=(VMEM,) * 5,
        compiler_params=params(8),
        cost_estimate=cost(DS * VOC_DEV * LANES),
    )(from_grp, tops, exp_s, ratio, weight, inverse, student_head)
    arrived = lax.ppermute(away, "grp", CORE_SWAP)
    stay, base, grad_head = pl.pallas_call(
        backward_two,
        out_shape=(
            half_rows,
            shape((2 * ROWS + 8, LANES), F32),
            shape((DS, VOC_DEV), BF),
        ),
        out_specs=(VMEM, VMEM, HBM),
        scratch_shapes=[pltpu.VMEM((2 * VOC, HALF_S, VOC_DEV), BF), sems(2 * VOC)],
        compiler_params=params(12),
        cost_estimate=cost(DS * VOC_DEV * LANES * 3),
    )(
        a, u, d, far, *other, other_far, scaled, grad, student_head,
        student_hidden, norm_gain[None], student_row, inverse, pull,
    )
    pair = pl.pallas_call(pair_kernel, out_shape=half_rows, compiler_params=params(8))(
        stay, arrived
    )
    pieces = exchange(pair, "voc")
    outgoing = pl.pallas_call(
        send_kernel,
        out_shape=shape((GROUPS, SEND, HALF_S), BF),
        compiler_params=params(8),
    )(pieces, student_row, block, inverse)
    pieces = exchange(outgoing, "grp")
    grad_hidden, grad_gain = pl.pallas_call(
        finish_kernel,
        out_shape=(shape((ROWS, 2 * HALF_S), BF), row),
        compiler_params=params(4),
    )(pieces, base)
    return (loss.reshape(()), grad_hidden, grad_gain.reshape(-1), grad_head)


def solution(mesh):
    placed = (
        P("grp", "voc"),
        P("voc"),
        P("grp", "voc"),
        P(None, ("grp", "voc")),
        P(None, ("grp", "voc")),
        P(),
        P(),
    )
    return jax.shard_map(
        local,
        mesh=mesh,
        in_specs=placed,
        out_specs=(P(), P("grp", "voc"), P("voc"), P(None, ("grp", "voc"))),
        check_vma=False,
    )
```
